32 devices in a mesh: genome: 8 (over y, x, core), offset: 4 (over z).
Axes of the slice: x: 2, y: 2, z: 4, core: 2. Of those that a mesh axis runs over, the one named last changes fastest.
Arguments:
- counts: int32 [512, 8, 128, 128], P('genome', 'offset'), may hold values from 1 to 512, as said below
- band_offset: int32 [8], P('offset'), may hold values from 0 to 7, as said below
- bin_mask: int32 [65536], P('genome'), may hold values 0 or 1
- row_factors: float32 [32, 65536], P(None, 'genome'), may hold values from 0.25 to 4
- col_factors: float32 [32, 65536], P(None, 'genome'), may hold values from 0.25 to 4
Outputs:
- bias: float32 [65536], P('genome')
- row_update: float32 [32, 65536], P(None, ('genome', 'offset'))
- col_update: float32 [32, 65536], P(None, ('genome', 'offset'))
The draws below stay inside these ranges and needn't reach their ends.
Inputs may be any that keep to these rules, and one draw needn't show every extreme that they name: `counts`: only the upper triangle of a tile whose slot has band offset 0 is read. `band_offset`: A permutation of 0 to 7.
All inputs are finite; a program needn't handle non-finite values. No bound on the sum of `bin_mask` on one device may be relied on, other than what follows from the above.
Results may differ from the reference program's by a relative error of at most 0.00011.
Values sent between devices are 32-bit elements; how exact they have to be, the bound alone decides.
No kernel may reach another device: no remote copies, remote signals or barrier semaphores. Data moves between devices by JAX's collectives and lax.ppermute only.
A program may use at most 128 MiB of HBM per device.

```python
import math
import jax
import jax.numpy as jnp
from jax import lax

TILE = 128
NOFF = 8
K = 32
ITERS = 3
NTILES = 512
BINS = 65536


def band_order(key):
    return jax.random.permutation(jax.random.fold_in(key, 7), NOFF).astype(jnp.int32)


def draw_band_offset(key, part):
    return band_order(key)


def draw_counts(key, part):
    perm_order = band_order(key)
    levels = jax.random.randint(jax.random.fold_in(key, 3), ((NTILES + NOFF) * TILE,), 0, 4)
    weights = jnp.array([1, 2, 4, 8], dtype=jnp.int32)[levels]
    by_tile = weights.reshape(NTILES + NOFF, TILE)
    row_weight = by_tile[:NTILES][:, None, :, None]
    col_index = jnp.arange(NTILES, dtype=jnp.int32)[:, None] + perm_order[None, :]
    col_weight = by_tile[col_index][:, :, None, :]
    base_counts = jax.random.randint(jax.random.fold_in(key, 5), (NTILES, NOFF, TILE, TILE), 1, 9)
    return (base_counts * row_weight * col_weight).astype(jnp.int32)


def set_ends(drawn, stream_key, least, top_value):
    spot = [jax.random.randint(jax.random.fold_in(stream_key, axis), (), 0, length) for axis, length in enumerate(drawn.shape)]
    longest = drawn.shape.index(max(drawn.shape))
    beside = spot[:longest] + [(spot[longest] + 1) % drawn.shape[longest]] + spot[longest + 1:]
    return drawn.at[tuple(spot)].set(least).at[tuple(beside)].set(top_value)


def level_of(key, extent, cuts, least, top_value):
    gain, own = 1.0, jax.random.fold_in(key, 6)
    for axis_at, shards_of in cuts:
        draws = jnp.exp(jax.random.uniform(jax.random.fold_in(own, axis_at), (shards_of,), jnp.float32, least / len(cuts), top_value / len(cuts)))
        gain = gain * jnp.repeat(draws, extent[axis_at] // shards_of).reshape([-1 if axis == axis_at else 1 for axis in range(len(extent))])
    return gain


def setup_inputs(seed: int = 0) -> dict:
    arg_keys = jax.random.split(jax.random.key(seed), 6)
    return {
        "counts": draw_counts(jax.random.fold_in(arg_keys[5], 71), 0),
        "band_offset": draw_band_offset(jax.random.fold_in(arg_keys[5], 71), 0),
        "bin_mask": set_ends((jax.random.randint(arg_keys[2], (BINS,), 0, 10) < 9).astype(jnp.int32), jax.random.fold_in(arg_keys[2], 1), 0, 1),
        "row_factors": jnp.clip(jnp.exp(math.log(4.0) - 2.7725887 * jax.random.uniform(arg_keys[3], (K, BINS), jnp.float32) ** level_of(arg_keys[3], (K, BINS), ((1, 8),), -0.2, 0.2)), 0.25, 4.0),
        "col_factors": jnp.clip(jnp.exp(math.log(4.0) - 2.7725887 * jax.random.uniform(arg_keys[4], (K, BINS), jnp.float32) ** level_of(arg_keys[4], (K, BINS), ((1, 8),), -0.2, 0.2)), 0.25, 4.0),
    }


def mirror_tile(count_block, offset_value):
    edge_size = count_block.shape[-1]
    upper_half = lax.broadcasted_iota(jnp.int32, (edge_size, edge_size), 0) <= lax.broadcasted_iota(jnp.int32, (edge_size, edge_size), 1)
    mirrored = jnp.where(upper_half, count_block, jnp.swapaxes(count_block, -1, -2))
    return jnp.where(offset_value == 0, mirrored, count_block)


def tile_values(count_block, offset_value, bias_rows, bias_ext):
    bias_cols = lax.dynamic_slice_in_dim(bias_ext, offset_value, bias_rows.shape[0], 0)
    values = mirror_tile(count_block.astype(jnp.float32), offset_value)
    return values * bias_rows[:, :, None] * bias_cols[:, None, :]


def band_coverage(counts, band_offset, bias_rows, bias_ext):
    row_count = counts.shape[0]
    tile_size = counts.shape[2]
    spread = bias_ext.shape[0]
    row_part = jnp.zeros((row_count, tile_size), jnp.float32)
    col_part = jnp.zeros((spread, tile_size), jnp.float32)
    for slot_index in range(counts.shape[1]):
        offset_value = band_offset[slot_index].astype(jnp.int32)
        values = tile_values(counts[:, slot_index], offset_value, bias_rows, bias_ext)
        row_part = row_part + jnp.sum(values, axis=2)
        column_terms = jnp.where(offset_value > 0, jnp.sum(values, axis=1), jnp.float32(0.0))
        col_part = col_part + lax.dynamic_update_slice_in_dim(jnp.zeros((spread, tile_size), jnp.float32), column_terms, offset_value, 0)
    return row_part, col_part


def factor_terms(counts, band_offset, bias_rows, bias_ext, mask_rows, mask_ext, w_rows, h_ext):
    factor_count, row_count, tile_size = w_rows.shape
    spread = h_ext.shape[1]
    w_masked = jnp.sum(w_rows * mask_rows[None], axis=2)
    w_num = jnp.zeros((factor_count, row_count, tile_size), jnp.float32)
    h_norm = jnp.zeros((factor_count, row_count), jnp.float32)
    h_num = jnp.zeros((factor_count, spread, tile_size), jnp.float32)
    w_spread = jnp.zeros((factor_count, spread), jnp.float32)
    highest = lax.Precision.HIGHEST
    for slot_index in range(counts.shape[1]):
        offset_value = band_offset[slot_index].astype(jnp.int32)
        values = tile_values(counts[:, slot_index], offset_value, bias_rows, bias_ext)
        h_cols = lax.dynamic_slice_in_dim(h_ext, offset_value, row_count, 1)
        m_cols = lax.dynamic_slice_in_dim(mask_ext, offset_value, row_count, 0)
        model_tiles = jnp.einsum('kip,kiq->ipq', w_rows, h_cols, precision=highest)
        ratio_tiles = values / jnp.where(m_cols[:, None, :] > 0, model_tiles, jnp.float32(1.0))
        w_num = w_num + jnp.einsum('ipq,kiq->kip', ratio_tiles, h_cols, precision=highest)
        h_norm = h_norm + jnp.sum(h_cols * m_cols[None], axis=2)
        col_terms = jnp.einsum('kip,ipq->kiq', w_rows, ratio_tiles, precision=highest)
        h_num = h_num + lax.dynamic_update_slice_in_dim(jnp.zeros((factor_count, spread, tile_size), jnp.float32), col_terms, offset_value, 1)
        w_spread = w_spread + lax.dynamic_update_slice_in_dim(jnp.zeros((factor_count, spread), jnp.float32), w_masked, offset_value, 1)
    return w_num, h_norm, h_num, w_spread


def update_flat(factor, numer, denom_small, mask_rows):
    factor_count = factor.shape[0]
    denom = (denom_small[:, :, None] * mask_rows[None]).reshape(factor_count, -1)
    live_bins = mask_rows.reshape(1, -1) > 0
    return jnp.where(live_bins, factor * numer / jnp.where(live_bins, denom, jnp.float32(1.0)), factor)


def reference(counts, band_offset, bin_mask, row_factors, col_factors):
    pad_bins = (NOFF - 1) * TILE
    mask_flat = bin_mask.astype(jnp.float32)
    live_flat = bin_mask > 0
    mask_rows = mask_flat.reshape(NTILES, TILE)
    bins_live = jnp.sum(mask_flat)
    bias = mask_flat
    for iteration in range(ITERS):
        bias_ext = jnp.concatenate([bias, jnp.zeros((pad_bins,), jnp.float32)]).reshape(NTILES + NOFF - 1, TILE)
        row_part, col_part = band_coverage(counts, band_offset, bias.reshape(NTILES, TILE), bias_ext)
        coverage = (row_part + col_part[:NTILES]).reshape(-1)
        mean_cover = jnp.sum(coverage) / bins_live
        bias = jnp.where(live_flat, bias * mean_cover / jnp.where(live_flat, coverage, jnp.float32(1.0)), jnp.float32(0.0))
    bias_ext = jnp.concatenate([bias, jnp.zeros((pad_bins,), jnp.float32)]).reshape(NTILES + NOFF - 1, TILE)
    mask_ext = jnp.concatenate([mask_flat, jnp.zeros((pad_bins,), jnp.float32)]).reshape(NTILES + NOFF - 1, TILE)
    w_rows = row_factors.reshape(K, NTILES, TILE)
    h_ext = jnp.concatenate([col_factors, jnp.zeros((K, pad_bins), jnp.float32)], axis=1).reshape(K, NTILES + NOFF - 1, TILE)
    w_num, h_norm, h_num, w_spread = factor_terms(counts, band_offset, bias.reshape(NTILES, TILE), bias_ext, mask_rows, mask_ext, w_rows, h_ext)
    row_update = update_flat(row_factors, w_num.reshape(K, -1), h_norm, mask_rows)
    col_update = update_flat(col_factors, h_num[:, :NTILES].reshape(K, -1), w_spread[:, :NTILES], mask_rows)
    return bias, row_update, col_update
```

```python
import functools

import jax
import jax.numpy as jnp
from jax import lax
from jax.experimental import pallas as pl
from jax.experimental.pallas import tpu as pltpu
from jax.sharding import PartitionSpec as P

ITERS = 3
STEP = 8
F32 = jnp.float32
BF16 = jnp.bfloat16
VMEM_LIMIT = 48 * 1024 * 1024


def split(x):
    hi = x.astype(BF16)
    lo = (x - hi.astype(F32)).astype(BF16)
    return hi, lo


def tree_sum(parts):
    while len(parts) > 1:
        parts = [a + b for a, b in zip(parts[::2], parts[1::2])]
    return parts[0]


def params():
    return pltpu.CompilerParams(vmem_limit_bytes=VMEM_LIMIT)


def whole(shape):
    return pl.BlockSpec(shape, lambda *_: (0,) * len(shape))


def scale_from(mask, parts):
    cover = tree_sum([p[...] for p in parts])
    live = mask[...] > 0
    return jnp.where(live, 1.0 / jnp.where(live, cover, 1.0), 0.0)


def cover_kernel(first, rows, offs, counts, mask, *refs):
    if first:
        parts, (v_out, edge_out, u_out, acc, weight) = (), refs
    else:
        parts, (v_out, edge_out, u_out, acc, weight) = refs[:-5], refs[-5:]
    step = pl.program_id(0)
    slots = counts.shape[1]
    tile = counts.shape[2]

    @pl.when(step == 0)
    def _():
        u_out[...] = mask[...] if first else scale_from(mask, parts)
        acc[...] = jnp.zeros_like(acc)
        r = lax.broadcasted_iota(jnp.int32, (tile, tile), 0)
        c = lax.broadcasted_iota(jnp.int32, (tile, tile), 1)
        half = jnp.where(r < c, 1.0, jnp.where(r == c, 0.5, 0.0))
        for s in range(slots):
            weight[s] = jnp.where(offs[s] == 0, half, 1.0)

    base = step * STEP
    u_cols = u_out[pl.ds(pl.multiple_of(base, STEP), STEP), :].T

    def tiles(weighted):
        sums = []
        for t in range(STEP):
            u_row = u_cols[:, t : t + 1]
            total = None
            for s in range(slots):
                c = counts[t, s].astype(F32)
                if weighted:
                    c = c * weight[s]
                j = base + t + offs[s]
                term = c * u_out[pl.ds(j, 1), :]
                total = term if total is None else total + term
                acc[pl.ds(j, 1), :] += jnp.sum(c * u_row, axis=0, keepdims=True)
            sums.append(jnp.sum(total, axis=1, keepdims=True))
        acc[pl.ds(pl.multiple_of(base, STEP), STEP), :] += jnp.concatenate(sums, axis=1).T

    on_diagonal = functools.reduce(jnp.logical_or, [offs[s] == 0 for s in range(slots)])

    @pl.when(on_diagonal)
    def _():
        tiles(True)

    @pl.when(jnp.logical_not(on_diagonal))
    def _():
        tiles(False)

    @pl.when(step == pl.num_programs(0) - 1)
    def _():
        pad = acc.shape[0] - rows
        v_out[...] = acc[...]
        edge_out[:pad] = acc[:pad]
        edge_out[pad:] = acc[rows:]


def cover_call(offs, counts, mask_ext, parts):
    rows, slots, tile = counts.shape[:3]
    ext = mask_ext.shape[0]
    flat = jax.ShapeDtypeStruct((ext, tile), F32)
    edge = jax.ShapeDtypeStruct((2 * (ext - rows), tile), F32)
    return pl.pallas_call(
        functools.partial(cover_kernel, not parts, rows),
        grid_spec=pltpu.PrefetchScalarGridSpec(
            num_scalar_prefetch=1,
            grid=(rows // STEP,),
            in_specs=[pl.BlockSpec((STEP, slots, tile, tile), lambda i, *_: (i, 0, 0, 0))]
            + [whole((ext, tile))] * (1 + len(parts)),
            out_specs=[whole((ext, tile)), whole(edge.shape), whole((ext, tile))],
            scratch_shapes=[pltpu.VMEM((ext, tile), F32), pltpu.VMEM((slots, tile, tile), F32)],
        ),
        out_shape=[flat, edge, flat],
        compiler_params=params(),
        name="cover",
    )(offs, counts, mask_ext, *parts)


def ratio_kernel(offs, counts, w_ref, h_ref, hi_out, lo_out):
    step = pl.program_id(0)
    slots, tile = counts.shape[1:3]
    base = step * STEP
    r = lax.broadcasted_iota(jnp.int32, (tile, tile), 0)
    c = lax.broadcasted_iota(jnp.int32, (tile, tile), 1)

    def body(t, carry):
        w_hi, w_lo = split(w_ref[:, pl.ds(pl.multiple_of(t * tile, tile), tile)])
        w4 = jnp.concatenate([w_hi, w_hi, w_lo, w_lo], axis=0).astype(F32).T.astype(BF16)
        for s in range(slots):
            j = base + t + offs[s]
            h_hi, h_lo = split(h_ref[:, pl.ds(pl.multiple_of(j * tile, tile), tile)])
            h4 = jnp.concatenate([h_hi, h_lo, h_hi, h_lo], axis=0)
            model = jnp.dot(w4, h4, preferred_element_type=F32)
            inverse = 1.0 / model
            values = counts[t, s].astype(F32)

            def put(x):
                hi, lo = split(x)
                hi_out[t, :, s * tile : (s + 1) * tile] = hi
                lo_out[t, :, s * tile : (s + 1) * tile] = lo

            @pl.when(offs[s] == 0)
            def _():
                put(jnp.where(r <= c, values, values.T) * inverse)

            @pl.when(offs[s] != 0)
            def _():
                put(values * inverse)

        return carry

    lax.fori_loop(0, STEP, body, 0, unroll=2)


def ratio_call(offs, counts, row_factors, col_ext):
    rows, slots, tile = counts.shape[:3]
    factors = row_factors.shape[0]
    out = jax.ShapeDtypeStruct((rows, tile, slots * tile), BF16)
    block = pl.BlockSpec((STEP, tile, slots * tile), lambda i, *_: (i, 0, 0))
    return pl.pallas_call(
        ratio_kernel,
        grid_spec=pltpu.PrefetchScalarGridSpec(
            num_scalar_prefetch=1,
            grid=(rows // STEP,),
            in_specs=[
                pl.BlockSpec((STEP, slots, tile, tile), lambda i, *_: (i, 0, 0, 0)),
                pl.BlockSpec((factors, STEP * tile), lambda i, *_: (0, i)),
                whole(col_ext.shape),
            ],
            out_specs=[block, block],
        ),
        out_shape=[out, out],
        compiler_params=params(),
        name="ratio",
    )(offs, counts, row_factors, col_ext)


NT = (((1,), (1,)), ((), ()))


def numer_kernel(shares, rows, scal, hi_ref, lo_ref, w_ref, h_ref, mask, *refs):
    offset_count = shares
    parts = refs[:offset_count]
    outs = refs[offset_count:]
    u_out = outs[0]
    w_outs = outs[1 : 1 + shares]
    h_outs = outs[1 + shares : 1 + 2 * shares]
    tail_out = outs[1 + 2 * shares]
    g_all, h_acc = outs[2 + 2 * shares :]
    step = pl.program_id(0)
    me = scal[0]
    share = jnp.bitwise_xor(step, me)
    per = rows // shares
    ext = mask.shape[0]
    tile = mask.shape[1]
    factors = w_ref.shape[0]
    slots = hi_ref.shape[2] // tile
    offs = [scal[1 + s] for s in range(slots)]

    @pl.when(step == 0)
    def _():
        u_out[...] = scale_from(mask, parts)
        h_acc[...] = jnp.zeros_like(h_acc)

        def fill(j, carry):
            x = h_ref[:, pl.ds(pl.multiple_of(j * tile, tile), tile)] * u_out[pl.ds(j, 1), :]
            hi, lo = split(x)
            g_all[j, :factors] = hi
            g_all[j, factors:] = lo
            return carry

        lax.fori_loop(0, ext, fill, 0, unroll=4)

    base = share * per

    def make(t, w_out):
        i = base + t
        u_row = u_out[pl.ds(i, 1), :]
        r_hi = hi_ref[t]
        r_lo = lo_ref[t]
        g = jnp.concatenate([g_all[i + offs[s]] for s in range(slots)], axis=1)
        big = lax.dot_general(g, r_hi, NT, preferred_element_type=F32)
        small = lax.dot_general(g[:factors], r_lo, NT, preferred_element_type=F32)
        w_out[t] = (big[:factors] + big[factors:] + small) * u_row
        a_hi, a_lo = split(w_ref[:, pl.ds(pl.multiple_of(t * tile, tile), tile)] * u_row)
        big = jnp.dot(jnp.concatenate([a_hi, a_lo], axis=0), r_hi, preferred_element_type=F32)
        small = jnp.dot(a_hi, r_lo, preferred_element_type=F32)
        cols = big[:factors] + big[factors:] + small
        for s in range(slots):
            h_acc[i + offs[s]] += cols[:, s * tile : (s + 1) * tile]

    for k in range(shares):

        @pl.when(step == k)
        def _():
            def body(t, carry):
                make(t, w_outs[k])
                return carry

            lax.fori_loop(0, per, body, 0, unroll=4)

    @pl.when(step == shares - 1)
    def _():
        for k in range(shares):
            first = jnp.bitwise_xor(me, k) * per
            for t in range(per):
                h_outs[k][t] = h_acc[first + t] * u_out[pl.ds(first + t, 1), :]
        for t in range(ext - rows):
            tail_out[t] = h_acc[rows + t] * u_out[pl.ds(rows + t, 1), :]


def numer_call(scal, r_hi, r_lo, row_factors, col_ext, mask_ext, parts):
    shares = len(parts)
    rows, tile, wide = r_hi.shape
    factors = row_factors.shape[0]
    ext = mask_ext.shape[0]
    per = rows // shares
    block = pl.BlockSpec((per, tile, wide), lambda i, scal: (jnp.bitwise_xor(i, scal[0]), 0, 0))
    piece = jax.ShapeDtypeStruct((per, factors, tile), F32)
    tail = jax.ShapeDtypeStruct((ext - rows, factors, tile), F32)
    flat = jax.ShapeDtypeStruct((ext, tile), F32)
    outs = [flat] + [piece] * (2 * shares) + [tail]
    res = pl.pallas_call(
        functools.partial(numer_kernel, shares, rows),
        grid_spec=pltpu.PrefetchScalarGridSpec(
            num_scalar_prefetch=1,
            grid=(shares,),
            in_specs=[
                block,
                block,
                pl.BlockSpec((factors, per * tile), lambda i, scal: (0, jnp.bitwise_xor(i, scal[0]))),
                whole(col_ext.shape),
                whole(mask_ext.shape),
            ]
            + [whole((ext, tile))] * shares,
            out_specs=[whole(x.shape) for x in outs],
            scratch_shapes=[
                pltpu.VMEM((ext, 2 * factors, tile), BF16),
                pltpu.VMEM((ext, factors, tile), F32),
            ],
        ),
        out_shape=outs,
        compiler_params=params(),
        name="numer",
    )(scal, r_hi, r_lo, row_factors, col_ext, mask_ext, *parts)
    return res[0], res[1 : 1 + shares], res[1 + shares : 1 + 2 * shares], res[-1]


def xor_exchange(x, axis, k):
    return lax.ppermute(x, axis, [(i, i ^ k) for i in range(lax.axis_size(axis))])


def both_sides(x):
    size = lax.axis_size("genome")
    me = lax.axis_index("genome")
    a = lax.ppermute(x, "genome", [(i, i ^ 1) for i in range(size)])
    b = lax.ppermute(x, "genome", [(i, (((i + 1) ^ 1) - 1) % size) for i in range(size)])
    even = me % 2 == 0
    return jnp.where(even, a, b), jnp.where(even, b, a)


def scatter_sum(pieces):
    size = lax.axis_size("offset")
    if size == 4:
        first = xor_exchange(pieces[2], "offset", 1)
        mine = xor_exchange(pieces[1], "offset", 1)
        far = xor_exchange(pieces[3] + first, "offset", 3)
        return (pieces[0] + mine) + far
    return tree_sum([pieces[0]] + [xor_exchange(pieces[k], "offset", k) for k in range(1, size)])


def per_device(counts, band_offset, bin_mask, row_factors, col_factors):
    rows, slots, tile = counts.shape[:3]
    factors = row_factors.shape[0]
    offset_count = lax.axis_size("offset")
    genome_count = lax.axis_size("genome")
    g = lax.axis_index("genome")
    o = lax.axis_index("offset")
    reach = slots * offset_count - 1
    pad = reach + 1
    offs = band_offset.astype(jnp.int32)
    scal = jnp.concatenate([o.astype(jnp.int32).reshape(1), offs])
    has_next = g < genome_count - 1
    has_prev = g > 0

    mask = bin_mask.astype(F32).reshape(rows, tile)
    mask_next, _ = both_sides(mask[:pad])
    keep = has_next & (lax.broadcasted_iota(jnp.int32, (pad, 1), 0) < reach)
    mask_ext = jnp.concatenate([mask, jnp.where(keep, mask_next, 0.0)])

    ring_left = [(i, (i - 1) % genome_count) for i in range(genome_count)]
    col_next = lax.ppermute(col_factors[:, : pad * tile], "genome", ring_left)
    col_next = jnp.where(has_next, col_next, 1.0)
    col_ext = jnp.concatenate([col_factors, col_next], axis=1)

    scales = []
    parts = []
    for _ in range(ITERS):
        v, edge, u = cover_call(offs, counts, mask_ext, parts)
        scales.append(u[:rows])
        after, before = both_sides(edge)
        front = v[:pad] + jnp.where(has_prev, before[pad:], 0.0)
        back = v[rows:] + jnp.where(has_next, after[:pad], 0.0)
        x = jnp.concatenate([front, v[pad:rows], back])
        parts = [x] + [xor_exchange(x, "offset", k) for k in range(1, offset_count)]

    r_hi, r_lo = ratio_call(offs, counts, row_factors, col_ext)
    u, w_parts, h_parts, tail = numer_call(scal, r_hi, r_lo, row_factors, col_ext, mask_ext, parts)
    u = u[:rows]
    scales.append(u)

    live = mask > 0
    sums = [jnp.sum(mask)]
    for t in range(ITERS):
        sums.append(jnp.sum(jnp.where(live, scales[t] / jnp.where(live, scales[t + 1], 1.0), 0.0)))
    sums = jnp.broadcast_to(jnp.stack(sums)[:, None], (ITERS + 1, tile))
    k = 1
    while k < genome_count:
        sums = sums + xor_exchange(sums, "genome", k)
        k *= 2
    factor = sums[1, 0] / sums[0, 0]
    for t in range(1, ITERS):
        factor = factor * (sums[t + 1, 0] / sums[0, 0])
    bias = jnp.where(live, u * factor, 0.0).reshape(-1)

    arrived = lax.ppermute(tail, "genome", [(i, (i + 1) % genome_count) for i in range(genome_count)])
    per = rows // offset_count
    arrived = jnp.where(has_prev, arrived, 0.0)
    for s in range(-(-pad // per)):
        piece = arrived[s * per : (s + 1) * per]
        h_parts = [
            h.at[: piece.shape[0]].add(jnp.where(jnp.bitwise_xor(o, k) == s, piece, 0.0))
            for k, h in enumerate(h_parts)
        ]

    h_tile = jnp.sum(col_factors.reshape(factors, rows, tile) * mask[None], axis=2)
    w_tile = jnp.sum(row_factors.reshape(factors, rows, tile) * mask[None], axis=2)
    ends = jnp.concatenate([h_tile[:, :pad], w_tile[:, rows - pad :]], axis=1)
    after, before = both_sides(ends)
    h_long = jnp.concatenate([h_tile, jnp.where(has_next, after[:, :pad], 0.0)], axis=1)
    w_long = jnp.concatenate([jnp.where(has_prev, before[:, pad:], 0.0), w_tile], axis=1)
    first = o * per
    w_den = tree_sum([lax.dynamic_slice_in_dim(h_long, first + d, per, 1) for d in range(pad)])
    h_den = tree_sum([lax.dynamic_slice_in_dim(w_long, first + pad - d, per, 1) for d in range(pad)])

    mask_share = lax.dynamic_slice_in_dim(mask, first, per, 0)
    row_share = lax.dynamic_slice_in_dim(row_factors, first * tile, per * tile, 1)
    col_share = lax.dynamic_slice_in_dim(col_factors, first * tile, per * tile, 1)

    def update(share, numer, den):
        live_share = mask_share[None] > 0
        share = share.reshape(factors, per, tile)
        numer = jnp.swapaxes(numer, 0, 1)
        den = jnp.where(live_share, den[:, :, None] * mask_share[None], 1.0)
        new = jnp.where(live_share, share * (numer * factor * factor) / den, share)
        return new.reshape(factors, per * tile)

    row_update = update(row_share, scatter_sum(w_parts), w_den)
    col_update = update(col_share, scatter_sum(h_parts), h_den)
    return bias, row_update, col_update


def solution(mesh):
    return jax.shard_map(
        per_device,
        mesh=mesh,
        in_specs=(
            P("genome", "offset", None, None),
            P("offset"),
            P("genome"),
            P(None, "genome"),
            P(None, "genome"),
        ),
        out_specs=(P("genome"), P(None, ("genome", "offset")), P(None, ("genome", "offset"))),
        check_vma=False,
    )
```

```python
import functools

import jax
import jax.numpy as jnp
from jax import lax
from jax.experimental import pallas as pl
from jax.experimental.pallas import tpu as pltpu
from jax.sharding import PartitionSpec as P

ITERS = 3
STEP = 8
EARLY = 2
F32 = jnp.float32
BF16 = jnp.bfloat16
VMEM_LIMIT = 20 * 1024 * 1024
NT = (((1,), (1,)), ((), ()))
TN = (((0,), (0,)), ((), ()))


def split(x):
    hi = x.astype(BF16)
    lo = (x - hi.astype(F32)).astype(BF16)
    return hi, lo


def tree_sum(parts):
    while len(parts) > 1:
        parts = [a + b for a, b in zip(parts[::2], parts[1::2])]
    return parts[0]


def params():
    return pltpu.CompilerParams(vmem_limit_bytes=VMEM_LIMIT)


def scale_from(mask, parts):
    cover = tree_sum([p[...] for p in parts])
    live = mask[...] > 0
    return jnp.where(live, 1.0 / jnp.where(live, cover, 1.0), 0.0)


def vmem():
    return pl.BlockSpec(memory_space=pltpu.VMEM)


def kernel_call(body, name, scalars, args, outs, scratch=(), aliases=None, specs=None):
    return pl.pallas_call(
        body,
        grid_spec=pltpu.PrefetchScalarGridSpec(
            num_scalar_prefetch=1,
            grid=(1,),
            in_specs=specs or [vmem() for _ in args],
            out_specs=[vmem() for _ in outs],
            scratch_shapes=list(scratch),
        ),
        out_shape=outs,
        input_output_aliases=aliases or {},
        compiler_params=params(),
        name=name,
    )(scalars, *args)


def by_diagonal(offs, slots, go):
    for s in range(slots):

        @pl.when(offs[s] == 0)
        def _():
            go(s)

    @pl.when(functools.reduce(jnp.logical_and, [offs[s] != 0 for s in range(slots)]))
    def _():
        go(-1)


def tile_value(counts, i, s, diagonal):
    c = counts[i, s].astype(F32)
    if s == diagonal:
        tile = c.shape[0]
        r = lax.broadcasted_iota(jnp.int32, (tile, tile), 0)
        q = lax.broadcasted_iota(jnp.int32, (tile, tile), 1)
        c = jnp.where(r < q, c, jnp.where(r == q, 0.5 * c, 0.0))
    return c


def cover_block(offs, counts, u_ref, acc, base, diagonal, kept=None):
    slots, tile = counts.shape[1:3]
    ones = jnp.ones((8, tile), BF16)
    u_block = u_ref[pl.ds(base, STEP), :]
    u_cols = u_block.T
    u_across = [u_ref[pl.ds(base + offs[s], STEP), :] for s in range(slots)]
    cols = [[] for _ in range(slots)]
    sums = []
    for t in range(STEP):
        total = None
        for s in range(slots):
            c = tile_value(counts, base + t, s, diagonal)
            if kept is not None:
                kept[base + t, s] = c
            term = c * u_across[s][t : t + 1]
            total = term if total is None else total + term
            cols[s].append(jnp.sum(c * u_cols[:, t : t + 1], axis=0, keepdims=True))
        hi, lo = split(total)
        row = lax.dot_general(ones, hi, NT, preferred_element_type=F32)
        row = row + lax.dot_general(ones, lo, NT, preferred_element_type=F32)
        sums.append(row[:1])
    acc[pl.ds(base, STEP), :] += jnp.concatenate(sums, axis=0)
    for s in range(slots):
        acc[pl.ds(base + offs[s], STEP), :] += jnp.concatenate(cols[s], axis=0)


def cover_edge_kernel(first, rows, offs, counts, mask, *refs):
    v_out, edge_out, u_out = refs[-3:]
    pad = mask.shape[0] - rows
    u_out[...] = mask[...] if first else scale_from(mask, refs[:-4])
    v_out[...] = jnp.zeros_like(v_out)

    def go(diagonal):
        for base in list(range(0, pad, STEP)) + list(range(rows - pad, rows, STEP)):
            cover_block(offs, counts, u_out, v_out, base, diagonal)

    if first:
        by_diagonal(offs, counts.shape[1], go)
    else:
        go(-1)
    edge_out[:pad] = v_out[:pad]
    edge_out[pad:] = v_out[rows:]


def cover_main_kernel(first, rows, offs, counts, u_ref, edge_v, v_out, *keep):
    kept = keep[0] if first else None
    pad = edge_v.shape[0] - rows
    v_out[...] = edge_v[...]

    def go(diagonal):
        def body(b, carry):
            cover_block(offs, counts, u_ref, v_out, pl.multiple_of(b * STEP, STEP), diagonal, kept)
            return carry

        lax.fori_loop(pad // STEP, (rows - pad) // STEP, body, 0)
        if first:

            def copy(i, carry):
                for s in range(counts.shape[1]):
                    kept[i, s] = tile_value(counts, i, s, diagonal)
                return carry

            lax.fori_loop(0, pad, copy, 0, unroll=4)
            lax.fori_loop(rows - pad, rows, copy, 0, unroll=4)

    if first:
        by_diagonal(offs, counts.shape[1], go)
    else:
        go(-1)


def cover_edge(offs, counts, mask_ext, parts, after):
    rows, tile = counts.shape[0], counts.shape[2]
    ext = mask_ext.shape[0]
    flat = jax.ShapeDtypeStruct((ext, tile), F32)
    edge = jax.ShapeDtypeStruct((2 * (ext - rows), tile), F32)
    return kernel_call(
        functools.partial(cover_edge_kernel, not parts, rows),
        "cover_edge",
        offs,
        [counts, mask_ext, *parts] + ([after] if parts else []),
        [flat, edge, flat],
    )


def cover_main(offs, counts, u, edge_v, first):
    outs = [jax.ShapeDtypeStruct(u.shape, F32)]
    if first:
        outs.append(pltpu.VMEM(counts.shape, F32))
    return kernel_call(
        functools.partial(cover_main_kernel, first, counts.shape[0]),
        "cover_main",
        offs,
        [counts, u, edge_v],
        outs,
    )


def ratio_kernel(start, count, offs, kept, w_ref, h_ref, after, *refs):
    hi_out, lo_out, h_terms = refs[-3:]
    rows, slots, tile = kept.shape[:3]
    pad = h_ref.shape[1] // tile - rows

    def prepare(j, carry):
        hi, lo = split(h_ref[:, pl.ds(pl.multiple_of(j * tile, tile), tile)])
        h_terms[j - start] = jnp.concatenate([hi, lo, hi, lo], axis=0)
        return carry

    lax.fori_loop(start, start + count + pad, prepare, 0, unroll=4)

    def go(diagonal):
        def body(i, carry):
            hi, lo = split(w_ref[:, pl.ds(pl.multiple_of(i * tile, tile), tile)])
            w_terms = jnp.concatenate([hi, hi, lo, lo], axis=0)
            for s in range(slots):
                model = lax.dot_general(
                    w_terms, h_terms[i - start + offs[s]], TN, preferred_element_type=F32
                )
                values = kept[i, s]
                if s == diagonal:
                    values = values + values.T
                r_hi, r_lo = split(values * (1.0 / model))
                hi_out[i, :, s * tile : (s + 1) * tile] = r_hi
                lo_out[i, :, s * tile : (s + 1) * tile] = r_lo
            return carry

        lax.fori_loop(start, start + count, body, 0, unroll=4)

    by_diagonal(offs, slots, go)


def ratio(offs, kept, row_factors, col_ext, after, earlier, start, count):
    rows, slots, tile = kept.shape[:3]
    factors = row_factors.shape[0]
    pad = col_ext.shape[1] // tile - rows
    out = pltpu.VMEM((rows, tile, slots * tile), BF16)
    return kernel_call(
        functools.partial(ratio_kernel, start, count),
        "ratio",
        offs,
        [kept, row_factors, col_ext, after, *earlier],
        [out, out],
        [pltpu.VMEM((count + pad, 4 * factors, tile), BF16)],
        {5: 0, 6: 1} if earlier else {},
    )


def row_numer(offs, g_all, hi_ref, lo_ref, u_ref, i):
    slots = hi_ref.shape[2] // g_all.shape[2]
    factors = g_all.shape[1] // 2
    g = jnp.concatenate([g_all[i + offs[s]] for s in range(slots)], axis=1)
    big = lax.dot_general(g, hi_ref[i], NT, preferred_element_type=F32)
    small = lax.dot_general(g[:factors], lo_ref[i], NT, preferred_element_type=F32)
    return (big[:factors] + big[factors:] + small) * u_ref[pl.ds(i, 1), :]


def col_numer(w_ref, hi_ref, lo_ref, u_ref, i):
    tile = u_ref.shape[1]
    factors = w_ref.shape[0]
    w = w_ref[:, pl.ds(pl.multiple_of(i * tile, tile), tile)]
    hi, lo = split(w * u_ref[pl.ds(i, 1), :])
    big = jnp.dot(jnp.concatenate([hi, lo], axis=0), hi_ref[i], preferred_element_type=F32)
    small = jnp.dot(hi, lo_ref[i], preferred_element_type=F32)
    return big[:factors] + big[factors:] + small


def col_loop(offs, w_ref, hi_ref, lo_ref, u_ref, acc, start, stop, shift):
    tile = u_ref.shape[1]

    def body(i, carry):
        cols = col_numer(w_ref, hi_ref, lo_ref, u_ref, i)
        for s in range(hi_ref.shape[2] // tile):
            acc[i + offs[s] - shift] += cols[:, s * tile : (s + 1) * tile]
        return carry

    lax.fori_loop(start, stop, body, 0, unroll=4)


def numer_first_kernel(rows, shares, scal, hi_ref, lo_ref, w_ref, h_ref, mask, *refs):
    parts = refs[:shares]
    u_out, g_out, piece_out, tail_out, acc = refs[shares:]
    offs = [scal[1 + s] for s in range(hi_ref.shape[2] // mask.shape[1])]
    ext, tile = mask.shape
    factors = w_ref.shape[0]
    pad = ext - rows
    per = rows // shares
    u_out[...] = scale_from(mask, parts)
    acc[...] = jnp.zeros_like(acc)

    col_loop(offs, w_ref, hi_ref, lo_ref, u_out, acc, rows - pad, rows, rows - pad)
    for t in range(pad):
        tail_out[t] = acc[pad + t] * u_out[rows + t : rows + t + 1, :]

    def fill(j, carry):
        x = h_ref[:, pl.ds(pl.multiple_of(j * tile, tile), tile)] * u_out[pl.ds(j, 1), :]
        hi, lo = split(x)
        g_out[j, :factors] = hi
        g_out[j, factors:] = lo
        return carry

    lax.fori_loop(0, ext, fill, 0, unroll=4)
    first = jnp.bitwise_xor(scal[0], EARLY) * per

    def body(t, carry):
        piece_out[t] = row_numer(offs, g_out, hi_ref, lo_ref, u_out, first + t)
        return carry

    lax.fori_loop(0, per, body, 0, unroll=4)


def numer_row_kernel(order, scal, hi_ref, lo_ref, g_ref, u_ref, *outs):
    offs = [scal[1 + s] for s in range(hi_ref.shape[2] // u_ref.shape[1])]
    per = outs[0].shape[0]
    for k, out in zip(order, outs):
        first = jnp.bitwise_xor(scal[0], k) * per

        def body(t, carry):
            out[t] = row_numer(offs, g_ref, hi_ref, lo_ref, u_ref, first + t)
            return carry

        lax.fori_loop(0, per, body, 0, unroll=4)


def numer_col_kernel(rows, scal, hi_ref, lo_ref, w_ref, u_ref, arrived, *refs):
    outs, acc = refs[:-1], refs[-1]
    offs = [scal[1 + s] for s in range(hi_ref.shape[2] // u_ref.shape[1])]
    per = outs[0].shape[0]
    pad = arrived.shape[0]
    acc[...] = jnp.zeros_like(acc)
    col_loop(offs, w_ref, hi_ref, lo_ref, u_ref, acc, 0, rows, 0)
    for k, out in enumerate(outs):
        share = jnp.bitwise_xor(scal[0], k)
        first = share * per

        def body(t, carry):
            out[t] = acc[first + t] * u_ref[pl.ds(first + t, 1), :]
            return carry

        lax.fori_loop(0, per, body, 0, unroll=4)
        for s in range(-(-pad // per)):

            @pl.when(share == s)
            def _():
                count = min(per, pad - s * per)
                out[:count] += arrived[s * per : s * per + count]


def numer_first(scal, r_hi, r_lo, row_factors, col_ext, mask_ext, parts):
    shares = len(parts)
    rows, tile = r_hi.shape[:2]
    factors = row_factors.shape[0]
    ext = mask_ext.shape[0]
    pad = ext - rows
    outs = [
        jax.ShapeDtypeStruct((ext, tile), F32),
        pltpu.VMEM((ext, 2 * factors, tile), BF16),
        jax.ShapeDtypeStruct((rows // shares, factors, tile), F32),
        jax.ShapeDtypeStruct((pad, factors, tile), F32),
    ]
    return kernel_call(
        functools.partial(numer_first_kernel, rows, shares),
        "numer_first",
        scal,
        [r_hi, r_lo, row_factors, col_ext, mask_ext, *parts],
        outs,
        [pltpu.VMEM((2 * pad, factors, tile), F32)],
    )


def numer_row(scal, r_hi, r_lo, g_all, u, order, shares):
    rows, tile = r_hi.shape[:2]
    piece = jax.ShapeDtypeStruct((rows // shares, g_all.shape[1] // 2, tile), F32)
    return kernel_call(
        functools.partial(numer_row_kernel, order),
        "numer_row",
        scal,
        [r_hi, r_lo, g_all, u],
        [piece] * len(order),
    )


def numer_col(scal, r_hi, r_lo, row_factors, u, arrived, shares):
    rows, tile = r_hi.shape[:2]
    factors = row_factors.shape[0]
    piece = jax.ShapeDtypeStruct((rows // shares, factors, tile), F32)
    return kernel_call(
        functools.partial(numer_col_kernel, rows),
        "numer_col",
        scal,
        [r_hi, r_lo, row_factors, u, arrived],
        [piece] * shares,
        [pltpu.VMEM((u.shape[0], factors, tile), F32)],
    )


def update_kernel(scal, factor_ref, mask, den, scale, *refs):
    terms, out = refs[:-1], refs[-1]
    per, _, tile = terms[0].shape
    c = scale[...]
    for t in range(per):
        at = slice(t * tile, (t + 1) * tile)
        live = mask[pl.ds(scal[0] * per + t, 1), :]
        numer = terms[0][t]
        for term in terms[1:]:
            numer = numer + term[t]
        old = factor_ref[:, at]
        lower = jnp.where(live > 0, den[:, t : t + 1] * live, 1.0)
        out[:, at] = jnp.where(live > 0, old * (numer * c * c) / lower, old)


def update(scal, factors, mask, den, scale, terms):
    count = factors.shape[0]
    per, _, tile = terms[0].shape
    specs = [pl.BlockSpec((count, per * tile), lambda i, scal: (0, scal[0]))]
    specs += [vmem() for _ in range(3 + len(terms))]
    return kernel_call(
        update_kernel,
        "update",
        scal,
        [factors, mask, den, scale, *terms],
        [jax.ShapeDtypeStruct((count, per * tile), F32)],
        specs=specs,
    )[0]


def xor_exchange(x, axis, k):
    return lax.ppermute(x, axis, [(i, i ^ k) for i in range(lax.axis_size(axis))])


def both_sides(x):
    size = lax.axis_size("genome")
    me = lax.axis_index("genome")
    a = lax.ppermute(x, "genome", [(i, i ^ 1) for i in range(size)])
    b = lax.ppermute(x, "genome", [(i, (((i + 1) ^ 1) - 1) % size) for i in range(size)])
    even = me % 2 == 0
    return jnp.where(even, a, b), jnp.where(even, b, a)


def scatter_terms(pieces):
    size = lax.axis_size("offset")
    if size == 4:
        first = xor_exchange(pieces[EARLY], "offset", 1)
        mine = xor_exchange(pieces[1], "offset", 1)
        far = xor_exchange(pieces[3] + first, "offset", 3)
        return [pieces[0], mine, far]
    return [pieces[0]] + [xor_exchange(pieces[k], "offset", k) for k in range(1, size)]


def per_device(counts, band_offset, bin_mask, row_factors, col_factors):
    rows, slots, tile = counts.shape[:3]
    factors = row_factors.shape[0]
    offset_count = lax.axis_size("offset")
    genome_count = lax.axis_size("genome")
    g = lax.axis_index("genome")
    o = lax.axis_index("offset")
    reach = slots * offset_count - 1
    pad = reach + 1
    offs = band_offset.astype(jnp.int32)
    scal = jnp.concatenate([o.astype(jnp.int32).reshape(1), offs])
    has_next = g < genome_count - 1
    has_prev = g > 0

    mask = bin_mask.astype(F32).reshape(rows, tile)
    mask_next, _ = both_sides(mask[:pad])
    keep = has_next & (lax.broadcasted_iota(jnp.int32, (pad, 1), 0) < reach)
    mask_ext = jnp.concatenate([mask, jnp.where(keep, mask_next, 0.0)])

    ring_left = [(i, (i - 1) % genome_count) for i in range(genome_count)]
    col_next = lax.ppermute(col_factors[:, : pad * tile], "genome", ring_left)
    col_next = jnp.where(has_next, col_next, 1.0)
    col_ext = jnp.concatenate([col_factors, col_next], axis=1)

    scales = []
    parts = []
    source = counts
    ratios = []
    cut = [0] + [(rows * (3 * t + 3) // (8 * STEP)) * STEP for t in range(ITERS - 1)] + [rows]
    for t in range(ITERS):
        edge_v, edge, u = cover_edge(offs, source, mask_ext, parts, ratios[0] if ratios else None)
        scales.append(u[:rows])
        after, before = both_sides(edge)
        res = cover_main(offs, source, u, edge_v, t == 0)
        v = res[0]
        if t == 0:
            source = res[1]
        front = v[:pad] + jnp.where(has_prev, before[pad:], 0.0)
        back = v[rows:] + jnp.where(has_next, after[:pad], 0.0)
        x = jnp.concatenate([front, v[pad:rows], back])
        parts = [x] + [xor_exchange(x, "offset", k) for k in range(1, offset_count)]
        ratios = ratio(offs, source, row_factors, col_ext, x, ratios, cut[t], cut[t + 1] - cut[t])

    r_hi, r_lo = ratios
    u_ext, g_all, early, tail = numer_first(
        scal, r_hi, r_lo, row_factors, col_ext, mask_ext, parts
    )
    u = u_ext[:rows]
    scales.append(u)
    arrived = lax.ppermute(tail, "genome", [(i, (i + 1) % genome_count) for i in range(genome_count)])
    arrived = jnp.where(has_prev, arrived, 0.0)
    order = [k for k in (1, 3, 0, *range(4, offset_count))]
    rest = numer_row(scal, r_hi, r_lo, g_all, u_ext, order, offset_count)
    w_parts = dict(zip(order, rest)) | {EARLY: early}
    w_terms = scatter_terms([w_parts[k] for k in range(offset_count)])
    h_parts = numer_col(scal, r_hi, r_lo, row_factors, u_ext, arrived, offset_count)
    h_terms = scatter_terms(h_parts)

    live = mask > 0
    sums = [jnp.sum(mask)]
    for t in range(ITERS):
        sums.append(jnp.sum(jnp.where(live, scales[t] / jnp.where(live, scales[t + 1], 1.0), 0.0)))
    sums = jnp.broadcast_to(jnp.stack(sums)[:, None], (ITERS + 1, tile))
    k = 1
    while k < genome_count:
        sums = sums + xor_exchange(sums, "genome", k)
        k *= 2
    factor = sums[1, 0] / sums[0, 0]
    for t in range(1, ITERS):
        factor = factor * (sums[t + 1, 0] / sums[0, 0])
    bias = jnp.where(live, u * factor, 0.0).reshape(-1)

    per = rows // offset_count
    h_tile = jnp.sum(col_factors.reshape(factors, rows, tile) * mask[None], axis=2)
    w_tile = jnp.sum(row_factors.reshape(factors, rows, tile) * mask[None], axis=2)
    ends = jnp.concatenate([h_tile[:, :pad], w_tile[:, rows - pad :]], axis=1)
    after, before = both_sides(ends)
    h_long = jnp.concatenate([h_tile, jnp.where(has_next, after[:, :pad], 0.0)], axis=1)
    w_long = jnp.concatenate([jnp.where(has_prev, before[:, pad:], 0.0), w_tile], axis=1)
    first = o * per
    w_den = tree_sum([lax.dynamic_slice_in_dim(h_long, first + d, per, 1) for d in range(pad)])
    h_den = tree_sum([lax.dynamic_slice_in_dim(w_long, first + pad - d, per, 1) for d in range(pad)])

    scale = jnp.broadcast_to(factor.reshape(1, 1), (1, tile))
    row_update = update(scal, row_factors, mask, w_den, scale, w_terms)
    col_update = update(scal, col_factors, mask, h_den, scale, h_terms)
    return bias, row_update, col_update


def solution(mesh):
    return jax.shard_map(
        per_device,
        mesh=mesh,
        in_specs=(
            P("genome", "offset", None, None),
            P("offset"),
            P("genome"),
            P(None, "genome"),
            P(None, "genome"),
        ),
        out_specs=(P("genome"), P(None, ("genome", "offset")), P(None, ("genome", "offset"))),
        check_vma=False,
    )
```

```python
import functools

import jax
import jax.numpy as jnp
from jax import lax
from jax.experimental import pallas as pl
from jax.experimental.pallas import tpu as pltpu
from jax.sharding import PartitionSpec as P

ITERS = 3
STEP = 8
EARLY = 2
F32 = jnp.float32
BF16 = jnp.bfloat16
VMEM_LIMIT = 20 * 1024 * 1024
NT = (((1,), (1,)), ((), ()))
TN = (((0,), (0,)), ((), ()))


def split(x):
    hi = x.astype(BF16)
    lo = (x - hi.astype(F32)).astype(BF16)
    return hi, lo


def tree_sum(parts):
    while len(parts) > 1:
        parts = [a + b for a, b in zip(parts[::2], parts[1::2])]
    return parts[0]


def params():
    return pltpu.CompilerParams(vmem_limit_bytes=VMEM_LIMIT)


def scale_from(mask, parts):
    cover = tree_sum([p[...] for p in parts])
    live = mask[...] > 0
    return jnp.where(live, 1.0 / jnp.where(live, cover, 1.0), 0.0)


def vmem():
    return pl.BlockSpec(memory_space=pltpu.VMEM)


def kernel_call(body, name, scalars, args, outs, scratch=(), aliases=None, specs=None):
    return pl.pallas_call(
        body,
        grid_spec=pltpu.PrefetchScalarGridSpec(
            num_scalar_prefetch=1,
            grid=(1,),
            in_specs=specs or [vmem() for _ in args],
            out_specs=[vmem() for _ in outs],
            scratch_shapes=list(scratch),
        ),
        out_shape=outs,
        input_output_aliases=aliases or {},
        compiler_params=params(),
        name=name,
    )(scalars, *args)


def by_diagonal(offs, slots, go):
    for s in range(slots):

        @pl.when(offs[s] == 0)
        def _():
            go(s)

    @pl.when(functools.reduce(jnp.logical_and, [offs[s] != 0 for s in range(slots)]))
    def _():
        go(-1)


def tile_value(counts, i, s, diagonal):
    c = counts[i, s].astype(F32)
    if s == diagonal:
        tile = c.shape[0]
        r = lax.broadcasted_iota(jnp.int32, (tile, tile), 0)
        q = lax.broadcasted_iota(jnp.int32, (tile, tile), 1)
        c = jnp.where(r < q, c, jnp.where(r == q, 0.5 * c, 0.0))
    return c


def cover_block(offs, counts, u_ref, acc, base, diagonal, kept=None):
    slots, tile = counts.shape[1:3]
    ones = jnp.ones((8, tile), BF16)
    u_block = u_ref[pl.ds(base, STEP), :]
    u_cols = u_block.T
    u_across = [u_ref[pl.ds(base + offs[s], STEP), :] for s in range(slots)]
    cols = [[] for _ in range(slots)]
    sums = []
    for t in range(STEP):
        total = None
        for s in range(slots):
            c = tile_value(counts, base + t, s, diagonal)
            if kept is not None:
                kept[base + t, s] = c
            term = c * u_across[s][t : t + 1]
            total = term if total is None else total + term
            cols[s].append(jnp.sum(c * u_cols[:, t : t + 1], axis=0, keepdims=True))
        hi, lo = split(total)
        row = lax.dot_general(ones, hi, NT, preferred_element_type=F32)
        row = row + lax.dot_general(ones, lo, NT, preferred_element_type=F32)
        sums.append(row[:1])
    acc[pl.ds(base, STEP), :] += jnp.concatenate(sums, axis=0)
    for s in range(slots):
        acc[pl.ds(base + offs[s], STEP), :] += jnp.concatenate(cols[s], axis=0)


def cover_edge_kernel(first, rows, offs, counts, mask, *refs):
    v_out, edge_out, u_out = refs[-3:]
    pad = mask.shape[0] - rows
    u_out[...] = mask[...] if first else scale_from(mask, refs[:-4])
    v_out[...] = jnp.zeros_like(v_out)

    def go(diagonal):
        for base in list(range(0, pad, STEP)) + list(range(rows - pad, rows, STEP)):
            cover_block(offs, counts, u_out, v_out, base, diagonal)

    if first:
        by_diagonal(offs, counts.shape[1], go)
    else:
        go(-1)
    edge_out[:pad] = v_out[:pad]
    edge_out[pad:] = v_out[rows:]


def cover_main_kernel(first, rows, offs, counts, u_ref, edge_v, v_out, *keep):
    kept = keep[0] if first else None
    pad = edge_v.shape[0] - rows
    v_out[...] = edge_v[...]

    def go(diagonal):
        def body(b, carry):
            cover_block(offs, counts, u_ref, v_out, pl.multiple_of(b * STEP, STEP), diagonal, kept)
            return carry

        lax.fori_loop(pad // STEP, (rows - pad) // STEP, body, 0)
        if first:

            def copy(i, carry):
                for s in range(counts.shape[1]):
                    kept[i, s] = tile_value(counts, i, s, diagonal)
                return carry

            lax.fori_loop(0, pad, copy, 0, unroll=4)
            lax.fori_loop(rows - pad, rows, copy, 0, unroll=4)

    if first:
        by_diagonal(offs, counts.shape[1], go)
    else:
        go(-1)


def cover_edge(offs, counts, mask_ext, parts, after):
    rows, tile = counts.shape[0], counts.shape[2]
    ext = mask_ext.shape[0]
    flat = jax.ShapeDtypeStruct((ext, tile), F32)
    edge = jax.ShapeDtypeStruct((2 * (ext - rows), tile), F32)
    return kernel_call(
        functools.partial(cover_edge_kernel, not parts, rows),
        "cover_edge",
        offs,
        [counts, mask_ext, *parts] + ([after] if parts else []),
        [flat, edge, flat],
    )


def cover_main(offs, counts, u, edge_v, first):
    outs = [jax.ShapeDtypeStruct(u.shape, F32)]
    if first:
        outs.append(pltpu.VMEM(counts.shape, F32))
    return kernel_call(
        functools.partial(cover_main_kernel, first, counts.shape[0]),
        "cover_main",
        offs,
        [counts, u, edge_v],
        outs,
    )


def ratio_kernel(start, count, offs, kept, w_ref, h_ref, after, *refs):
    hi_out, lo_out, h_terms = refs[-3:]
    rows, slots, tile = kept.shape[:3]
    pad = h_ref.shape[1] // tile - rows

    def prepare(j, carry):
        hi, lo = split(h_ref[:, pl.ds(pl.multiple_of(j * tile, tile), tile)])
        h_terms[j - start] = jnp.concatenate([hi, lo, hi, lo], axis=0)
        return carry

    lax.fori_loop(start, start + count + pad, prepare, 0, unroll=4)

    def go(diagonal):
        def body(i, carry):
            hi, lo = split(w_ref[:, pl.ds(pl.multiple_of(i * tile, tile), tile)])
            w_terms = jnp.concatenate([hi, hi, lo, lo], axis=0)
            for s in range(slots):
                model = lax.dot_general(
                    w_terms, h_terms[i - start + offs[s]], TN, preferred_element_type=F32
                )
                values = kept[i, s]
                if s == diagonal:
                    values = values + values.T
                r_hi, r_lo = split(values * (1.0 / model))
                hi_out[i, :, s * tile : (s + 1) * tile] = r_hi
                lo_out[i, :, s * tile : (s + 1) * tile] = r_lo
            return carry

        lax.fori_loop(start, start + count, body, 0, unroll=4)

    by_diagonal(offs, slots, go)


def ratio(offs, kept, row_factors, col_ext, after, earlier, start, count):
    rows, slots, tile = kept.shape[:3]
    factors = row_factors.shape[0]
    pad = col_ext.shape[1] // tile - rows
    out = pltpu.VMEM((rows, tile, slots * tile), BF16)
    return kernel_call(
        functools.partial(ratio_kernel, start, count),
        "ratio",
        offs,
        [kept, row_factors, col_ext, after, *earlier],
        [out, out],
        [pltpu.VMEM((count + pad, 4 * factors, tile), BF16)],
        {5: 0, 6: 1} if earlier else {},
    )


def row_numer(offs, g_all, hi_ref, lo_ref, u_ref, i):
    slots = hi_ref.shape[2] // g_all.shape[2]
    factors = g_all.shape[1] // 2
    g = jnp.concatenate([g_all[i + offs[s]] for s in range(slots)], axis=1)
    big = lax.dot_general(g, hi_ref[i], NT, preferred_element_type=F32)
    small = lax.dot_general(g[:factors], lo_ref[i], NT, preferred_element_type=F32)
    return (big[:factors] + big[factors:] + small) * u_ref[pl.ds(i, 1), :]


def col_numer(w_ref, hi_ref, lo_ref, u_ref, i):
    tile = u_ref.shape[1]
    factors = w_ref.shape[0]
    w = w_ref[:, pl.ds(pl.multiple_of(i * tile, tile), tile)]
    hi, lo = split(w * u_ref[pl.ds(i, 1), :])
    big = jnp.dot(jnp.concatenate([hi, lo], axis=0), hi_ref[i], preferred_element_type=F32)
    small = jnp.dot(hi, lo_ref[i], preferred_element_type=F32)
    return big[:factors] + big[factors:] + small


def col_loop(offs, w_ref, hi_ref, lo_ref, u_ref, acc, start, stop, shift):
    tile = u_ref.shape[1]

    def body(i, carry):
        cols = col_numer(w_ref, hi_ref, lo_ref, u_ref, i)
        for s in range(hi_ref.shape[2] // tile):
            acc[i + offs[s] - shift] += cols[:, s * tile : (s + 1) * tile]
        return carry

    lax.fori_loop(start, stop, body, 0, unroll=4)


def numer_first_kernel(rows, shares, scal, hi_ref, lo_ref, w_ref, h_ref, mask, *refs):
    parts = refs[:shares]
    u_out, g_out, piece_out, tail_out, acc = refs[shares:]
    offs = [scal[1 + s] for s in range(hi_ref.shape[2] // mask.shape[1])]
    ext, tile = mask.shape
    factors = w_ref.shape[0]
    pad = ext - rows
    per = rows // shares
    u_out[...] = scale_from(mask, parts)
    acc[...] = jnp.zeros_like(acc)

    col_loop(offs, w_ref, hi_ref, lo_ref, u_out, acc, rows - pad, rows, rows - pad)
    for t in range(pad):
        tail_out[t] = acc[pad + t] * u_out[rows + t : rows + t + 1, :]

    def fill(j, carry):
        x = h_ref[:, pl.ds(pl.multiple_of(j * tile, tile), tile)] * u_out[pl.ds(j, 1), :]
        hi, lo = split(x)
        g_out[j, :factors] = hi
        g_out[j, factors:] = lo
        return carry

    lax.fori_loop(0, ext, fill, 0, unroll=4)
    first = jnp.bitwise_xor(scal[0], EARLY) * per

    def body(t, carry):
        piece_out[t] = row_numer(offs, g_out, hi_ref, lo_ref, u_out, first + t)
        return carry

    lax.fori_loop(0, per, body, 0, unroll=4)


def numer_row_kernel(order, rows, scal, hi_ref, lo_ref, g_ref, *refs):
    scales = refs[: ITERS + 1]
    sums_out, outs = refs[ITERS + 1], refs[ITERS + 2 :]
    u_ref = scales[-1]
    offs = [scal[1 + s] for s in range(hi_ref.shape[2] // u_ref.shape[1])]
    per = outs[0].shape[0]
    for k, out in zip(order, outs):
        first = jnp.bitwise_xor(scal[0], k) * per

        def body(t, carry):
            out[t] = row_numer(offs, g_ref, hi_ref, lo_ref, u_ref, first + t)
            return carry

        lax.fori_loop(0, per, body, 0, unroll=4)
    sums_out[...] = jnp.zeros_like(sums_out)
    mask = scales[0][:rows]
    totals = [mask]
    for t in range(ITERS):
        below = jnp.where(mask > 0, scales[t + 1][:rows], 1.0)
        totals.append(jnp.where(mask > 0, scales[t][:rows] / below, 0.0))
    for t, total in enumerate(totals):
        line = jnp.sum(jnp.sum(total, axis=0, keepdims=True), axis=1, keepdims=True)
        sums_out[t : t + 1, :] = jnp.broadcast_to(line, (1, mask.shape[1]))


def numer_col_kernel(rows, scal, hi_ref, lo_ref, w_ref, u_ref, arrived, after, *refs):
    outs, acc = refs[:-1], refs[-1]
    offs = [scal[1 + s] for s in range(hi_ref.shape[2] // u_ref.shape[1])]
    per = outs[0].shape[0]
    pad = arrived.shape[0]
    acc[...] = jnp.zeros_like(acc)
    col_loop(offs, w_ref, hi_ref, lo_ref, u_ref, acc, 0, rows, 0)
    for k, out in enumerate(outs):
        share = jnp.bitwise_xor(scal[0], k)
        first = share * per

        def body(t, carry):
            out[t] = acc[first + t] * u_ref[pl.ds(first + t, 1), :]
            return carry

        lax.fori_loop(0, per, body, 0, unroll=4)
        for s in range(-(-pad // per)):

            @pl.when(share == s)
            def _():
                count = min(per, pad - s * per)
                out[:count] += arrived[s * per : s * per + count]


def numer_first(scal, r_hi, r_lo, row_factors, col_ext, mask_ext, parts):
    shares = len(parts)
    rows, tile = r_hi.shape[:2]
    factors = row_factors.shape[0]
    ext = mask_ext.shape[0]
    pad = ext - rows
    outs = [
        jax.ShapeDtypeStruct((ext, tile), F32),
        pltpu.VMEM((ext, 2 * factors, tile), BF16),
        jax.ShapeDtypeStruct((rows // shares, factors, tile), F32),
        jax.ShapeDtypeStruct((pad, factors, tile), F32),
    ]
    return kernel_call(
        functools.partial(numer_first_kernel, rows, shares),
        "numer_first",
        scal,
        [r_hi, r_lo, row_factors, col_ext, mask_ext, *parts],
        outs,
        [pltpu.VMEM((2 * pad, factors, tile), F32)],
    )


def numer_row(scal, r_hi, r_lo, g_all, scales, order, shares):
    rows, tile = r_hi.shape[:2]
    piece = jax.ShapeDtypeStruct((rows // shares, g_all.shape[1] // 2, tile), F32)
    res = kernel_call(
        functools.partial(numer_row_kernel, order, rows),
        "numer_row",
        scal,
        [r_hi, r_lo, g_all, *scales],
        [jax.ShapeDtypeStruct((8, tile), F32)] + [piece] * len(order),
    )
    return res[0], res[1:]


def numer_col(scal, r_hi, r_lo, row_factors, u, arrived, shares, after):
    rows, tile = r_hi.shape[:2]
    factors = row_factors.shape[0]
    piece = jax.ShapeDtypeStruct((rows // shares, factors, tile), F32)
    return kernel_call(
        functools.partial(numer_col_kernel, rows),
        "numer_col",
        scal,
        [r_hi, r_lo, row_factors, u, arrived, after],
        [piece] * shares,
        [pltpu.VMEM((u.shape[0], factors, tile), F32)],
    )


def mean_scale(sums):
    scale = sums[1:2, :] / sums[0:1, :]
    for t in range(1, ITERS):
        scale = scale * (sums[t + 1 : t + 2, :] / sums[0:1, :])
    return scale


def update_kernel(scal, factor_ref, mask, den, sums, *refs):
    terms, out = refs[:-1], refs[-1]
    per, _, tile = terms[0].shape
    c = mean_scale(sums[...])
    lanes = den.shape[1]
    den_here = pltpu.roll(den[...], lax.rem(lanes - scal[0] * per, lanes), 1)
    for t in range(per):
        at = slice(t * tile, (t + 1) * tile)
        live = mask[pl.ds(scal[0] * per + t, 1), :]
        numer = terms[0][t]
        for term in terms[1:]:
            numer = numer + term[t]
        old = factor_ref[:, at]
        lower = jnp.where(live > 0, den_here[:, t : t + 1] * live, 1.0)
        out[:, at] = jnp.where(live > 0, old * (numer * c * c) / lower, old)


def update(scal, factors, mask, den, sums, terms):
    count = factors.shape[0]
    per, _, tile = terms[0].shape
    specs = [pl.BlockSpec((count, per * tile), lambda i, scal: (0, scal[0]))]
    specs += [vmem() for _ in range(3 + len(terms))]
    return kernel_call(
        update_kernel,
        "update",
        scal,
        [factors, mask, den, sums, *terms],
        [jax.ShapeDtypeStruct((count, per * tile), F32)],
        specs=specs,
    )[0]


def xor_exchange(x, axis, k):
    return lax.ppermute(x, axis, [(i, i ^ k) for i in range(lax.axis_size(axis))])


def both_sides(x, even):
    size = lax.axis_size("genome")
    a = lax.ppermute(x, "genome", [(i, i ^ 1) for i in range(size)])
    b = lax.ppermute(x, "genome", [(i, (((i + 1) ^ 1) - 1) % size) for i in range(size)])
    return jnp.where(even > 0, a, b), jnp.where(even > 0, b, a)


def scatter_terms(pieces):
    size = lax.axis_size("offset")
    if size == 4:
        first = xor_exchange(pieces[EARLY], "offset", 1)
        mine = xor_exchange(pieces[1], "offset", 1)
        far = xor_exchange(pieces[3] + first, "offset", 3)
        return [pieces[0], mine, far]
    return [pieces[0]] + [xor_exchange(pieces[k], "offset", k) for k in range(1, size)]


def per_device(counts, band_offset, bin_mask, row_factors, col_factors):
    rows, slots, tile = counts.shape[:3]
    factors = row_factors.shape[0]
    offset_count = lax.axis_size("offset")
    genome_count = lax.axis_size("genome")
    g = lax.axis_index("genome")
    o = lax.axis_index("offset").astype(jnp.int32)
    reach = slots * offset_count - 1
    pad = reach + 1

    line = jnp.broadcast_to(g, (1, tile))
    even = (line % 2 == 0).astype(F32)
    has_next = (line < genome_count - 1).astype(F32)
    has_prev = (line > 0).astype(F32)
    flags = jnp.concatenate([even, has_next, has_prev])
    scal = jnp.concatenate([jnp.broadcast_to(o, (1,)), band_offset])
    flags, scal, band_offset = lax.optimization_barrier((flags, scal, band_offset))
    even, has_next, has_prev = flags[0:1], flags[1:2], flags[2:3]

    mask = bin_mask.astype(F32).reshape(rows, tile)
    mask_next, _ = both_sides(mask[:pad], even)
    keep = lax.broadcasted_iota(jnp.int32, (pad, 1), 0) < reach
    mask_ext = jnp.concatenate([mask, jnp.where(keep, mask_next * has_next, 0.0)])

    ring_left = [(i, (i - 1) % genome_count) for i in range(genome_count)]
    col_next = lax.ppermute(col_factors[:, : pad * tile], "genome", ring_left)
    col_next = jnp.where(has_next[:, :1] > 0, col_next, 1.0)
    col_ext = jnp.concatenate([col_factors, col_next], axis=1)

    scales = []
    parts = []
    source = counts
    ratios = []
    cut = [0] + [(rows * (3 * t + 3) // (8 * STEP)) * STEP for t in range(ITERS - 1)] + [rows]
    for t in range(ITERS):
        edge_v, edge, u = cover_edge(
            band_offset, source, mask_ext, parts, ratios[0] if ratios else None
        )
        scales.append(u)
        after, before = both_sides(edge, even)
        res = cover_main(band_offset, source, u, edge_v, t == 0)
        v = res[0]
        if t == 0:
            source = res[1]
        front = v[:pad] + before[pad:] * has_prev
        back = v[rows:] + after[:pad] * has_next
        x = jnp.concatenate([front, v[pad:rows], back])
        parts = [x] + [xor_exchange(x, "offset", k) for k in range(1, offset_count)]
        ratios = ratio(
            band_offset, source, row_factors, col_ext, x, ratios, cut[t], cut[t + 1] - cut[t]
        )

    r_hi, r_lo = ratios
    u, g_all, early, tail = numer_first(scal, r_hi, r_lo, row_factors, col_ext, mask_ext, parts)
    scales.append(u)
    ring_right = [(i, (i + 1) % genome_count) for i in range(genome_count)]
    arrived = lax.ppermute(tail, "genome", ring_right) * has_prev
    order = [k for k in (1, 3, 0, *range(4, offset_count))]
    sums, rest = numer_row(scal, r_hi, r_lo, g_all, scales, order, offset_count)
    w_parts = dict(zip(order, rest)) | {EARLY: early}
    w_terms = scatter_terms([w_parts[k] for k in range(offset_count)])
    h_parts = numer_col(scal, r_hi, r_lo, row_factors, u, arrived, offset_count, rest[0])
    h_terms = scatter_terms(h_parts)

    k = 1
    while k < genome_count:
        sums = sums + xor_exchange(sums, "genome", k)
        k *= 2
    bias = (u[:rows] * mean_scale(sums)).reshape(-1)

    h_tile = jnp.sum(col_factors.reshape(factors, rows, tile) * mask[None], axis=2)
    w_tile = jnp.sum(row_factors.reshape(factors, rows, tile) * mask[None], axis=2)
    ends = jnp.concatenate([h_tile[:, :pad], w_tile[:, rows - pad :]], axis=1)
    after, before = both_sides(ends, even[:, :1])
    h_long = jnp.concatenate([h_tile, after[:, :pad] * has_next[:, :1]], axis=1)
    w_long = jnp.concatenate([before[:, pad:] * has_prev[:, :1], w_tile], axis=1)
    w_den = tree_sum([h_long[:, d : d + rows] for d in range(pad)])
    h_den = tree_sum([w_long[:, pad - d : pad - d + rows] for d in range(pad)])
    fill = ((0, 0), (0, -rows % tile))
    w_den = jnp.pad(w_den, fill)
    h_den = jnp.pad(h_den, fill)

    row_update = update(scal, row_factors, mask, w_den, sums, w_terms)
    col_update = update(scal, col_factors, mask, h_den, sums, h_terms)
    return bias, row_update, col_update


def solution(mesh):
    return jax.shard_map(
        per_device,
        mesh=mesh,
        in_specs=(
            P("genome", "offset", None, None),
            P("offset"),
            P("genome"),
            P(None, "genome"),
            P(None, "genome"),
        ),
        out_specs=(P("genome"), P(None, ("genome", "offset")), P(None, ("genome", "offset"))),
        check_vma=False,
    )
```

```python
import functools

import jax
import jax.numpy as jnp
from jax import lax
from jax.experimental import pallas as pl
from jax.experimental.pallas import tpu as pltpu
from jax.sharding import PartitionSpec as P

ITERS = 3
STEP = 8
F32 = jnp.float32
BF16 = jnp.bfloat16
VMEM_LIMIT = 20 * 1024 * 1024
NT = (((1,), (1,)), ((), ()))
TN = (((0,), (0,)), ((), ()))


def split(x):
    hi = x.astype(BF16)
    lo = (x - hi.astype(F32)).astype(BF16)
    return hi, lo


def tree_sum(parts):
    while len(parts) > 1:
        parts = [a + b for a, b in zip(parts[::2], parts[1::2])]
    return parts[0]


def params():
    return pltpu.CompilerParams(vmem_limit_bytes=VMEM_LIMIT)


def scale_from(mask, parts):
    cover = tree_sum([p[...] for p in parts])
    live = mask[...] > 0
    return jnp.where(live, 1.0 / jnp.where(live, cover, 1.0), 0.0)


def vmem():
    return pl.BlockSpec(memory_space=pltpu.VMEM)


def kernel_call(body, name, scalars, args, outs, scratch=(), aliases=None, specs=None):
    return pl.pallas_call(
        body,
        grid_spec=pltpu.PrefetchScalarGridSpec(
            num_scalar_prefetch=1,
            grid=(1,),
            in_specs=specs or [vmem() for _ in args],
            out_specs=[vmem() for _ in outs],
            scratch_shapes=list(scratch),
        ),
        out_shape=outs,
        input_output_aliases=aliases or {},
        compiler_params=params(),
        name=name,
    )(scalars, *args)


def offsets(scal, slots):
    return [scal[1 + s] for s in range(slots)]


def by_diagonal(offs, slots, go):
    for s in range(slots):

        @pl.when(offs[s] == 0)
        def _():
            go(s)

    @pl.when(functools.reduce(jnp.logical_and, [offs[s] != 0 for s in range(slots)]))
    def _():
        go(-1)


def tile_value(counts, i, s, diagonal):
    c = counts[i, s].astype(F32)
    if s == diagonal:
        tile = c.shape[0]
        r = lax.broadcasted_iota(jnp.int32, (tile, tile), 0)
        q = lax.broadcasted_iota(jnp.int32, (tile, tile), 1)
        c = jnp.where(r < q, c, jnp.where(r == q, 0.5 * c, 0.0))
    return c


def cover_block(offs, counts, u_ref, acc, base, diagonal, at, kept=None):
    slots, tile = counts.shape[1:3]
    ones = jnp.ones((8, tile), BF16)
    u_block = u_ref[pl.ds(base, STEP), :]
    u_cols = u_block.T
    u_across = [u_ref[pl.ds(base + offs[s], STEP), :] for s in range(slots)]
    cols = [[] for _ in range(slots)]
    sums = []
    for t in range(STEP):
        total = None
        for s in range(slots):
            c = tile_value(counts, at + t, s, diagonal)
            if kept is not None:
                kept[base + t, s] = c
            term = c * u_across[s][t : t + 1]
            total = term if total is None else total + term
            cols[s].append(jnp.sum(c * u_cols[:, t : t + 1], axis=0, keepdims=True))
        hi, lo = split(total)
        row = lax.dot_general(ones, hi, NT, preferred_element_type=F32)
        row = row + lax.dot_general(ones, lo, NT, preferred_element_type=F32)
        sums.append(row[:1])
    acc[pl.ds(base, STEP), :] += jnp.concatenate(sums, axis=0)
    for s in range(slots):
        acc[pl.ds(base + offs[s], STEP), :] += jnp.concatenate(cols[s], axis=0)


def block_copies(hbm, buffer, sems, bases):
    return [
        pltpu.make_async_copy(
            hbm.at[pl.ds(base, STEP)], buffer.at[pl.ds(k * STEP, STEP)], sems.at[k]
        )
        for k, base in enumerate(bases)
    ]


def edge_bases(rows, pad):
    return list(range(0, pad, STEP)) + list(range(rows - pad, rows, STEP))


def write_edge(v_out, edge_out, rows):
    pad = v_out.shape[0] - rows
    edge_out[:pad] = v_out[:pad]
    edge_out[pad:] = v_out[rows:]


def first_edge_kernel(scal, hbm, u_ref, v_out, edge_out, kept, buffer, sems):
    rows, slots = hbm.shape[:2]
    offs = offsets(scal, slots)
    bases = edge_bases(rows, u_ref.shape[0] - rows)
    copies = block_copies(hbm, buffer, sems, bases)
    for copy in copies:
        copy.start()
    v_out[...] = jnp.zeros_like(v_out)
    for copy in copies:
        copy.wait()

    def go(diagonal):
        for k, base in enumerate(bases):
            cover_block(offs, buffer, u_ref, v_out, base, diagonal, k * STEP, kept)

    by_diagonal(offs, slots, go)
    write_edge(v_out, edge_out, rows)


def first_main_kernel(scal, hbm, u_ref, edge_v, kept_in, v_out, kept, buffer, sems):
    rows, slots = hbm.shape[:2]
    offs = offsets(scal, slots)
    pad = u_ref.shape[0] - rows
    bases = list(range(pad, rows - pad, STEP))
    copies = block_copies(hbm, buffer, sems, bases)
    for copy in copies:
        copy.start()
    v_out[...] = edge_v[...]

    def go(diagonal):
        for k, base in enumerate(bases):
            copies[k].wait()
            cover_block(offs, buffer, u_ref, v_out, base, diagonal, k * STEP, kept)

    by_diagonal(offs, slots, go)


def edge_kernel(scal, kept, mask, *refs):
    v_out, edge_out, u_out = refs[-3:]
    rows, slots = kept.shape[:2]
    offs = offsets(scal, slots)
    u_out[...] = scale_from(mask, refs[:-4])
    v_out[...] = jnp.zeros_like(v_out)
    for base in edge_bases(rows, mask.shape[0] - rows):
        cover_block(offs, kept, u_out, v_out, base, -1, base)
    write_edge(v_out, edge_out, rows)


def main_kernel(scal, kept, u_ref, edge_v, v_out):
    rows, slots = kept.shape[:2]
    offs = offsets(scal, slots)
    pad = edge_v.shape[0] - rows
    v_out[...] = edge_v[...]
    for base in range(pad, rows - pad, STEP):
        cover_block(offs, kept, u_ref, v_out, base, -1, base)


def first_edge(scal, counts, u):
    rows, slots, tile = counts.shape[:3]
    ext = u.shape[0]
    pad = ext - rows
    outs = [
        jax.ShapeDtypeStruct(u.shape, F32),
        jax.ShapeDtypeStruct((2 * pad, tile), F32),
        pltpu.VMEM(counts.shape, F32),
    ]
    return kernel_call(
        first_edge_kernel,
        "first_edge",
        scal,
        [counts, u],
        outs,
        [
            pltpu.VMEM((2 * pad, slots, tile, tile), counts.dtype),
            pltpu.SemaphoreType.DMA((2 * pad // STEP,)),
        ],
        specs=[pl.BlockSpec(memory_space=pltpu.HBM), vmem()],
    )


def first_main(scal, counts, u, edge_v, kept):
    rows, slots, tile = counts.shape[:3]
    inner = rows - 2 * (u.shape[0] - rows)
    outs = [jax.ShapeDtypeStruct(u.shape, F32), pltpu.VMEM(counts.shape, F32)]
    return kernel_call(
        first_main_kernel,
        "first_main",
        scal,
        [counts, u, edge_v, kept],
        outs,
        [
            pltpu.VMEM((inner, slots, tile, tile), counts.dtype),
            pltpu.SemaphoreType.DMA((inner // STEP,)),
        ],
        aliases={4: 1},
        specs=[pl.BlockSpec(memory_space=pltpu.HBM), vmem(), vmem(), vmem()],
    )


def cover_edge(scal, kept, mask_ext, parts, after):
    rows, tile = kept.shape[0], kept.shape[2]
    flat = jax.ShapeDtypeStruct(mask_ext.shape, F32)
    edge = jax.ShapeDtypeStruct((2 * (mask_ext.shape[0] - rows), tile), F32)
    args = [kept, mask_ext, *parts, after]
    return kernel_call(edge_kernel, "cover_edge", scal, args, [flat, edge, flat])


def cover_main(scal, kept, u, edge_v):
    outs = [jax.ShapeDtypeStruct(u.shape, F32)]
    return kernel_call(main_kernel, "cover_main", scal, [kept, u, edge_v], outs)[0]


def ratio_kernel(start, count, scal, kept, w_ref, h_ref, after, *refs):
    hi_out, lo_out, h_terms = refs[-3:]
    rows, slots, tile = kept.shape[:3]
    offs = offsets(scal, slots)
    pad = h_ref.shape[1] // tile - rows

    def prepare(j, carry):
        hi, lo = split(h_ref[:, pl.ds(pl.multiple_of(j * tile, tile), tile)])
        h_terms[j - start] = jnp.concatenate([hi, lo, hi, lo], axis=0)
        return carry

    lax.fori_loop(start, start + count + pad, prepare, 0, unroll=4)

    def go(diagonal):
        def body(i, carry):
            hi, lo = split(w_ref[:, pl.ds(pl.multiple_of(i * tile, tile), tile)])
            w_terms = jnp.concatenate([hi, hi, lo, lo], axis=0)
            for s in range(slots):
                model = lax.dot_general(
                    w_terms, h_terms[i - start + offs[s]], TN, preferred_element_type=F32
                )
                values = kept[i, s]
                if s == diagonal:
                    values = values + values.T
                r_hi, r_lo = split(values * (1.0 / model))
                hi_out[i, :, s * tile : (s + 1) * tile] = r_hi
                lo_out[i, :, s * tile : (s + 1) * tile] = r_lo
            return carry

        lax.fori_loop(start, start + count, body, 0, unroll=4)

    by_diagonal(offs, slots, go)


def ratio(scal, kept, row_factors, col_ext, after, earlier, start, count):
    rows, slots, tile = kept.shape[:3]
    factors = row_factors.shape[0]
    pad = col_ext.shape[1] // tile - rows
    out = pltpu.VMEM((rows, tile, slots * tile), BF16)
    return kernel_call(
        functools.partial(ratio_kernel, start, count),
        "ratio",
        scal,
        [kept, row_factors, col_ext, after, *earlier],
        [out, out],
        [pltpu.VMEM((count + pad, 4 * factors, tile), BF16)],
        {5: 0, 6: 1} if earlier else {},
    )


def row_numer(offs, g_all, hi_ref, lo_ref, u_ref, i):
    slots = hi_ref.shape[2] // g_all.shape[2]
    factors = g_all.shape[1] // 2
    g = jnp.concatenate([g_all[i + offs[s]] for s in range(slots)], axis=1)
    big = lax.dot_general(g, hi_ref[i], NT, preferred_element_type=F32)
    small = lax.dot_general(g[:factors], lo_ref[i], NT, preferred_element_type=F32)
    return (big[:factors] + big[factors:] + small) * u_ref[pl.ds(i, 1), :]


def col_numer(w_ref, hi_ref, lo_ref, u_ref, i):
    tile = u_ref.shape[1]
    factors = w_ref.shape[0]
    w = w_ref[:, pl.ds(pl.multiple_of(i * tile, tile), tile)]
    hi, lo = split(w * u_ref[pl.ds(i, 1), :])
    big = jnp.dot(jnp.concatenate([hi, lo], axis=0), hi_ref[i], preferred_element_type=F32)
    small = jnp.dot(hi, lo_ref[i], preferred_element_type=F32)
    return big[:factors] + big[factors:] + small


def col_loop(offs, w_ref, hi_ref, lo_ref, u_ref, acc, start, stop, shift):
    tile = u_ref.shape[1]

    def body(i, carry):
        cols = col_numer(w_ref, hi_ref, lo_ref, u_ref, i)
        for s in range(hi_ref.shape[2] // tile):
            acc[i + offs[s] - shift] += cols[:, s * tile : (s + 1) * tile]
        return carry

    lax.fori_loop(start, stop, body, 0, unroll=4)


def row_pieces(scal, offs, g_ref, hi_ref, lo_ref, u_ref, order, outs):
    for k, out in zip(order, outs):
        per = out.shape[0]
        first = jnp.bitwise_xor(scal[0], k) * per

        def body(t, carry):
            out[t] = row_numer(offs, g_ref, hi_ref, lo_ref, u_ref, first + t)
            return carry

        lax.fori_loop(0, per, body, 0, unroll=4)


def numer_col_kernel(shares, scal, hi_ref, lo_ref, w_ref, mask, *refs):
    parts, scales, refs = refs[:shares], refs[shares : shares + ITERS], refs[shares + ITERS :]
    u_out, tail_out, sums_out = refs[:3]
    outs, acc = refs[3:-1], refs[-1]
    rows = hi_ref.shape[0]
    ext, tile = mask.shape
    offs = offsets(scal, hi_ref.shape[2] // tile)
    per = rows // shares
    u_out[...] = scale_from(mask, parts)
    acc[...] = jnp.zeros_like(acc)
    col_loop(offs, w_ref, hi_ref, lo_ref, u_out, acc, 0, rows, 0)
    for k, out in enumerate(outs):
        first = jnp.bitwise_xor(scal[0], k) * per

        def body(t, carry):
            out[t] = acc[first + t] * u_out[pl.ds(first + t, 1), :]
            return carry

        lax.fori_loop(0, per, body, 0, unroll=4)
    for t in range(ext - rows):
        tail_out[t] = acc[rows + t] * u_out[rows + t : rows + t + 1, :]
    pad = ext - rows
    lane = lax.broadcasted_iota(jnp.int32, tail_out.shape[1:], 1)
    ends = jnp.zeros(tail_out.shape[1:], F32)
    for t in range(pad):
        ends = jnp.where(lane == t, tile_sum(w_ref, mask, rows - pad + t), ends)
    tail_out[pad] = ends
    write_sums(sums_out, [*scales, u_out], rows)


def write_sums(sums_out, scales, rows):
    sums_out[...] = jnp.zeros_like(sums_out)
    mask = scales[0][:rows]
    totals = [mask]
    for t in range(ITERS):
        below = jnp.where(mask > 0, scales[t + 1][:rows], 1.0)
        totals.append(jnp.where(mask > 0, scales[t][:rows] / below, 0.0))
    for t, total in enumerate(totals):
        line = jnp.sum(jnp.sum(total, axis=0, keepdims=True), axis=1, keepdims=True)
        sums_out[t : t + 1, :] = jnp.broadcast_to(line, (1, mask.shape[1]))


def numer_row_kernel(scal, hi_ref, lo_ref, h_ref, *refs):
    u_ref, outs, terms = refs[0], refs[1:-1], refs[-1]
    ext, tile = u_ref.shape
    factors = h_ref.shape[0]
    offs = offsets(scal, hi_ref.shape[2] // tile)

    def fill(j, carry):
        x = h_ref[:, pl.ds(pl.multiple_of(j * tile, tile), tile)] * u_ref[pl.ds(j, 1), :]
        hi, lo = split(x)
        terms[j, :factors] = hi
        terms[j, factors:] = lo
        return carry

    lax.fori_loop(0, ext, fill, 0, unroll=4)
    row_pieces(scal, offs, terms, hi_ref, lo_ref, u_ref, range(len(outs)), outs)


def numer_col(scal, r_hi, r_lo, row_factors, mask_ext, parts, scales):
    shares = len(parts)
    rows, tile = r_hi.shape[:2]
    factors = row_factors.shape[0]
    ext = mask_ext.shape[0]
    piece = jax.ShapeDtypeStruct((rows // shares, factors, tile), F32)
    outs = [
        jax.ShapeDtypeStruct((ext, tile), F32),
        jax.ShapeDtypeStruct((ext - rows + 1, factors, tile), F32),
        jax.ShapeDtypeStruct((8, tile), F32),
    ]
    res = kernel_call(
        functools.partial(numer_col_kernel, shares),
        "numer_col",
        scal,
        [r_hi, r_lo, row_factors, mask_ext, *parts, *scales],
        outs + [piece] * shares,
        [pltpu.VMEM((ext, factors, tile), F32)],
    )
    return *res[:3], res[3:]


def numer_row(scal, r_hi, r_lo, col_ext, u, shares):
    rows, tile = r_hi.shape[:2]
    factors = col_ext.shape[0]
    piece = jax.ShapeDtypeStruct((rows // shares, factors, tile), F32)
    return kernel_call(
        numer_row_kernel,
        "numer_row",
        scal,
        [r_hi, r_lo, col_ext, u],
        [piece] * shares,
        [pltpu.VMEM((u.shape[0], 2 * factors, tile), BF16)],
    )


def mean_scale(sums):
    scale = sums[1:2, :] / sums[0:1, :]
    for t in range(1, ITERS):
        scale = scale * (sums[t + 1 : t + 2, :] / sums[0:1, :])
    return scale


def tile_sum(factor_ref, mask, j):
    tile = mask.shape[1]
    x = factor_ref[:, pl.ds(pl.multiple_of(j * tile, tile), tile)] * mask[pl.ds(j, 1), :]
    return jnp.sum(x, axis=1, keepdims=True)


def windows(sums, per):
    return [tree_sum(sums[t : t + len(sums) - per]) for t in range(per)]


def write_coefficient(old_ref, mask, first, lowers, times_out, plus_out):
    tile = mask.shape[1]
    for t, lower in enumerate(lowers):
        live = mask[pl.ds(first + t, 1), :]
        old = old_ref[:, t * tile : (t + 1) * tile]
        times_out[t] = jnp.where(live > 0, old / jnp.where(live > 0, lower * live, 1.0), 0.0)
        plus_out[t] = jnp.where(live > 0, 0.0, old)


def row_coefficient_kernel(pad, scal, old_ref, mask, other, times_out, plus_out):
    per = times_out.shape[0]
    first = scal[0] * per
    sums = [tile_sum(other, mask, first + t) for t in range(per + pad)]
    write_coefficient(old_ref, mask, first, windows(sums, per), times_out, plus_out)


def col_coefficient_kernel(pad, scal, old_ref, mask, other, ends, times_out, plus_out):
    per = times_out.shape[0]
    first = scal[0] * per
    sums = []
    for j in range(1, per + pad):
        total = tile_sum(other, mask, jnp.maximum(first - pad + j, 0))
        for start in range(0, pad, per):
            if start + j < pad:
                before = jnp.where(scal[scal.shape[0] - 1] > 0, ends[:, start + j : start + j + 1], 0.0)
                total = jnp.where(first == start, before, total)
        sums.append(total)
    sums.append(jnp.zeros_like(sums[0]))
    write_coefficient(old_ref, mask, first, windows(sums, per), times_out, plus_out)


def coefficient(kernel, scal, shares, old, mask_ext, other, *ends):
    factors = old.shape[0]
    tile = mask_ext.shape[1]
    rows = old.shape[1] // tile
    per = rows // shares
    specs = [pl.BlockSpec((factors, per * tile), lambda i, scal: (0, scal[0]))]
    specs += [vmem() for _ in range(2 + len(ends))]
    return kernel_call(
        functools.partial(kernel, mask_ext.shape[0] - rows),
        "coefficient",
        scal,
        [old, mask_ext, other, *ends],
        [jax.ShapeDtypeStruct((per, factors, tile), F32)] * 2,
        specs=specs,
    )


def update_kernel(scal, sums, times, plus, *refs):
    terms, out = refs[:-1], refs[-1]
    per, _, tile = times.shape
    c = mean_scale(sums[...])
    for t in range(per):
        numer = terms[0][t]
        for term in terms[1:]:
            numer = numer + term[t]
        out[:, t * tile : (t + 1) * tile] = times[t] * (numer * c * c) + plus[t]


def update(scal, sums, times, plus, terms):
    per, count, tile = terms[0].shape
    return kernel_call(
        update_kernel,
        "update",
        scal,
        [sums, times, plus, *terms],
        [jax.ShapeDtypeStruct((count, per * tile), F32)],
    )[0]


def xor_exchange(x, axis, k):
    return lax.ppermute(x, axis, [(i, i ^ k) for i in range(lax.axis_size(axis))])


def both_sides(x, even):
    size = lax.axis_size("genome")
    a = lax.ppermute(x, "genome", [(i, i ^ 1) for i in range(size)])
    b = lax.ppermute(x, "genome", [(i, (((i + 1) ^ 1) - 1) % size) for i in range(size)])
    return jnp.where(even > 0, a, b), jnp.where(even > 0, b, a)


def scatter_terms(pieces, extra=None, across=None):
    size = lax.axis_size("offset")

    def piece(k):
        return pieces[k] if extra is None else put(pieces[k], extra[k])

    def put(x, y):
        return x.at[: y.shape[0]].add(y)

    if size == 4:
        far = pieces[3] + xor_exchange(pieces[2], "offset", 1)
        if extra is not None:
            far = put(far, extra[3] + across)
        moved = xor_exchange(far, "offset", 3)
        return [piece(0), xor_exchange(piece(1), "offset", 1), moved], far
    moved = [xor_exchange(piece(k), "offset", k) for k in range(1, size)]
    return [piece(0), *moved], moved[0]


def per_device(counts, band_offset, bin_mask, row_factors, col_factors):
    rows, slots, tile = counts.shape[:3]
    factors = row_factors.shape[0]
    offset_count = lax.axis_size("offset")
    genome_count = lax.axis_size("genome")
    g = lax.axis_index("genome")
    o = lax.axis_index("offset").astype(jnp.int32)
    reach = slots * offset_count - 1
    pad = reach + 1

    line = jnp.broadcast_to(g, (1, tile))
    even = (line % 2 == 0).astype(F32)
    has_next = (line < genome_count - 1).astype(F32)
    has_prev = (line > 0).astype(F32)
    count = offset_count * -(-pad * offset_count // rows)
    index = lax.broadcasted_iota(jnp.int32, (count, tile), 0)
    share, k = index // offset_count, index % offset_count
    mine = (jnp.bitwise_xor(share, k) == o).astype(F32) * has_prev
    flags = jnp.concatenate([even, has_next, has_prev, mine])
    before = jnp.broadcast_to((g > 0).astype(jnp.int32), (1,))
    scal = jnp.concatenate([jnp.broadcast_to(o, (1,)), band_offset, before])
    flags, scal, bin_mask = lax.optimization_barrier((flags, scal, bin_mask))
    even, has_next, has_prev = flags[0:1], flags[1:2], flags[2:3]
    mine = flags[3:]

    mask = bin_mask.astype(F32).reshape(rows, tile)
    mask_next, _ = both_sides(mask[:pad], even)
    keep = lax.broadcasted_iota(jnp.int32, (pad, 1), 0) < reach
    mask_ext = jnp.concatenate([mask, jnp.where(keep, mask_next * has_next, 0.0)])

    scales = []
    ratios = []
    cut = [0] + [(rows * (3 * t + 3) // (8 * STEP)) * STEP for t in range(ITERS - 1)] + [rows]
    for t in range(ITERS):
        if t == 0:
            u = mask_ext
            counts = pltpu.with_memory_space_constraint(counts, pltpu.HBM)
            edge_v, edge, kept = first_edge(scal, counts, u)
        else:
            edge_v, edge, u = cover_edge(scal, kept, mask_ext, parts, ratios[0])
        scales.append(u)
        after, before = both_sides(edge, even)
        if t == 0:
            v, kept = first_main(scal, counts, u, edge_v, kept)
            col_late, _ = lax.optimization_barrier((col_factors, v))
            ring_left = [(i, (i - 1) % genome_count) for i in range(genome_count)]
            col_next = lax.ppermute(col_late[:, : pad * tile], "genome", ring_left)
            col_next = jnp.where(has_next[:, :1] > 0, col_next, 1.0)
            col_ext = jnp.concatenate([col_factors, col_next], axis=1)
        else:
            v = cover_main(scal, kept, u, edge_v)
        front = v[:pad] + before[pad:] * has_prev
        back = v[rows:] + after[:pad] * has_next
        x = jnp.concatenate([front, v[pad:rows], back])
        parts = [x] + [xor_exchange(x, "offset", k) for k in range(1, offset_count)]
        ratios = ratio(
            scal, kept, row_factors, col_ext, x, ratios, cut[t], cut[t + 1] - cut[t]
        )

    r_hi, r_lo = ratios
    u, tail, sums, h_parts = numer_col(scal, r_hi, r_lo, row_factors, mask_ext, parts, scales)
    w_parts = numer_row(scal, r_hi, r_lo, col_ext, u, offset_count)
    per = rows // offset_count

    right = [(i, (i + 1) % genome_count) for i in range(genome_count)]
    arrived = lax.ppermute(tail, "genome", right)
    if offset_count == 4 and pad <= per:
        diagonal = [
            (i * 4 + j, (i + 1) % genome_count * 4 + (j ^ 1))
            for i in range(genome_count)
            for j in range(4)
        ]
        across = lax.ppermute(tail[:pad], ("genome", "offset"), diagonal)
        extra = [arrived[:pad] * mine[k : k + 1] for k in range(4)]
        h_terms, half_way = scatter_terms(h_parts, extra, across * mine[3:4])
    else:
        h_parts = list(h_parts)
        for s in range(-(-pad // per)):
            piece = arrived[s * per : min(pad, (s + 1) * per)]
            for k in range(offset_count):
                at = s * offset_count + k
                h_parts[k] = h_parts[k].at[: piece.shape[0]].add(piece * mine[at : at + 1])
        h_terms, half_way = scatter_terms(h_parts)
    w_terms, half_way_too = scatter_terms(w_parts)

    sums, _ = lax.optimization_barrier((sums, half_way_too))
    sums = jnp.sum(lax.all_gather(sums, "genome"), axis=0)
    bias = (u[:rows] * mean_scale(sums)).reshape(-1)

    row_terms = coefficient(
        row_coefficient_kernel, scal, offset_count, row_factors, mask_ext, col_ext
    )
    col_terms = coefficient(
        col_coefficient_kernel, scal, offset_count, col_factors, mask_ext, row_factors, arrived[pad]
    )
    col_update = update(scal, sums, *col_terms, h_terms)
    row_update = update(scal, sums, *row_terms, w_terms)
    return bias, row_update, col_update


def solution(mesh):
    return jax.shard_map(
        per_device,
        mesh=mesh,
        in_specs=(
            P("genome", "offset", None, None),
            P("offset"),
            P("genome"),
            P(None, "genome"),
            P(None, "genome"),
        ),
        out_specs=(P("genome"), P(None, ("genome", "offset")), P(None, ("genome", "offset"))),
        check_vma=False,
    )
```

```python
import functools

import jax
import jax.numpy as jnp
from jax import lax
from jax.experimental import pallas as pl
from jax.experimental.pallas import tpu as pltpu
from jax.sharding import PartitionSpec as P

ITERS = 3
STEP = 8
EARLY = 2
F32 = jnp.float32
BF16 = jnp.bfloat16
VMEM_LIMIT = 20 * 1024 * 1024
NT = (((1,), (1,)), ((), ()))
TN = (((0,), (0,)), ((), ()))


def split(x):
    hi = x.astype(BF16)
    lo = (x - hi.astype(F32)).astype(BF16)
    return hi, lo


def tree_sum(parts):
    while len(parts) > 1:
        parts = [a + b for a, b in zip(parts[::2], parts[1::2])]
    return parts[0]


def params():
    return pltpu.CompilerParams(vmem_limit_bytes=VMEM_LIMIT)


def scale_from(mask, parts):
    cover = tree_sum([p[...] for p in parts[:1] + parts[:0:-1]])
    live = mask[...] > 0
    return jnp.where(live, 1.0 / jnp.where(live, cover, 1.0), 0.0)


def vmem():
    return pl.BlockSpec(memory_space=pltpu.VMEM)


def kernel_call(body, name, scalars, args, outs, scratch=(), aliases=None, specs=None):
    return pl.pallas_call(
        body,
        grid_spec=pltpu.PrefetchScalarGridSpec(
            num_scalar_prefetch=1,
            grid=(1,),
            in_specs=specs or [vmem() for _ in args],
            out_specs=[vmem() for _ in outs],
            scratch_shapes=list(scratch),
        ),
        out_shape=outs,
        input_output_aliases=aliases or {},
        compiler_params=params(),
        name=name,
    )(scalars, *args)


def offsets(scal, slots):
    return [scal[1 + s] for s in range(slots)]


def by_diagonal(offs, slots, go):
    for s in range(slots):

        @pl.when(offs[s] == 0)
        def _():
            go(s)

    @pl.when(functools.reduce(jnp.logical_and, [offs[s] != 0 for s in range(slots)]))
    def _():
        go(-1)


def tile_value(counts, i, s, diagonal):
    c = counts[i, s].astype(F32)
    if s == diagonal:
        tile = c.shape[0]
        r = lax.broadcasted_iota(jnp.int32, (tile, tile), 0)
        q = lax.broadcasted_iota(jnp.int32, (tile, tile), 1)
        c = jnp.where(r < q, c, jnp.where(r == q, 0.5 * c, 0.0))
    return c


def cover_block(offs, counts, u_ref, acc, base, diagonal, at, kept=None):
    slots, tile = counts.shape[1:3]
    ones = jnp.ones((8, tile), BF16)
    u_block = u_ref[pl.ds(base, STEP), :]
    u_cols = u_block.T
    u_across = [u_ref[pl.ds(base + offs[s], STEP), :] for s in range(slots)]
    cols = [[] for _ in range(slots)]
    sums = []
    for t in range(STEP):
        total = None
        for s in range(slots):
            c = tile_value(counts, at + t, s, diagonal)
            if kept is not None:
                kept[base + t, s] = c
            term = c * u_across[s][t : t + 1]
            total = term if total is None else total + term
            cols[s].append(jnp.sum(c * u_cols[:, t : t + 1], axis=0, keepdims=True))
        hi, lo = split(total)
        row = lax.dot_general(ones, hi, NT, preferred_element_type=F32)
        row = row + lax.dot_general(ones, lo, NT, preferred_element_type=F32)
        sums.append(row[:1])
    acc[pl.ds(base, STEP), :] += jnp.concatenate(sums, axis=0)
    for s in range(slots):
        acc[pl.ds(base + offs[s], STEP), :] += jnp.concatenate(cols[s], axis=0)


def block_copies(hbm, buffer, sems, bases):
    return [
        pltpu.make_async_copy(
            hbm.at[pl.ds(base, STEP)], buffer.at[pl.ds(k * STEP, STEP)], sems.at[k]
        )
        for k, base in enumerate(bases)
    ]


def edge_bases(rows, pad):
    return list(range(0, pad, STEP)) + list(range(rows - pad, rows, STEP))


def write_edge(v_out, edge_out, rows):
    pad = v_out.shape[0] - rows
    edge_out[:pad] = v_out[:pad]
    edge_out[pad:] = v_out[rows:]


def first_main_kernel(scal, hbm, mask, v_out, kept, buffer, sems):
    rows, slots = hbm.shape[:2]
    offs = offsets(scal, slots)
    pad = v_out.shape[0] - rows
    inner = list(range(pad, rows - pad, STEP))
    bases = inner + edge_bases(rows, pad)
    copies = block_copies(hbm, buffer, sems, bases)
    for copy in copies:
        copy.start()
    v_out[...] = jnp.zeros_like(v_out)

    def go(diagonal):
        for k, base in enumerate(bases):
            copies[k].wait()
            at = k * STEP
            if base in inner:
                cover_block(offs, buffer, mask, v_out, base, diagonal, at, kept)
            else:
                for t in range(STEP):
                    for s in range(slots):
                        kept[base + t, s] = tile_value(buffer, at + t, s, diagonal)

    by_diagonal(offs, slots, go)


def first_edge_kernel(scal, kept, u_ref, inner_v, v_out, edge_out):
    rows, slots = kept.shape[:2]
    offs = offsets(scal, slots)
    v_out[...] = inner_v[...]
    for base in edge_bases(rows, u_ref.shape[0] - rows):
        cover_block(offs, kept, u_ref, v_out, base, -1, base)
    write_edge(v_out, edge_out, rows)


def edge_kernel(scal, kept, mask, *refs):
    v_out, edge_out, u_out = refs[-3:]
    rows, slots = kept.shape[:2]
    offs = offsets(scal, slots)
    u_out[...] = scale_from(mask, refs[:-4])
    v_out[...] = jnp.zeros_like(v_out)
    for base in edge_bases(rows, mask.shape[0] - rows):
        cover_block(offs, kept, u_out, v_out, base, -1, base)
    write_edge(v_out, edge_out, rows)


def main_kernel(scal, kept, u_ref, edge_v, v_out):
    rows, slots = kept.shape[:2]
    offs = offsets(scal, slots)
    pad = edge_v.shape[0] - rows
    v_out[...] = edge_v[...]
    for base in range(pad, rows - pad, STEP):
        cover_block(offs, kept, u_ref, v_out, base, -1, base)


def first_main(scal, counts, mask, ext):
    rows, slots, tile = counts.shape[:3]
    outs = [jax.ShapeDtypeStruct((ext, tile), F32), pltpu.VMEM(counts.shape, F32)]
    return kernel_call(
        first_main_kernel,
        "first_main",
        scal,
        [counts, mask],
        outs,
        [pltpu.VMEM(counts.shape, counts.dtype), pltpu.SemaphoreType.DMA((rows // STEP,))],
        specs=[pl.BlockSpec(memory_space=pltpu.HBM), vmem()],
    )


def first_edge(scal, kept, u, inner_v):
    rows, tile = kept.shape[0], kept.shape[2]
    flat = jax.ShapeDtypeStruct(u.shape, F32)
    edge = jax.ShapeDtypeStruct((2 * (u.shape[0] - rows), tile), F32)
    return kernel_call(first_edge_kernel, "first_edge", scal, [kept, u, inner_v], [flat, edge])


def cover_edge(scal, kept, mask_ext, parts, after):
    rows, tile = kept.shape[0], kept.shape[2]
    flat = jax.ShapeDtypeStruct(mask_ext.shape, F32)
    edge = jax.ShapeDtypeStruct((2 * (mask_ext.shape[0] - rows), tile), F32)
    args = [kept, mask_ext, *parts, after]
    return kernel_call(edge_kernel, "cover_edge", scal, args, [flat, edge, flat])


def cover_main(scal, kept, u, edge_v):
    outs = [jax.ShapeDtypeStruct(u.shape, F32)]
    return kernel_call(main_kernel, "cover_main", scal, [kept, u, edge_v], outs)[0]


def ratio_kernel(start, count, pad, scal, kept, w_ref, h_ref, after, *refs):
    slots, tile = kept.shape[1:3]
    offs = offsets(scal, slots)
    if start == 0:
        hi_out, lo_out, same, h_terms = refs
        same[...] = after[...]
    else:
        hi_out, lo_out, h_terms = refs[-3:]

    def prepare(j, carry):
        hi, lo = split(h_ref[:, pl.ds(pl.multiple_of(j * tile, tile), tile)])
        h_terms[j - start] = jnp.concatenate([hi, lo, hi, lo], axis=0)
        return carry

    lax.fori_loop(start, start + count + pad, prepare, 0, unroll=4)

    def go(diagonal):
        def body(i, carry):
            hi, lo = split(w_ref[:, pl.ds(pl.multiple_of(i * tile, tile), tile)])
            w_terms = jnp.concatenate([hi, hi, lo, lo], axis=0)
            for s in range(slots):
                model = lax.dot_general(
                    w_terms, h_terms[i - start + offs[s]], TN, preferred_element_type=F32
                )
                values = kept[i, s]
                if s == diagonal:
                    values = values + values.T
                r_hi, r_lo = split(values * (1.0 / model))
                hi_out[i, :, s * tile : (s + 1) * tile] = r_hi
                lo_out[i, :, s * tile : (s + 1) * tile] = r_lo
            return carry

        lax.fori_loop(start, start + count, body, 0, unroll=4)

    by_diagonal(offs, slots, go)


def ratio(scal, kept, row_factors, col_ext, after, earlier, start, count):
    rows, slots, tile = kept.shape[:3]
    factors = row_factors.shape[0]
    pad = after.shape[0] - rows
    out = pltpu.VMEM((rows, tile, slots * tile), BF16)
    return kernel_call(
        functools.partial(ratio_kernel, start, count, pad),
        "ratio",
        scal,
        [kept, row_factors, col_ext, after, *earlier],
        [out, out] + [jax.ShapeDtypeStruct(after.shape, F32)] * (start == 0),
        [pltpu.VMEM((count + pad, 4 * factors, tile), BF16)],
        {5: 0, 6: 1} if earlier else {},
    )


def row_numer(offs, g_all, hi_ref, lo_ref, u_ref, i):
    slots = hi_ref.shape[2] // g_all.shape[2]
    factors = g_all.shape[1] // 2
    g = jnp.concatenate([g_all[i + offs[s]] for s in range(slots)], axis=1)
    big = lax.dot_general(g, hi_ref[i], NT, preferred_element_type=F32)
    small = lax.dot_general(g[:factors], lo_ref[i], NT, preferred_element_type=F32)
    return (big[:factors] + big[factors:] + small) * u_ref[pl.ds(i, 1), :]


def col_numer(w_ref, hi_ref, lo_ref, u_ref, i):
    tile = u_ref.shape[1]
    factors = w_ref.shape[0]
    w = w_ref[:, pl.ds(pl.multiple_of(i * tile, tile), tile)]
    hi, lo = split(w * u_ref[pl.ds(i, 1), :])
    big = jnp.dot(jnp.concatenate([hi, lo], axis=0), hi_ref[i], preferred_element_type=F32)
    small = jnp.dot(hi, lo_ref[i], preferred_element_type=F32)
    return big[:factors] + big[factors:] + small


def col_loop(offs, w_ref, hi_ref, lo_ref, u_ref, acc, start, count, shift):
    tile = u_ref.shape[1]

    def body(n, carry):
        i = start + n
        cols = col_numer(w_ref, hi_ref, lo_ref, u_ref, i)
        for s in range(hi_ref.shape[2] // tile):
            acc[i + offs[s] - shift] += cols[:, s * tile : (s + 1) * tile]
        return carry

    lax.fori_loop(0, count, body, 0, unroll=4)


def row_pieces(scal, offs, g_ref, hi_ref, lo_ref, u_ref, order, outs):
    for k, out in zip(order, outs):
        per = out.shape[0]
        first = jnp.bitwise_xor(scal[0], k) * per

        def body(t, carry):
            out[t] = row_numer(offs, g_ref, hi_ref, lo_ref, u_ref, first + t)
            return carry

        lax.fori_loop(0, per, body, 0, unroll=4)


def scaled_terms(h_ref, u_ref, terms, start, count):
    tile = u_ref.shape[1]
    factors = h_ref.shape[0]

    def fill(n, carry):
        j = start + n
        x = h_ref[:, pl.ds(pl.multiple_of(j * tile, tile), tile)] * u_ref[pl.ds(j, 1), :]
        hi, lo = split(x)
        terms[j, :factors] = hi
        terms[j, factors:] = lo
        return carry

    lax.fori_loop(0, count, fill, 0, unroll=4)


def numer_first_kernel(k, shares, scal, hi_ref, lo_ref, w_ref, mask, *refs):
    parts, scales = refs[:shares], refs[shares : shares + ITERS]
    u_out, tail_out, sums_out, out, acc = refs[shares + ITERS :]
    rows = hi_ref.shape[0]
    ext, tile = mask.shape
    offs = offsets(scal, hi_ref.shape[2] // tile)
    per = rows // shares
    pad = ext - rows
    u_out[...] = scale_from(mask, parts)

    acc[...] = jnp.zeros_like(acc)
    col_loop(offs, w_ref, hi_ref, lo_ref, u_out, acc, rows - pad, pad, rows - pad)
    for t in range(pad):
        tail_out[t] = acc[pad + t] * u_out[rows + t : rows + t + 1, :]
    lane = lax.broadcasted_iota(jnp.int32, tail_out.shape[1:], 1)
    ends = jnp.zeros(tail_out.shape[1:], F32)
    for t in range(pad):
        ends = jnp.where(lane == t, tile_sum(w_ref, mask, rows - pad + t), ends)
    tail_out[pad] = ends

    first = jnp.bitwise_xor(scal[0], k) * per
    acc[...] = jnp.zeros_like(acc)
    block = min(per, pad)
    col_loop(offs, w_ref, hi_ref, lo_ref, u_out, acc, first, per, first - pad)
    for q in range(1, pad // block + 1):

        @pl.when(first >= q * block)
        def _():
            start = first - q * block
            col_loop(offs, w_ref, hi_ref, lo_ref, u_out, acc, start, block, first - pad)

    for t in range(per):
        out[t] = acc[pad + t] * u_out[pl.ds(first + t, 1), :]
    write_sums(sums_out, [*scales, u_out], rows)


def numer_col_kernel(order, scal, hi_ref, lo_ref, w_ref, u_ref, after, *refs):
    outs, acc = refs[:-1], refs[-1]
    rows = hi_ref.shape[0]
    tile = u_ref.shape[1]
    offs = offsets(scal, hi_ref.shape[2] // tile)
    per = outs[0].shape[0]
    acc[...] = jnp.zeros_like(acc)
    col_loop(offs, w_ref, hi_ref, lo_ref, u_ref, acc, 0, rows, 0)
    for k, out in zip(order, outs):
        first = jnp.bitwise_xor(scal[0], k) * per

        def body(t, carry):
            out[t] = acc[first + t] * u_ref[pl.ds(first + t, 1), :]
            return carry

        lax.fori_loop(0, per, body, 0, unroll=4)


def write_sums(sums_out, scales, rows):
    sums_out[...] = jnp.zeros_like(sums_out)
    mask = scales[0][:rows]
    totals = [mask]
    for t in range(ITERS):
        below = jnp.where(mask > 0, scales[t + 1][:rows], 1.0)
        totals.append(jnp.where(mask > 0, scales[t][:rows] / below, 0.0))
    for t, total in enumerate(totals):
        line = jnp.sum(jnp.sum(total, axis=0, keepdims=True), axis=1, keepdims=True)
        sums_out[t : t + 1, :] = jnp.broadcast_to(line, (1, mask.shape[1]))


def numer_row_kernel(scal, hi_ref, lo_ref, h_ref, u_ref, *refs):
    outs, terms = refs[:-1], refs[-1]
    ext, tile = u_ref.shape
    offs = offsets(scal, hi_ref.shape[2] // tile)
    scaled_terms(h_ref, u_ref, terms, 0, ext)
    row_pieces(scal, offs, terms, hi_ref, lo_ref, u_ref, range(len(outs)), outs)


def numer_first(scal, r_hi, r_lo, row_factors, mask_ext, parts, scales, k):
    shares = len(parts)
    rows, tile = r_hi.shape[:2]
    factors = row_factors.shape[0]
    ext = mask_ext.shape[0]
    pad = ext - rows
    per = rows // shares
    return kernel_call(
        functools.partial(numer_first_kernel, k, shares),
        "numer_first",
        scal,
        [r_hi, r_lo, row_factors, mask_ext, *parts, *scales],
        [
            jax.ShapeDtypeStruct((ext, tile), F32),
            jax.ShapeDtypeStruct((pad + 1, factors, tile), F32),
            jax.ShapeDtypeStruct((8, tile), F32),
            jax.ShapeDtypeStruct((per, factors, tile), F32),
        ],
        [pltpu.VMEM((per + 2 * pad, factors, tile), F32)],
    )


def numer_col(scal, r_hi, r_lo, row_factors, u, after, order, shares):
    rows, tile = r_hi.shape[:2]
    factors = row_factors.shape[0]
    piece = jax.ShapeDtypeStruct((rows // shares, factors, tile), F32)
    return kernel_call(
        functools.partial(numer_col_kernel, order),
        "numer_col",
        scal,
        [r_hi, r_lo, row_factors, u, after],
        [piece] * len(order),
        [pltpu.VMEM((u.shape[0], factors, tile), F32)],
    )


def numer_row(scal, r_hi, r_lo, col_ext, u, shares):
    rows, tile = r_hi.shape[:2]
    factors = col_ext.shape[0]
    piece = jax.ShapeDtypeStruct((rows // shares, factors, tile), F32)
    return kernel_call(
        numer_row_kernel,
        "numer_row",
        scal,
        [r_hi, r_lo, col_ext, u],
        [piece] * shares,
        [pltpu.VMEM((u.shape[0], 2 * factors, tile), BF16)],
    )


def mean_scale(sums):
    scale = sums[1:2, :] / sums[0:1, :]
    for t in range(1, ITERS):
        scale = scale * (sums[t + 1 : t + 2, :] / sums[0:1, :])
    return scale


def tile_sum(factor_ref, mask, j):
    tile = mask.shape[1]
    x = factor_ref[:, pl.ds(pl.multiple_of(j * tile, tile), tile)] * mask[pl.ds(j, 1), :]
    return jnp.sum(x, axis=1, keepdims=True)


def windows(sums, per):
    return [tree_sum(sums[t : t + len(sums) - per]) for t in range(per)]


def write_coefficient(old_ref, mask, first, lowers, times_out, plus_out):
    tile = mask.shape[1]
    for t, lower in enumerate(lowers):
        live = mask[pl.ds(first + t, 1), :]
        old = old_ref[:, t * tile : (t + 1) * tile]
        times_out[t] = jnp.where(live > 0, old / jnp.where(live > 0, lower * live, 1.0), 0.0)
        plus_out[t] = jnp.where(live > 0, 0.0, old)


def row_coefficient_kernel(pad, scal, old_ref, mask, other, times_out, plus_out):
    per = times_out.shape[0]
    first = scal[0] * per
    sums = [tile_sum(other, mask, first + t) for t in range(per + pad)]
    write_coefficient(old_ref, mask, first, windows(sums, per), times_out, plus_out)


def col_coefficient_kernel(pad, scal, old_ref, mask, other, ends, times_out, plus_out):
    per = times_out.shape[0]
    first = scal[0] * per
    sums = []
    for j in range(1, per + pad):
        total = tile_sum(other, mask, jnp.maximum(first - pad + j, 0))
        for start in range(0, pad, per):
            if start + j < pad:
                before = jnp.where(scal[scal.shape[0] - 1] > 0, ends[:, start + j : start + j + 1], 0.0)
                total = jnp.where(first == start, before, total)
        sums.append(total)
    sums.append(jnp.zeros_like(sums[0]))
    write_coefficient(old_ref, mask, first, windows(sums, per), times_out, plus_out)


def coefficient(kernel, scal, shares, old, mask_ext, other, *ends):
    factors = old.shape[0]
    tile = mask_ext.shape[1]
    rows = old.shape[1] // tile
    per = rows // shares
    specs = [pl.BlockSpec((factors, per * tile), lambda i, scal: (0, scal[0]))]
    specs += [vmem() for _ in range(2 + len(ends))]
    return kernel_call(
        functools.partial(kernel, mask_ext.shape[0] - rows),
        "coefficient",
        scal,
        [old, mask_ext, other, *ends],
        [jax.ShapeDtypeStruct((per, factors, tile), F32)] * 2,
        specs=specs,
    )


def update_kernel(scal, sums, times, plus, *refs):
    terms, out = refs[:-1], refs[-1]
    per, _, tile = times.shape
    c = mean_scale(sums[...])
    for t in range(per):
        numer = terms[0][t]
        for term in terms[1:]:
            numer = numer + term[t]
        out[:, t * tile : (t + 1) * tile] = times[t] * (numer * c * c) + plus[t]


def update(scal, sums, times, plus, terms):
    per, count, tile = terms[0].shape
    return kernel_call(
        update_kernel,
        "update",
        scal,
        [sums, times, plus, *terms],
        [jax.ShapeDtypeStruct((count, per * tile), F32)],
    )[0]


def xor_exchange(x, axis, k):
    return lax.ppermute(x, axis, [(i, i ^ k) for i in range(lax.axis_size(axis))])


def both_sides(x, even):
    size = lax.axis_size("genome")
    a = lax.ppermute(x, "genome", [(i, i ^ 1) for i in range(size)])
    b = lax.ppermute(x, "genome", [(i, (((i + 1) ^ 1) - 1) % size) for i in range(size)])
    return jnp.where(even > 0, a, b), jnp.where(even > 0, b, a)


def scatter_terms(pieces, extra=None, across=None):
    size = lax.axis_size("offset")

    def piece(k):
        return pieces[k] if extra is None else put(pieces[k], extra[k])

    def put(x, y):
        return x.at[: y.shape[0]].add(y)

    if size == 4:
        far = pieces[3] + xor_exchange(pieces[2], "offset", 1)
        if extra is not None:
            far = put(far, extra[3] + across)
        moved = xor_exchange(far, "offset", 3)
        return [piece(0), xor_exchange(piece(1), "offset", 1), moved], far
    moved = [xor_exchange(piece(k), "offset", k) for k in range(1, size)]
    return [piece(0), *moved], moved[0]


def per_device(counts, band_offset, bin_mask, row_factors, col_factors):
    rows, slots, tile = counts.shape[:3]
    factors = row_factors.shape[0]
    offset_count = lax.axis_size("offset")
    genome_count = lax.axis_size("genome")
    g = lax.axis_index("genome")
    o = lax.axis_index("offset").astype(jnp.int32)
    reach = slots * offset_count - 1
    pad = reach + 1

    line = jnp.broadcast_to(g, (1, tile))
    even = (line % 2 == 0).astype(F32)
    has_next = (line < genome_count - 1).astype(F32)
    has_prev = (line > 0).astype(F32)
    count = offset_count * -(-pad * offset_count // rows)
    index = lax.broadcasted_iota(jnp.int32, (count, tile), 0)
    share, k = index // offset_count, index % offset_count
    mine = (jnp.bitwise_xor(share, k) == o).astype(F32) * has_prev
    flags = jnp.concatenate([even, has_next, has_prev, mine])
    before = jnp.broadcast_to((g > 0).astype(jnp.int32), (1,))
    scal = jnp.concatenate([jnp.broadcast_to(o, (1,)), band_offset, before])
    flags, scal, bin_mask = lax.optimization_barrier((flags, scal, bin_mask))
    even, has_next, has_prev = flags[0:1], flags[1:2], flags[2:3]
    mine = flags[3:]

    mask = bin_mask.astype(F32).reshape(rows, tile)
    mask_next, _ = both_sides(mask[:pad], even)
    keep = lax.broadcasted_iota(jnp.int32, (pad, 1), 0) < reach
    mask_ext = jnp.concatenate([mask, jnp.where(keep, mask_next * has_next, 0.0)])

    counts = pltpu.with_memory_space_constraint(counts, pltpu.HBM)
    inner_v, kept = first_main(scal, counts, mask, rows + pad)
    col_late, _ = lax.optimization_barrier((col_factors, inner_v))
    ring_left = [(i, (i - 1) % genome_count) for i in range(genome_count)]
    col_next = lax.ppermute(col_late[:, : pad * tile], "genome", ring_left)
    col_next = jnp.where(has_next[:, :1] > 0, col_next, 1.0)
    col_ext = jnp.concatenate([col_factors, col_next], axis=1)

    scales = []
    quarter = rows // (ITERS + 1)
    for t in range(ITERS):
        if t == 0:
            u = mask_ext
            v, edge = first_edge(scal, kept, u, inner_v)
        else:
            v, edge, u = cover_edge(scal, kept, mask_ext, parts, ratios[0])
        scales.append(u)
        after, before = both_sides(edge, even)
        if t > 0:
            v = cover_main(scal, kept, u, v)
        else:
            *ratios, v = ratio(scal, kept, row_factors, col_factors, v, [], 0, quarter)
        front = v[:pad] + before[pad:] * has_prev
        back = v[rows:] + after[:pad] * has_next
        x = jnp.concatenate([front, v[pad:rows], back])
        others = {k: xor_exchange(x, "offset", k) for k in reversed(range(1, offset_count))}
        parts = [x, *others.values()]
        start = (t + 1) * quarter
        ratios = ratio(scal, kept, row_factors, col_ext, x, ratios, start, quarter)

    r_hi, r_lo = ratios
    u, tail, sums, early = numer_first(
        scal, r_hi, r_lo, row_factors, mask_ext, parts, scales, EARLY
    )
    w_parts = numer_row(scal, r_hi, r_lo, col_ext, u, offset_count)
    right = [(i, (i + 1) % genome_count) for i in range(genome_count)]
    arrived = lax.ppermute(tail, "genome", right)
    row_terms = coefficient(
        row_coefficient_kernel, scal, offset_count, row_factors, mask_ext, col_ext
    )
    col_terms = coefficient(
        col_coefficient_kernel, scal, offset_count, col_factors, mask_ext, row_factors, arrived[pad]
    )
    order = [k for k in (3, 1, 0, *range(4, offset_count))]
    rest = numer_col(scal, r_hi, r_lo, row_factors, u, col_terms[0], order, offset_count)
    h_parts = dict(zip(order, rest)) | {EARLY: early}
    h_parts = [h_parts[k] for k in range(offset_count)]
    per = rows // offset_count

    if offset_count == 4 and pad <= per:
        diagonal = [
            (i * 4 + j, (i + 1) % genome_count * 4 + (j ^ 1))
            for i in range(genome_count)
            for j in range(4)
        ]
        across = lax.ppermute(tail[:pad], ("genome", "offset"), diagonal)
        extra = [arrived[:pad] * mine[k : k + 1] for k in range(4)]
        h_terms, half_way = scatter_terms(h_parts, extra, across * mine[3:4])
    else:
        h_parts = list(h_parts)
        for s in range(-(-pad // per)):
            piece = arrived[s * per : min(pad, (s + 1) * per)]
            for k in range(offset_count):
                at = s * offset_count + k
                h_parts[k] = h_parts[k].at[: piece.shape[0]].add(piece * mine[at : at + 1])
        h_terms, half_way = scatter_terms(h_parts)
    w_terms, half_way_too = scatter_terms(w_parts)

    sums, _ = lax.optimization_barrier((sums, half_way_too))
    sums = jnp.sum(lax.all_gather(sums, "genome"), axis=0)
    bias = (u[:rows] * mean_scale(sums)).reshape(-1)

    col_update = update(scal, sums, *col_terms, h_terms)
    row_update = update(scal, sums, *row_terms, w_terms)
    return bias, row_update, col_update


def solution(mesh):
    return jax.shard_map(
        per_device,
        mesh=mesh,
        in_specs=(
            P("genome", "offset", None, None),
            P("offset"),
            P("genome"),
            P(None, "genome"),
            P(None, "genome"),
        ),
        out_specs=(P("genome"), P(None, ("genome", "offset")), P(None, ("genome", "offset"))),
        check_vma=False,
    )
```

```python
import functools

import jax
import jax.numpy as jnp
from jax import lax
from jax.experimental import pallas as pl
from jax.experimental.pallas import tpu as pltpu
from jax.sharding import PartitionSpec as P

ITERS = 3
STEP = 8
EARLY = 2
F32 = jnp.float32
BF16 = jnp.bfloat16
VMEM_LIMIT = 20 * 1024 * 1024
NT = (((1,), (1,)), ((), ()))
TN = (((0,), (0,)), ((), ()))


def split(x):
    hi = x.astype(BF16)
    lo = (x - hi.astype(F32)).astype(BF16)
    return hi, lo


def tree_sum(parts):
    while len(parts) > 1:
        parts = [a + b for a, b in zip(parts[::2], parts[1::2])]
    return parts[0]


def params():
    return pltpu.CompilerParams(vmem_limit_bytes=VMEM_LIMIT)


def scale_from(mask, parts):
    cover = tree_sum([p[...] for p in parts[:1] + parts[:0:-1]])
    live = mask[...] > 0
    return jnp.where(live, 1.0 / jnp.where(live, cover, 1.0), 0.0)


def vmem():
    return pl.BlockSpec(memory_space=pltpu.VMEM)


def kernel_call(body, name, scalars, args, outs, scratch=(), aliases=None, specs=None):
    return pl.pallas_call(
        body,
        grid_spec=pltpu.PrefetchScalarGridSpec(
            num_scalar_prefetch=1,
            grid=(1,),
            in_specs=specs or [vmem() for _ in args],
            out_specs=[vmem() for _ in outs],
            scratch_shapes=list(scratch),
        ),
        out_shape=outs,
        input_output_aliases=aliases or {},
        compiler_params=params(),
        name=name,
    )(scalars, *args)


def offsets(scal, slots):
    return [scal[1 + s] for s in range(slots)]


def by_diagonal(offs, slots, go):
    for s in range(slots):

        @pl.when(offs[s] == 0)
        def _():
            go(s)

    @pl.when(functools.reduce(jnp.logical_and, [offs[s] != 0 for s in range(slots)]))
    def _():
        go(-1)


def tile_value(counts, i, s, diagonal):
    c = counts[i, s].astype(F32)
    if s == diagonal:
        tile = c.shape[0]
        r = lax.broadcasted_iota(jnp.int32, (tile, tile), 0)
        q = lax.broadcasted_iota(jnp.int32, (tile, tile), 1)
        c = jnp.where(r < q, c, jnp.where(r == q, 0.5 * c, 0.0))
    return c


def cover_block(offs, counts, u_ref, acc, base, diagonal, at, kept=None):
    slots, tile = counts.shape[1:3]
    ones = jnp.ones((8, tile), BF16)
    u_block = u_ref[pl.ds(base, STEP), :]
    u_cols = u_block.T
    u_across = [u_ref[pl.ds(base + offs[s], STEP), :] for s in range(slots)]
    cols = [[] for _ in range(slots)]
    sums = []
    for t in range(STEP):
        total = None
        for s in range(slots):
            c = tile_value(counts, at + t, s, diagonal)
            if kept is not None:
                kept[base + t, s] = c
            term = c * u_across[s][t : t + 1]
            total = term if total is None else total + term
            cols[s].append(jnp.sum(c * u_cols[:, t : t + 1], axis=0, keepdims=True))
        hi, lo = split(total)
        row = lax.dot_general(ones, hi, NT, preferred_element_type=F32)
        row = row + lax.dot_general(ones, lo, NT, preferred_element_type=F32)
        sums.append(row[:1])
    acc[pl.ds(base, STEP), :] += jnp.concatenate(sums, axis=0)
    for s in range(slots):
        acc[pl.ds(base + offs[s], STEP), :] += jnp.concatenate(cols[s], axis=0)


def block_copies(hbm, buffer, sems, bases):
    return [
        pltpu.make_async_copy(
            hbm.at[pl.ds(base, STEP)], buffer.at[pl.ds(k * STEP, STEP)], sems.at[k]
        )
        for k, base in enumerate(bases)
    ]


def edge_bases(rows, pad):
    return list(range(0, pad, STEP)) + list(range(rows - pad, rows, STEP))


def write_edge(v_out, edge_out, rows):
    pad = v_out.shape[0] - rows
    edge_out[:pad] = v_out[:pad]
    edge_out[pad:] = v_out[rows:]


def first_main_kernel(scal, hbm, mask, v_out, kept, buffer, sems):
    rows, slots = hbm.shape[:2]
    offs = offsets(scal, slots)
    pad = v_out.shape[0] - rows
    inner = list(range(pad, rows - pad, STEP))
    bases = inner + edge_bases(rows, pad)
    copies = block_copies(hbm, buffer, sems, bases)
    for copy in copies:
        copy.start()
    v_out[...] = jnp.zeros_like(v_out)

    def go(diagonal):
        for k, base in enumerate(bases):
            copies[k].wait()
            at = k * STEP
            if base in inner:
                cover_block(offs, buffer, mask, v_out, base, diagonal, at, kept)
            else:
                for t in range(STEP):
                    for s in range(slots):
                        kept[base + t, s] = tile_value(buffer, at + t, s, diagonal)

    by_diagonal(offs, slots, go)


def first_edge_kernel(scal, kept, u_ref, inner_v, v_out, edge_out):
    rows, slots = kept.shape[:2]
    offs = offsets(scal, slots)
    v_out[...] = inner_v[...]
    for base in edge_bases(rows, u_ref.shape[0] - rows):
        cover_block(offs, kept, u_ref, v_out, base, -1, base)
    write_edge(v_out, edge_out, rows)


def edge_kernel(scal, kept, mask, *refs):
    v_out, edge_out, u_out = refs[-3:]
    rows, slots = kept.shape[:2]
    offs = offsets(scal, slots)
    u_out[...] = scale_from(mask, refs[:-4])
    v_out[...] = jnp.zeros_like(v_out)
    for base in edge_bases(rows, mask.shape[0] - rows):
        cover_block(offs, kept, u_out, v_out, base, -1, base)
    write_edge(v_out, edge_out, rows)


def main_kernel(scal, kept, u_ref, edge_v, v_out):
    rows, slots = kept.shape[:2]
    offs = offsets(scal, slots)
    pad = edge_v.shape[0] - rows
    v_out[...] = edge_v[...]
    for base in range(pad, rows - pad, STEP):
        cover_block(offs, kept, u_ref, v_out, base, -1, base)


def first_main(scal, counts, mask, ext):
    rows, slots, tile = counts.shape[:3]
    outs = [jax.ShapeDtypeStruct((ext, tile), F32), pltpu.VMEM(counts.shape, F32)]
    return kernel_call(
        first_main_kernel,
        "first_main",
        scal,
        [counts, mask],
        outs,
        [pltpu.VMEM(counts.shape, counts.dtype), pltpu.SemaphoreType.DMA((rows // STEP,))],
        specs=[pl.BlockSpec(memory_space=pltpu.HBM), vmem()],
    )


def first_edge(scal, kept, u, inner_v):
    rows, tile = kept.shape[0], kept.shape[2]
    flat = jax.ShapeDtypeStruct(u.shape, F32)
    edge = jax.ShapeDtypeStruct((2 * (u.shape[0] - rows), tile), F32)
    return kernel_call(first_edge_kernel, "first_edge", scal, [kept, u, inner_v], [flat, edge])


def cover_edge(scal, kept, mask_ext, parts, after):
    rows, tile = kept.shape[0], kept.shape[2]
    flat = jax.ShapeDtypeStruct(mask_ext.shape, F32)
    edge = jax.ShapeDtypeStruct((2 * (mask_ext.shape[0] - rows), tile), F32)
    args = [kept, mask_ext, *parts, after]
    return kernel_call(edge_kernel, "cover_edge", scal, args, [flat, edge, flat])


def cover_main(scal, kept, u, edge_v):
    outs = [jax.ShapeDtypeStruct(u.shape, F32)]
    return kernel_call(main_kernel, "cover_main", scal, [kept, u, edge_v], outs)[0]


def ratio_kernel(start, count, pad, scal, kept, w_ref, h_ref, after, *refs):
    slots, tile = kept.shape[1:3]
    offs = offsets(scal, slots)
    if start == 0:
        hi_out, lo_out, same, h_terms = refs
        same[...] = after[...]
    else:
        hi_out, lo_out, h_terms = refs[-3:]

    def prepare(j, carry):
        hi, lo = split(h_ref[:, pl.ds(pl.multiple_of(j * tile, tile), tile)])
        h_terms[j - start] = jnp.concatenate([hi, lo, hi, lo], axis=0)
        return carry

    lax.fori_loop(start, start + count + pad, prepare, 0, unroll=4)

    def go(diagonal):
        def body(i, carry):
            hi, lo = split(w_ref[:, pl.ds(pl.multiple_of(i * tile, tile), tile)])
            w_terms = jnp.concatenate([hi, hi, lo, lo], axis=0)
            for s in range(slots):
                model = lax.dot_general(
                    w_terms, h_terms[i - start + offs[s]], TN, preferred_element_type=F32
                )
                values = kept[i, s]
                if s == diagonal:
                    values = values + values.T
                r_hi, r_lo = split(values * (1.0 / model))
                hi_out[i, :, s * tile : (s + 1) * tile] = r_hi
                lo_out[i, :, s * tile : (s + 1) * tile] = r_lo
            return carry

        lax.fori_loop(start, start + count, body, 0, unroll=4)

    by_diagonal(offs, slots, go)


def ratio(scal, kept, row_factors, col_ext, after, earlier, start, count):
    rows, slots, tile = kept.shape[:3]
    factors = row_factors.shape[0]
    pad = after.shape[0] - rows
    out = pltpu.VMEM((rows, tile, slots * tile), BF16)
    return kernel_call(
        functools.partial(ratio_kernel, start, count, pad),
        "ratio",
        scal,
        [kept, row_factors, col_ext, after, *earlier],
        [out, out] + [jax.ShapeDtypeStruct(after.shape, F32)] * (start == 0),
        [pltpu.VMEM((count + pad, 4 * factors, tile), BF16)],
        {5: 0, 6: 1} if earlier else {},
    )


def row_numer(offs, g_all, hi_ref, lo_ref, u_ref, i):
    slots = hi_ref.shape[2] // g_all.shape[2]
    factors = g_all.shape[1] // 2
    g = jnp.concatenate([g_all[i + offs[s]] for s in range(slots)], axis=1)
    big = lax.dot_general(g, hi_ref[i], NT, preferred_element_type=F32)
    small = lax.dot_general(g[:factors], lo_ref[i], NT, preferred_element_type=F32)
    return (big[:factors] + big[factors:] + small) * u_ref[pl.ds(i, 1), :]


def col_numer(w_ref, hi_ref, lo_ref, u_ref, i):
    tile = u_ref.shape[1]
    factors = w_ref.shape[0]
    w = w_ref[:, pl.ds(pl.multiple_of(i * tile, tile), tile)]
    hi, lo = split(w * u_ref[pl.ds(i, 1), :])
    big = jnp.dot(jnp.concatenate([hi, lo], axis=0), hi_ref[i], preferred_element_type=F32)
    small = jnp.dot(hi, lo_ref[i], preferred_element_type=F32)
    return big[:factors] + big[factors:] + small


def col_loop(offs, w_ref, hi_ref, lo_ref, u_ref, acc, start, count, shift):
    tile = u_ref.shape[1]

    def body(n, carry):
        i = start + n
        cols = col_numer(w_ref, hi_ref, lo_ref, u_ref, i)
        for s in range(hi_ref.shape[2] // tile):
            acc[i + offs[s] - shift] += cols[:, s * tile : (s + 1) * tile]
        return carry

    lax.fori_loop(0, count, body, 0, unroll=4)


def row_pieces(scal, offs, g_ref, hi_ref, lo_ref, u_ref, order, outs):
    for k, out in zip(order, outs):
        per = out.shape[0]
        first = jnp.bitwise_xor(scal[0], k) * per

        def body(t, carry):
            out[t] = row_numer(offs, g_ref, hi_ref, lo_ref, u_ref, first + t)
            return carry

        lax.fori_loop(0, per, body, 0, unroll=4)


def scaled_terms(h_ref, u_ref, terms, start, count):
    tile = u_ref.shape[1]
    factors = h_ref.shape[0]

    def fill(n, carry):
        j = start + n
        x = h_ref[:, pl.ds(pl.multiple_of(j * tile, tile), tile)] * u_ref[pl.ds(j, 1), :]
        hi, lo = split(x)
        terms[j, :factors] = hi
        terms[j, factors:] = lo
        return carry

    lax.fori_loop(0, count, fill, 0, unroll=4)


def numer_first_kernel(k, shares, scal, hi_ref, lo_ref, w_ref, mask, *refs):
    parts, scales = refs[:shares], refs[shares : shares + ITERS]
    u_out, tail_out, sums_out, out, acc = refs[shares + ITERS :]
    rows = hi_ref.shape[0]
    ext, tile = mask.shape
    offs = offsets(scal, hi_ref.shape[2] // tile)
    per = rows // shares
    pad = ext - rows
    u_out[...] = scale_from(mask, parts)

    acc[...] = jnp.zeros_like(acc)
    col_loop(offs, w_ref, hi_ref, lo_ref, u_out, acc, rows - pad, pad, rows - pad)
    for t in range(pad):
        tail_out[t] = acc[pad + t] * u_out[rows + t : rows + t + 1, :]
    lane = lax.broadcasted_iota(jnp.int32, tail_out.shape[1:], 1)
    ends = jnp.zeros(tail_out.shape[1:], F32)
    for t in range(pad):
        ends = jnp.where(lane == t, tile_sum(w_ref, mask, rows - pad + t), ends)
    tail_out[pad] = ends

    first = jnp.bitwise_xor(scal[0], k) * per
    acc[...] = jnp.zeros_like(acc)
    block = min(per, pad)
    col_loop(offs, w_ref, hi_ref, lo_ref, u_out, acc, first, per, first - pad)
    for q in range(1, pad // block + 1):

        @pl.when(first >= q * block)
        def _():
            start = first - q * block
            col_loop(offs, w_ref, hi_ref, lo_ref, u_out, acc, start, block, first - pad)

    for t in range(per):
        out[t] = acc[pad + t] * u_out[pl.ds(first + t, 1), :]
    write_sums(sums_out, [*scales, u_out], rows)


def numer_col_kernel(order, scal, hi_ref, lo_ref, w_ref, u_ref, after, *refs):
    outs, acc = refs[:-1], refs[-1]
    rows = hi_ref.shape[0]
    tile = u_ref.shape[1]
    offs = offsets(scal, hi_ref.shape[2] // tile)
    per = outs[0].shape[0]
    acc[...] = jnp.zeros_like(acc)
    col_loop(offs, w_ref, hi_ref, lo_ref, u_ref, acc, 0, rows, 0)
    for k, out in zip(order, outs):
        first = jnp.bitwise_xor(scal[0], k) * per

        def body(t, carry):
            out[t] = acc[first + t] * u_ref[pl.ds(first + t, 1), :]
            return carry

        lax.fori_loop(0, per, body, 0, unroll=4)


def write_sums(sums_out, scales, rows):
    sums_out[...] = jnp.zeros_like(sums_out)
    mask = scales[0][:rows]
    totals = [mask]
    for t in range(ITERS):
        below = jnp.where(mask > 0, scales[t + 1][:rows], 1.0)
        totals.append(jnp.where(mask > 0, scales[t][:rows] / below, 0.0))
    for t, total in enumerate(totals):
        line = jnp.sum(jnp.sum(total, axis=0, keepdims=True), axis=1, keepdims=True)
        sums_out[t : t + 1, :] = jnp.broadcast_to(line, (1, mask.shape[1]))


def numer_row_kernel(order, scal, hi_ref, lo_ref, h_ref, u_ref, after, *refs):
    outs, terms = refs[:-1], refs[-1]
    ext, tile = u_ref.shape
    offs = offsets(scal, hi_ref.shape[2] // tile)
    rows, per = hi_ref.shape[0], outs[0].shape[0]
    if len(outs) > 1:
        scaled_terms(h_ref, u_ref, terms, 0, ext)
    else:
        first = jnp.bitwise_xor(scal[0], order[0]) * per
        scaled_terms(h_ref, u_ref, terms, first, per + ext - rows)
    row_pieces(scal, offs, terms, hi_ref, lo_ref, u_ref, order, outs)


def numer_first(scal, r_hi, r_lo, row_factors, mask_ext, parts, scales, k):
    shares = len(parts)
    rows, tile = r_hi.shape[:2]
    factors = row_factors.shape[0]
    ext = mask_ext.shape[0]
    pad = ext - rows
    per = rows // shares
    return kernel_call(
        functools.partial(numer_first_kernel, k, shares),
        "numer_first",
        scal,
        [r_hi, r_lo, row_factors, mask_ext, *parts, *scales],
        [
            jax.ShapeDtypeStruct((ext, tile), F32),
            jax.ShapeDtypeStruct((pad + 1, factors, tile), F32),
            jax.ShapeDtypeStruct((8, tile), F32),
            jax.ShapeDtypeStruct((per, factors, tile), F32),
        ],
        [pltpu.VMEM((per + 2 * pad, factors, tile), F32)],
    )


def numer_col(scal, r_hi, r_lo, row_factors, u, after, order, shares):
    rows, tile = r_hi.shape[:2]
    factors = row_factors.shape[0]
    piece = jax.ShapeDtypeStruct((rows // shares, factors, tile), F32)
    return kernel_call(
        functools.partial(numer_col_kernel, order),
        "numer_col",
        scal,
        [r_hi, r_lo, row_factors, u, after],
        [piece] * len(order),
        [pltpu.VMEM((u.shape[0], factors, tile), F32)],
    )


def numer_row(scal, r_hi, r_lo, col_ext, u, after, order, shares):
    rows, tile = r_hi.shape[:2]
    factors = col_ext.shape[0]
    piece = jax.ShapeDtypeStruct((rows // shares, factors, tile), F32)
    return kernel_call(
        functools.partial(numer_row_kernel, order),
        "numer_row",
        scal,
        [r_hi, r_lo, col_ext, u, after],
        [piece] * len(order),
        [pltpu.VMEM((u.shape[0], 2 * factors, tile), BF16)],
    )


def mean_scale(sums):
    scale = sums[1:2, :] / sums[0:1, :]
    for t in range(1, ITERS):
        scale = scale * (sums[t + 1 : t + 2, :] / sums[0:1, :])
    return scale


def tile_sum(factor_ref, mask, j):
    tile = mask.shape[1]
    x = factor_ref[:, pl.ds(pl.multiple_of(j * tile, tile), tile)] * mask[pl.ds(j, 1), :]
    return jnp.sum(x, axis=1, keepdims=True)


def windows(sums, per):
    return [tree_sum(sums[t : t + len(sums) - per]) for t in range(per)]


def write_coefficient(old_ref, mask, first, lowers, times_out, plus_out):
    tile = mask.shape[1]
    for t, lower in enumerate(lowers):
        live = mask[pl.ds(first + t, 1), :]
        old = old_ref[:, t * tile : (t + 1) * tile]
        times_out[t] = jnp.where(live > 0, old / jnp.where(live > 0, lower * live, 1.0), 0.0)
        plus_out[t] = jnp.where(live > 0, 0.0, old)


def row_coefficient_kernel(pad, scal, old_ref, mask, other, times_out, plus_out):
    per = times_out.shape[0]
    first = scal[0] * per
    sums = [tile_sum(other, mask, first + t) for t in range(per + pad)]
    write_coefficient(old_ref, mask, first, windows(sums, per), times_out, plus_out)


def col_coefficient_kernel(pad, scal, old_ref, mask, other, ends, times_out, plus_out):
    per = times_out.shape[0]
    first = scal[0] * per
    sums = []
    for j in range(1, per + pad):
        total = tile_sum(other, mask, jnp.maximum(first - pad + j, 0))
        for start in range(0, pad, per):
            if start + j < pad:
                before = jnp.where(scal[scal.shape[0] - 1] > 0, ends[:, start + j : start + j + 1], 0.0)
                total = jnp.where(first == start, before, total)
        sums.append(total)
    sums.append(jnp.zeros_like(sums[0]))
    write_coefficient(old_ref, mask, first, windows(sums, per), times_out, plus_out)


def coefficient(kernel, scal, shares, old, mask_ext, other, *ends):
    factors = old.shape[0]
    tile = mask_ext.shape[1]
    rows = old.shape[1] // tile
    per = rows // shares
    specs = [pl.BlockSpec((factors, per * tile), lambda i, scal: (0, scal[0]))]
    specs += [vmem() for _ in range(2 + len(ends))]
    return kernel_call(
        functools.partial(kernel, mask_ext.shape[0] - rows),
        "coefficient",
        scal,
        [old, mask_ext, other, *ends],
        [jax.ShapeDtypeStruct((per, factors, tile), F32)] * 2,
        specs=specs,
    )


def update_kernel(scal, sums, times, plus, *refs):
    terms, out = refs[:-1], refs[-1]
    per, _, tile = times.shape
    c = mean_scale(sums[...])
    for t in range(per):
        numer = terms[0][t]
        for term in terms[1:]:
            numer = numer + term[t]
        out[:, t * tile : (t + 1) * tile] = times[t] * (numer * c * c) + plus[t]


def update(scal, sums, times, plus, terms):
    per, count, tile = terms[0].shape
    return kernel_call(
        update_kernel,
        "update",
        scal,
        [sums, times, plus, *terms],
        [jax.ShapeDtypeStruct((count, per * tile), F32)],
    )[0]


def xor_exchange(x, axis, k):
    return lax.ppermute(x, axis, [(i, i ^ k) for i in range(lax.axis_size(axis))])


def both_sides(x, even):
    size = lax.axis_size("genome")
    a = lax.ppermute(x, "genome", [(i, i ^ 1) for i in range(size)])
    b = lax.ppermute(x, "genome", [(i, (((i + 1) ^ 1) - 1) % size) for i in range(size)])
    return jnp.where(even > 0, a, b), jnp.where(even > 0, b, a)


def scatter_terms(pieces, extra=None, across=None):
    size = lax.axis_size("offset")

    def piece(k):
        return pieces[k] if extra is None else put(pieces[k], extra[k])

    def put(x, y):
        return x.at[: y.shape[0]].add(y)

    if size == 4:
        far = pieces[3] + xor_exchange(pieces[2], "offset", 1)
        if extra is not None:
            far = put(far, extra[3] + across)
        moved = xor_exchange(far, "offset", 3)
        return [piece(0), xor_exchange(piece(1), "offset", 1), moved], far
    moved = [xor_exchange(piece(k), "offset", k) for k in range(1, size)]
    return [piece(0), *moved], moved[0]


def per_device(counts, band_offset, bin_mask, row_factors, col_factors):
    rows, slots, tile = counts.shape[:3]
    factors = row_factors.shape[0]
    offset_count = lax.axis_size("offset")
    genome_count = lax.axis_size("genome")
    g = lax.axis_index("genome")
    o = lax.axis_index("offset").astype(jnp.int32)
    reach = slots * offset_count - 1
    pad = reach + 1

    line = jnp.broadcast_to(g, (1, tile))
    even = (line % 2 == 0).astype(F32)
    has_next = (line < genome_count - 1).astype(F32)
    has_prev = (line > 0).astype(F32)
    count = offset_count * -(-pad * offset_count // rows)
    index = lax.broadcasted_iota(jnp.int32, (count, tile), 0)
    share, k = index // offset_count, index % offset_count
    mine = (jnp.bitwise_xor(share, k) == o).astype(F32) * has_prev
    flags = jnp.concatenate([even, has_next, has_prev, mine])
    before = jnp.broadcast_to((g > 0).astype(jnp.int32), (1,))
    scal = jnp.concatenate([jnp.broadcast_to(o, (1,)), band_offset, before])
    flags, scal, bin_mask = lax.optimization_barrier((flags, scal, bin_mask))
    even, has_next, has_prev = flags[0:1], flags[1:2], flags[2:3]
    mine = flags[3:]

    mask = bin_mask.astype(F32).reshape(rows, tile)
    mask_next, _ = both_sides(mask[:pad], even)
    keep = lax.broadcasted_iota(jnp.int32, (pad, 1), 0) < reach
    mask_ext = jnp.concatenate([mask, jnp.where(keep, mask_next * has_next, 0.0)])

    counts = pltpu.with_memory_space_constraint(counts, pltpu.HBM)
    inner_v, kept = first_main(scal, counts, mask, rows + pad)
    col_late, _ = lax.optimization_barrier((col_factors, inner_v))
    ring_left = [(i, (i - 1) % genome_count) for i in range(genome_count)]
    col_next = lax.ppermute(col_late[:, : pad * tile], "genome", ring_left)
    col_next = jnp.where(has_next[:, :1] > 0, col_next, 1.0)
    col_ext = jnp.concatenate([col_factors, col_next], axis=1)

    scales = []
    quarter = rows // (ITERS + 1)
    for t in range(ITERS):
        if t == 0:
            u = mask_ext
            v, edge = first_edge(scal, kept, u, inner_v)
        else:
            v, edge, u = cover_edge(scal, kept, mask_ext, parts, ratios[0])
        scales.append(u)
        after, before = both_sides(edge, even)
        if t > 0:
            v = cover_main(scal, kept, u, v)
        else:
            *ratios, v = ratio(scal, kept, row_factors, col_factors, v, [], 0, quarter)
        front = v[:pad] + before[pad:] * has_prev
        back = v[rows:] + after[:pad] * has_next
        x = jnp.concatenate([front, v[pad:rows], back])
        others = {k: xor_exchange(x, "offset", k) for k in reversed(range(1, offset_count))}
        parts = [x, *others.values()]
        start = (t + 1) * quarter
        ratios = ratio(scal, kept, row_factors, col_ext, x, ratios, start, quarter)

    r_hi, r_lo = ratios
    u, tail, sums, early = numer_first(
        scal, r_hi, r_lo, row_factors, mask_ext, parts, scales, EARLY
    )
    (w_early,) = numer_row(scal, r_hi, r_lo, col_ext, u, sums, [EARLY], offset_count)
    right = [(i, (i + 1) % genome_count) for i in range(genome_count)]
    arrived = lax.ppermute(tail, "genome", right)
    row_terms = coefficient(
        row_coefficient_kernel, scal, offset_count, row_factors, mask_ext, col_ext
    )
    col_terms = coefficient(
        col_coefficient_kernel, scal, offset_count, col_factors, mask_ext, row_factors, arrived[pad]
    )
    order = [k for k in (3, 1, 0, *range(4, offset_count))]
    rest = numer_col(scal, r_hi, r_lo, row_factors, u, col_terms[0], order, offset_count)
    h_parts = dict(zip(order, rest)) | {EARLY: early}
    h_parts = [h_parts[k] for k in range(offset_count)]
    per = rows // offset_count

    if offset_count == 4 and pad <= per:
        diagonal = [
            (i * 4 + j, (i + 1) % genome_count * 4 + (j ^ 1))
            for i in range(genome_count)
            for j in range(4)
        ]
        across = lax.ppermute(tail[:pad], ("genome", "offset"), diagonal)
        extra = [arrived[:pad] * mine[k : k + 1] for k in range(4)]
        h_terms, half_way = scatter_terms(h_parts, extra, across * mine[3:4])
    else:
        h_parts = list(h_parts)
        for s in range(-(-pad // per)):
            piece = arrived[s * per : min(pad, (s + 1) * per)]
            for k in range(offset_count):
                at = s * offset_count + k
                h_parts[k] = h_parts[k].at[: piece.shape[0]].add(piece * mine[at : at + 1])
        h_terms, half_way = scatter_terms(h_parts)
    w_rest = numer_row(scal, r_hi, r_lo, col_ext, u, half_way, order, offset_count)
    w_parts = dict(zip(order, w_rest)) | {EARLY: w_early}
    w_terms, _ = scatter_terms([w_parts[k] for k in range(offset_count)])

    sums, _ = lax.optimization_barrier((sums, h_terms[2]))
    sums = jnp.sum(lax.all_gather(sums, "genome"), axis=0)
    bias = (u[:rows] * mean_scale(sums)).reshape(-1)

    col_update = update(scal, sums, *col_terms, h_terms)
    row_update = update(scal, sums, *row_terms, w_terms)
    return bias, row_update, col_update


def solution(mesh):
    return jax.shard_map(
        per_device,
        mesh=mesh,
        in_specs=(
            P("genome", "offset", None, None),
            P("offset"),
            P("genome"),
            P(None, "genome"),
            P(None, "genome"),
        ),
        out_specs=(P("genome"), P(None, ("genome", "offset")), P(None, ("genome", "offset"))),
        check_vma=False,
    )
```

```python
import functools

import jax
import jax.numpy as jnp
from jax import lax
from jax.experimental import pallas as pl
from jax.experimental.pallas import tpu as pltpu
from jax.sharding import PartitionSpec as P

ITERS = 3
STEP = 8
EARLY = 2
F32 = jnp.float32
BF16 = jnp.bfloat16
VMEM_LIMIT = 20 * 1024 * 1024
NT = (((1,), (1,)), ((), ()))
TN = (((0,), (0,)), ((), ()))


def split(x):
    hi = x.astype(BF16)
    lo = (x - hi.astype(F32)).astype(BF16)
    return hi, lo


def tree_sum(parts):
    while len(parts) > 1:
        parts = [a + b for a, b in zip(parts[::2], parts[1::2])]
    return parts[0]


def params():
    return pltpu.CompilerParams(vmem_limit_bytes=VMEM_LIMIT)


def scale_from(mask, parts):
    cover = tree_sum([p[...] for p in parts[:1] + parts[:0:-1]])
    live = mask[...] > 0
    return jnp.where(live, 1.0 / jnp.where(live, cover, 1.0), 0.0)


def vmem():
    return pl.BlockSpec(memory_space=pltpu.VMEM)


def kernel_call(body, name, scalars, args, outs, scratch=(), aliases=None, specs=None):
    return pl.pallas_call(
        body,
        grid_spec=pltpu.PrefetchScalarGridSpec(
            num_scalar_prefetch=1,
            grid=(1,),
            in_specs=specs or [vmem() for _ in args],
            out_specs=[vmem() for _ in outs],
            scratch_shapes=list(scratch),
        ),
        out_shape=outs,
        input_output_aliases=aliases or {},
        compiler_params=params(),
        name=name,
    )(scalars, *args)


def offsets(scal, slots):
    return [scal[1 + s] for s in range(slots)]


def by_diagonal(offs, slots, go):
    for s in range(slots):

        @pl.when(offs[s] == 0)
        def _():
            go(s)

    @pl.when(functools.reduce(jnp.logical_and, [offs[s] != 0 for s in range(slots)]))
    def _():
        go(-1)


def tile_value(counts, i, s, diagonal):
    c = counts[i, s].astype(F32)
    if s == diagonal:
        tile = c.shape[0]
        r = lax.broadcasted_iota(jnp.int32, (tile, tile), 0)
        q = lax.broadcasted_iota(jnp.int32, (tile, tile), 1)
        c = jnp.where(r < q, c, jnp.where(r == q, 0.5 * c, 0.0))
    return c


def cover_block(offs, counts, u_ref, acc, base, diagonal, at, kept=None):
    slots, tile = counts.shape[1:3]
    ones = jnp.ones((8, tile), BF16)
    u_block = u_ref[pl.ds(base, STEP), :]
    u_cols = u_block.T
    u_across = [u_ref[pl.ds(base + offs[s], STEP), :] for s in range(slots)]
    cols = [[] for _ in range(slots)]
    sums = []
    for t in range(STEP):
        total = None
        for s in range(slots):
            c = tile_value(counts, at + t, s, diagonal)
            if kept is not None:
                kept[base + t, s] = c
            term = c * u_across[s][t : t + 1]
            total = term if total is None else total + term
            cols[s].append(jnp.sum(c * u_cols[:, t : t + 1], axis=0, keepdims=True))
        hi, lo = split(total)
        row = lax.dot_general(ones, hi, NT, preferred_element_type=F32)
        row = row + lax.dot_general(ones, lo, NT, preferred_element_type=F32)
        sums.append(row[:1])
    acc[pl.ds(base, STEP), :] += jnp.concatenate(sums, axis=0)
    for s in range(slots):
        acc[pl.ds(base + offs[s], STEP), :] += jnp.concatenate(cols[s], axis=0)


def block_copies(hbm, buffer, sems, bases):
    return [
        pltpu.make_async_copy(
            hbm.at[pl.ds(base, STEP)], buffer.at[pl.ds(k * STEP, STEP)], sems.at[k]
        )
        for k, base in enumerate(bases)
    ]


def edge_bases(rows, pad):
    return list(range(0, pad, STEP)) + list(range(rows - pad, rows, STEP))


def write_edge(v_out, edge_out, rows):
    pad = v_out.shape[0] - rows
    edge_out[:pad] = v_out[:pad]
    edge_out[pad:] = v_out[rows:]


def first_main_kernel(scal, hbm, mask, v_out, kept, buffer, sems):
    rows, slots = hbm.shape[:2]
    offs = offsets(scal, slots)
    pad = v_out.shape[0] - rows
    inner = list(range(pad, rows - pad, STEP))
    bases = inner + edge_bases(rows, pad)
    copies = block_copies(hbm, buffer, sems, bases)
    for copy in copies:
        copy.start()
    v_out[...] = jnp.zeros_like(v_out)

    def go(diagonal):
        for k, base in enumerate(bases):
            copies[k].wait()
            at = k * STEP
            if base in inner:
                cover_block(offs, buffer, mask, v_out, base, diagonal, at, kept)
            else:
                for t in range(STEP):
                    for s in range(slots):
                        kept[base + t, s] = tile_value(buffer, at + t, s, diagonal)

    by_diagonal(offs, slots, go)


def first_edge_kernel(scal, kept, u_ref, inner_v, v_out, edge_out):
    rows, slots = kept.shape[:2]
    offs = offsets(scal, slots)
    v_out[...] = inner_v[...]
    for base in edge_bases(rows, u_ref.shape[0] - rows):
        cover_block(offs, kept, u_ref, v_out, base, -1, base)
    write_edge(v_out, edge_out, rows)


def edge_kernel(scal, kept, mask, *refs):
    v_out, edge_out, u_out = refs[-3:]
    rows, slots = kept.shape[:2]
    offs = offsets(scal, slots)
    u_out[...] = scale_from(mask, refs[:-4])
    v_out[...] = jnp.zeros_like(v_out)
    for base in edge_bases(rows, mask.shape[0] - rows):
        cover_block(offs, kept, u_out, v_out, base, -1, base)
    write_edge(v_out, edge_out, rows)


def main_kernel(scal, kept, u_ref, edge_v, v_out):
    rows, slots = kept.shape[:2]
    offs = offsets(scal, slots)
    pad = edge_v.shape[0] - rows
    v_out[...] = edge_v[...]
    for base in range(pad, rows - pad, STEP):
        cover_block(offs, kept, u_ref, v_out, base, -1, base)


def first_main(scal, counts, mask, ext):
    rows, slots, tile = counts.shape[:3]
    outs = [jax.ShapeDtypeStruct((ext, tile), F32), pltpu.VMEM(counts.shape, F32)]
    return kernel_call(
        first_main_kernel,
        "first_main",
        scal,
        [counts, mask],
        outs,
        [pltpu.VMEM(counts.shape, counts.dtype), pltpu.SemaphoreType.DMA((rows // STEP,))],
        specs=[pl.BlockSpec(memory_space=pltpu.HBM), vmem()],
    )


def first_edge(scal, kept, u, inner_v):
    rows, tile = kept.shape[0], kept.shape[2]
    flat = jax.ShapeDtypeStruct(u.shape, F32)
    edge = jax.ShapeDtypeStruct((2 * (u.shape[0] - rows), tile), F32)
    return kernel_call(first_edge_kernel, "first_edge", scal, [kept, u, inner_v], [flat, edge])


def cover_edge(scal, kept, mask_ext, parts, after):
    rows, tile = kept.shape[0], kept.shape[2]
    flat = jax.ShapeDtypeStruct(mask_ext.shape, F32)
    edge = jax.ShapeDtypeStruct((2 * (mask_ext.shape[0] - rows), tile), F32)
    args = [kept, mask_ext, *parts, after]
    return kernel_call(edge_kernel, "cover_edge", scal, args, [flat, edge, flat])


def cover_main(scal, kept, u, edge_v):
    outs = [jax.ShapeDtypeStruct(u.shape, F32)]
    return kernel_call(main_kernel, "cover_main", scal, [kept, u, edge_v], outs)[0]


def ratio_kernel(start, count, pad, scal, kept, w_ref, h_ref, after, *refs):
    slots, tile = kept.shape[1:3]
    offs = offsets(scal, slots)
    if start == 0:
        hi_out, lo_out, same, h_terms = refs
        same[...] = after[...]
    else:
        hi_out, lo_out, h_terms = refs[-3:]

    def prepare(j, carry):
        hi, lo = split(h_ref[:, pl.ds(pl.multiple_of(j * tile, tile), tile)])
        h_terms[j - start] = jnp.concatenate([hi, lo, hi, lo], axis=0)
        return carry

    lax.fori_loop(start, start + count + pad, prepare, 0, unroll=4)

    def go(diagonal):
        def body(i, carry):
            hi, lo = split(w_ref[:, pl.ds(pl.multiple_of(i * tile, tile), tile)])
            w_terms = jnp.concatenate([hi, hi, lo, lo], axis=0)
            for s in range(slots):
                model = lax.dot_general(
                    w_terms, h_terms[i - start + offs[s]], TN, preferred_element_type=F32
                )
                values = kept[i, s]
                if s == diagonal:
                    values = values + values.T
                r_hi, r_lo = split(values * (1.0 / model))
                hi_out[i, :, s * tile : (s + 1) * tile] = r_hi
                lo_out[i, :, s * tile : (s + 1) * tile] = r_lo
            return carry

        lax.fori_loop(start, start + count, body, 0, unroll=4)

    by_diagonal(offs, slots, go)


def ratio(scal, kept, row_factors, col_ext, after, earlier, start, count):
    rows, slots, tile = kept.shape[:3]
    factors = row_factors.shape[0]
    pad = after.shape[0] - rows
    out = pltpu.VMEM((rows, tile, slots * tile), BF16)
    return kernel_call(
        functools.partial(ratio_kernel, start, count, pad),
        "ratio",
        scal,
        [kept, row_factors, col_ext, after, *earlier],
        [out, out] + [jax.ShapeDtypeStruct(after.shape, F32)] * (start == 0),
        [pltpu.VMEM((count + pad, 4 * factors, tile), BF16)],
        {5: 0, 6: 1} if earlier else {},
    )


def row_numer(offs, g_all, hi_ref, lo_ref, u_ref, i):
    slots = hi_ref.shape[2] // g_all.shape[2]
    factors = g_all.shape[1] // 2
    g = jnp.concatenate([g_all[i + offs[s]] for s in range(slots)], axis=1)
    big = lax.dot_general(g, hi_ref[i], NT, preferred_element_type=F32)
    small = lax.dot_general(g[:factors], lo_ref[i], NT, preferred_element_type=F32)
    return (big[:factors] + big[factors:] + small) * u_ref[pl.ds(i, 1), :]


def col_numer(w_ref, hi_ref, lo_ref, u_ref, i):
    tile = u_ref.shape[1]
    factors = w_ref.shape[0]
    w = w_ref[:, pl.ds(pl.multiple_of(i * tile, tile), tile)]
    hi, lo = split(w * u_ref[pl.ds(i, 1), :])
    big = jnp.dot(jnp.concatenate([hi, lo], axis=0), hi_ref[i], preferred_element_type=F32)
    small = jnp.dot(hi, lo_ref[i], preferred_element_type=F32)
    return big[:factors] + big[factors:] + small


def col_loop(offs, w_ref, hi_ref, lo_ref, u_ref, acc, start, count, shift):
    tile = u_ref.shape[1]

    def body(n, carry):
        i = start + n
        cols = col_numer(w_ref, hi_ref, lo_ref, u_ref, i)
        for s in range(hi_ref.shape[2] // tile):
            acc[i + offs[s] - shift] += cols[:, s * tile : (s + 1) * tile]
        return carry

    lax.fori_loop(0, count, body, 0, unroll=4)


def row_pieces(scal, offs, g_ref, hi_ref, lo_ref, u_ref, order, outs):
    for k, out in zip(order, outs):
        per = out.shape[0]
        first = jnp.bitwise_xor(scal[0], k) * per

        def body(t, carry):
            out[t] = row_numer(offs, g_ref, hi_ref, lo_ref, u_ref, first + t)
            return carry

        lax.fori_loop(0, per, body, 0, unroll=4)


def scaled_terms(h_ref, u_ref, terms, start, count):
    tile = u_ref.shape[1]
    factors = h_ref.shape[0]

    def fill(n, carry):
        j = start + n
        x = h_ref[:, pl.ds(pl.multiple_of(j * tile, tile), tile)] * u_ref[pl.ds(j, 1), :]
        hi, lo = split(x)
        terms[j, :factors] = hi
        terms[j, factors:] = lo
        return carry

    lax.fori_loop(0, count, fill, 0, unroll=4)


def numer_first_kernel(k, shares, scal, hi_ref, lo_ref, w_ref, h_ref, mask, *refs):
    parts, scales = refs[:shares], refs[shares : shares + ITERS]
    u_out, tail_out, sums_out, out, acc, terms = refs[shares + ITERS :]
    rows = hi_ref.shape[0]
    ext, tile = mask.shape
    offs = offsets(scal, hi_ref.shape[2] // tile)
    per = rows // shares
    pad = ext - rows
    u_out[...] = scale_from(mask, parts)

    acc[...] = jnp.zeros_like(acc)
    col_loop(offs, w_ref, hi_ref, lo_ref, u_out, acc, rows - pad, pad, rows - pad)
    for t in range(pad):
        tail_out[t] = acc[pad + t] * u_out[rows + t : rows + t + 1, :]
    lane = lax.broadcasted_iota(jnp.int32, tail_out.shape[1:], 1)
    ends = jnp.zeros(tail_out.shape[1:], F32)
    for t in range(pad):
        ends = jnp.where(lane == t, tile_sum(w_ref, mask, rows - pad + t), ends)
    tail_out[pad] = ends

    first = jnp.bitwise_xor(scal[0], k) * per
    scaled_terms(h_ref, u_out, terms, first, per + pad)
    row_pieces(scal, offs, terms, hi_ref, lo_ref, u_out, [k], [out])
    write_sums(sums_out, [*scales, u_out], rows)


def numer_col_kernel(order, scal, hi_ref, lo_ref, w_ref, u_ref, after, *refs):
    outs, acc = refs[:-1], refs[-1]
    rows = hi_ref.shape[0]
    tile = u_ref.shape[1]
    offs = offsets(scal, hi_ref.shape[2] // tile)
    per = outs[0].shape[0]
    acc[...] = jnp.zeros_like(acc)
    col_loop(offs, w_ref, hi_ref, lo_ref, u_ref, acc, 0, rows, 0)
    for k, out in zip(order, outs):
        first = jnp.bitwise_xor(scal[0], k) * per

        def body(t, carry):
            out[t] = acc[first + t] * u_ref[pl.ds(first + t, 1), :]
            return carry

        lax.fori_loop(0, per, body, 0, unroll=4)


def write_sums(sums_out, scales, rows):
    sums_out[...] = jnp.zeros_like(sums_out)
    mask = scales[0][:rows]
    totals = [mask]
    for t in range(ITERS):
        below = jnp.where(mask > 0, scales[t + 1][:rows], 1.0)
        totals.append(jnp.where(mask > 0, scales[t][:rows] / below, 0.0))
    for t, total in enumerate(totals):
        line = jnp.sum(jnp.sum(total, axis=0, keepdims=True), axis=1, keepdims=True)
        sums_out[t : t + 1, :] = jnp.broadcast_to(line, (1, mask.shape[1]))


def numer_row_kernel(order, scal, hi_ref, lo_ref, h_ref, u_ref, after, *refs):
    outs, terms = refs[:-1], refs[-1]
    ext, tile = u_ref.shape
    offs = offsets(scal, hi_ref.shape[2] // tile)
    scaled_terms(h_ref, u_ref, terms, 0, ext)
    row_pieces(scal, offs, terms, hi_ref, lo_ref, u_ref, order, outs)


def numer_first(scal, r_hi, r_lo, row_factors, col_ext, mask_ext, parts, scales, k):
    shares = len(parts)
    rows, tile = r_hi.shape[:2]
    factors = row_factors.shape[0]
    ext = mask_ext.shape[0]
    pad = ext - rows
    per = rows // shares
    return kernel_call(
        functools.partial(numer_first_kernel, k, shares),
        "numer_first",
        scal,
        [r_hi, r_lo, row_factors, col_ext, mask_ext, *parts, *scales],
        [
            jax.ShapeDtypeStruct((ext, tile), F32),
            jax.ShapeDtypeStruct((pad + 1, factors, tile), F32),
            jax.ShapeDtypeStruct((8, tile), F32),
            jax.ShapeDtypeStruct((per, factors, tile), F32),
        ],
        [
            pltpu.VMEM((2 * pad, factors, tile), F32),
            pltpu.VMEM((ext, 2 * factors, tile), BF16),
        ],
    )


def numer_col(scal, r_hi, r_lo, row_factors, u, after, order, shares):
    rows, tile = r_hi.shape[:2]
    factors = row_factors.shape[0]
    piece = jax.ShapeDtypeStruct((rows // shares, factors, tile), F32)
    return kernel_call(
        functools.partial(numer_col_kernel, order),
        "numer_col",
        scal,
        [r_hi, r_lo, row_factors, u, after],
        [piece] * len(order),
        [pltpu.VMEM((u.shape[0], factors, tile), F32)],
    )


def numer_row(scal, r_hi, r_lo, col_ext, u, after, order, shares):
    rows, tile = r_hi.shape[:2]
    factors = col_ext.shape[0]
    piece = jax.ShapeDtypeStruct((rows // shares, factors, tile), F32)
    return kernel_call(
        functools.partial(numer_row_kernel, order),
        "numer_row",
        scal,
        [r_hi, r_lo, col_ext, u, after],
        [piece] * len(order),
        [pltpu.VMEM((u.shape[0], 2 * factors, tile), BF16)],
    )


def mean_scale(sums):
    scale = sums[1:2, :] / sums[0:1, :]
    for t in range(1, ITERS):
        scale = scale * (sums[t + 1 : t + 2, :] / sums[0:1, :])
    return scale


def tile_sum(factor_ref, mask, j):
    tile = mask.shape[1]
    x = factor_ref[:, pl.ds(pl.multiple_of(j * tile, tile), tile)] * mask[pl.ds(j, 1), :]
    return jnp.sum(x, axis=1, keepdims=True)


def windows(sums, per):
    return [tree_sum(sums[t : t + len(sums) - per]) for t in range(per)]


def write_coefficient(old_ref, mask, first, lowers, times_out, plus_out):
    tile = mask.shape[1]
    for t, lower in enumerate(lowers):
        live = mask[pl.ds(first + t, 1), :]
        old = old_ref[:, t * tile : (t + 1) * tile]
        times_out[t] = jnp.where(live > 0, old / jnp.where(live > 0, lower * live, 1.0), 0.0)
        plus_out[t] = jnp.where(live > 0, 0.0, old)


def row_coefficient_kernel(pad, scal, old_ref, mask, other, times_out, plus_out):
    per = times_out.shape[0]
    first = scal[0] * per
    sums = [tile_sum(other, mask, first + t) for t in range(per + pad)]
    write_coefficient(old_ref, mask, first, windows(sums, per), times_out, plus_out)


def col_coefficient_kernel(pad, scal, old_ref, mask, other, ends, times_out, plus_out):
    per = times_out.shape[0]
    first = scal[0] * per
    sums = []
    for j in range(1, per + pad):
        total = tile_sum(other, mask, jnp.maximum(first - pad + j, 0))
        for start in range(0, pad, per):
            if start + j < pad:
                before = jnp.where(scal[scal.shape[0] - 1] > 0, ends[:, start + j : start + j + 1], 0.0)
                total = jnp.where(first == start, before, total)
        sums.append(total)
    sums.append(jnp.zeros_like(sums[0]))
    write_coefficient(old_ref, mask, first, windows(sums, per), times_out, plus_out)


def coefficient(kernel, scal, shares, old, mask_ext, other, *ends):
    factors = old.shape[0]
    tile = mask_ext.shape[1]
    rows = old.shape[1] // tile
    per = rows // shares
    specs = [pl.BlockSpec((factors, per * tile), lambda i, scal: (0, scal[0]))]
    specs += [vmem() for _ in range(2 + len(ends))]
    return kernel_call(
        functools.partial(kernel, mask_ext.shape[0] - rows),
        "coefficient",
        scal,
        [old, mask_ext, other, *ends],
        [jax.ShapeDtypeStruct((per, factors, tile), F32)] * 2,
        specs=specs,
    )


def update_kernel(scal, sums, times, plus, *refs):
    terms, out = refs[:-1], refs[-1]
    per, _, tile = times.shape
    c = mean_scale(sums[...])
    for t in range(per):
        numer = terms[0][t]
        for term in terms[1:]:
            numer = numer + term[t]
        out[:, t * tile : (t + 1) * tile] = times[t] * (numer * c * c) + plus[t]


def update(scal, sums, times, plus, terms):
    per, count, tile = terms[0].shape
    return kernel_call(
        update_kernel,
        "update",
        scal,
        [sums, times, plus, *terms],
        [jax.ShapeDtypeStruct((count, per * tile), F32)],
    )[0]


def xor_exchange(x, axis, k):
    return lax.ppermute(x, axis, [(i, i ^ k) for i in range(lax.axis_size(axis))])


def both_sides(x, even):
    size = lax.axis_size("genome")
    a = lax.ppermute(x, "genome", [(i, i ^ 1) for i in range(size)])
    b = lax.ppermute(x, "genome", [(i, (((i + 1) ^ 1) - 1) % size) for i in range(size)])
    return jnp.where(even > 0, a, b), jnp.where(even > 0, b, a)


def scatter_terms(pieces):
    size = lax.axis_size("offset")
    if size == 4:
        far = pieces[3] + xor_exchange(pieces[2], "offset", 1)
        far = xor_exchange(far, "offset", 3)
        return [pieces[0], xor_exchange(pieces[1], "offset", 1), far]
    return [pieces[0]] + [xor_exchange(pieces[k], "offset", k) for k in range(1, size)]


def per_device(counts, band_offset, bin_mask, row_factors, col_factors):
    rows, slots, tile = counts.shape[:3]
    factors = row_factors.shape[0]
    offset_count = lax.axis_size("offset")
    genome_count = lax.axis_size("genome")
    g = lax.axis_index("genome")
    o = lax.axis_index("offset").astype(jnp.int32)
    reach = slots * offset_count - 1
    pad = reach + 1

    line = jnp.broadcast_to(g, (1, tile))
    even = (line % 2 == 0).astype(F32)
    has_next = (line < genome_count - 1).astype(F32)
    has_prev = (line > 0).astype(F32)
    count = offset_count * -(-pad * offset_count // rows)
    index = lax.broadcasted_iota(jnp.int32, (count, tile), 0)
    share, k = index // offset_count, index % offset_count
    mine = (jnp.bitwise_xor(share, k) == o).astype(F32) * has_prev
    flags = jnp.concatenate([even, has_next, has_prev, mine])
    before = jnp.broadcast_to((g > 0).astype(jnp.int32), (1,))
    scal = jnp.concatenate([jnp.broadcast_to(o, (1,)), band_offset, before])
    flags, scal, bin_mask = lax.optimization_barrier((flags, scal, bin_mask))
    even, has_next, has_prev = flags[0:1], flags[1:2], flags[2:3]
    mine = flags[3:]

    mask = bin_mask.astype(F32).reshape(rows, tile)
    mask_next, _ = both_sides(mask[:pad], even)
    keep = lax.broadcasted_iota(jnp.int32, (pad, 1), 0) < reach
    mask_ext = jnp.concatenate([mask, jnp.where(keep, mask_next * has_next, 0.0)])

    counts = pltpu.with_memory_space_constraint(counts, pltpu.HBM)
    inner_v, kept = first_main(scal, counts, mask, rows + pad)
    col_late, _ = lax.optimization_barrier((col_factors, inner_v))
    ring_left = [(i, (i - 1) % genome_count) for i in range(genome_count)]
    col_next = lax.ppermute(col_late[:, : pad * tile], "genome", ring_left)
    col_next = jnp.where(has_next[:, :1] > 0, col_next, 1.0)
    col_ext = jnp.concatenate([col_factors, col_next], axis=1)

    scales = []
    quarter = rows // (ITERS + 1)
    for t in range(ITERS):
        if t == 0:
            u = mask_ext
            v, edge = first_edge(scal, kept, u, inner_v)
        else:
            v, edge, u = cover_edge(scal, kept, mask_ext, parts, ratios[0])
        scales.append(u)
        after, before = both_sides(edge, even)
        if t > 0:
            v = cover_main(scal, kept, u, v)
        else:
            *ratios, v = ratio(scal, kept, row_factors, col_factors, v, [], 0, quarter)
        front = v[:pad] + before[pad:] * has_prev
        back = v[rows:] + after[:pad] * has_next
        x = jnp.concatenate([front, v[pad:rows], back])
        others = {k: xor_exchange(x, "offset", k) for k in reversed(range(1, offset_count))}
        parts = [x, *others.values()]
        start = (t + 1) * quarter
        ratios = ratio(scal, kept, row_factors, col_ext, x, ratios, start, quarter)

    r_hi, r_lo = ratios
    per = rows // offset_count
    u, tail, sums, early = numer_first(
        scal, r_hi, r_lo, row_factors, col_ext, mask_ext, parts, scales, EARLY
    )
    order = [EARLY, *(k for k in range(offset_count) if k != EARLY)]
    pieces = numer_col(scal, r_hi, r_lo, row_factors, u, sums, order, offset_count)
    h_parts = dict(zip(order, pieces))

    right = [(i, (i + 1) % genome_count) for i in range(genome_count)]
    arrived = lax.ppermute(tail, "genome", right)
    for s in range(-(-pad // per)):
        piece = arrived[s * per : min(pad, (s + 1) * per)]
        for k in range(offset_count):
            at = s * offset_count + k
            h_parts[k] = h_parts[k].at[: piece.shape[0]].add(piece * mine[at : at + 1])

    row_terms = coefficient(
        row_coefficient_kernel, scal, offset_count, row_factors, mask_ext, col_ext
    )
    col_terms = coefficient(
        col_coefficient_kernel, scal, offset_count, col_factors, mask_ext, row_factors, arrived[pad]
    )
    order = [k for k in (3, 1, 0, *range(4, offset_count))]
    pieces = numer_row(scal, r_hi, r_lo, col_ext, u, h_parts[EARLY], order, offset_count)
    w_parts = dict(zip(order, pieces)) | {EARLY: early}
    w_terms = scatter_terms([w_parts[k] for k in range(offset_count)])
    h_terms = scatter_terms([h_parts[k] for k in range(offset_count)])

    sums, _ = lax.optimization_barrier((sums, w_terms[2]))
    sums = jnp.sum(lax.all_gather(sums, "genome"), axis=0)
    bias = (u[:rows] * mean_scale(sums)).reshape(-1)

    col_update = update(scal, sums, *col_terms, h_terms)
    row_update = update(scal, sums, *row_terms, w_terms)
    return bias, row_update, col_update


def solution(mesh):
    return jax.shard_map(
        per_device,
        mesh=mesh,
        in_specs=(
            P("genome", "offset", None, None),
            P("offset"),
            P("genome"),
            P(None, "genome"),
            P(None, "genome"),
        ),
        out_specs=(P("genome"), P(None, ("genome", "offset")), P(None, ("genome", "offset"))),
        check_vma=False,
    )
```

```python
import functools

import jax
import jax.numpy as jnp
from jax import lax
from jax.experimental import pallas as pl
from jax.experimental.pallas import tpu as pltpu
from jax.sharding import PartitionSpec as P

ITERS = 3
STEP = 8
EARLY = 2
F32 = jnp.float32
BF16 = jnp.bfloat16
VMEM_LIMIT = 20 * 1024 * 1024
NT = (((1,), (1,)), ((), ()))
TN = (((0,), (0,)), ((), ()))


def split(x):
    hi = x.astype(BF16)
    lo = (x - hi.astype(F32)).astype(BF16)
    return hi, lo


def tree_sum(parts):
    while len(parts) > 1:
        parts = [a + b for a, b in zip(parts[::2], parts[1::2])]
    return parts[0]


def params():
    return pltpu.CompilerParams(vmem_limit_bytes=VMEM_LIMIT)


def scale_from(mask, parts):
    cover = tree_sum([p[...] for p in parts[:1] + parts[:0:-1]])
    live = mask[...] > 0
    return jnp.where(live, 1.0 / jnp.where(live, cover, 1.0), 0.0)


def vmem():
    return pl.BlockSpec(memory_space=pltpu.VMEM)


def kernel_call(body, name, scalars, args, outs, scratch=(), aliases=None, specs=None):
    return pl.pallas_call(
        body,
        grid_spec=pltpu.PrefetchScalarGridSpec(
            num_scalar_prefetch=1,
            grid=(1,),
            in_specs=specs or [vmem() for _ in args],
            out_specs=[vmem() for _ in outs],
            scratch_shapes=list(scratch),
        ),
        out_shape=outs,
        input_output_aliases=aliases or {},
        compiler_params=params(),
        name=name,
    )(scalars, *args)


def offsets(scal, slots):
    return [scal[1 + s] for s in range(slots)]


def by_diagonal(offs, slots, go):
    for s in range(slots):

        @pl.when(offs[s] == 0)
        def _():
            go(s)

    @pl.when(functools.reduce(jnp.logical_and, [offs[s] != 0 for s in range(slots)]))
    def _():
        go(-1)


def tile_value(counts, i, s, diagonal):
    c = counts[i, s].astype(F32)
    if s == diagonal:
        tile = c.shape[0]
        r = lax.broadcasted_iota(jnp.int32, (tile, tile), 0)
        q = lax.broadcasted_iota(jnp.int32, (tile, tile), 1)
        c = jnp.where(r < q, c, jnp.where(r == q, 0.5 * c, 0.0))
    return c


def cover_block(offs, counts, u_ref, acc, base, diagonal, at, kept=None):
    slots, tile = counts.shape[1:3]
    ones = jnp.ones((8, tile), BF16)
    u_block = u_ref[pl.ds(base, STEP), :]
    u_cols = u_block.T
    u_across = [u_ref[pl.ds(base + offs[s], STEP), :] for s in range(slots)]
    cols = [[] for _ in range(slots)]
    sums = []
    for t in range(STEP):
        total = None
        for s in range(slots):
            c = tile_value(counts, at + t, s, diagonal)
            if kept is not None:
                kept[base + t, s] = c
            term = c * u_across[s][t : t + 1]
            total = term if total is None else total + term
            cols[s].append(jnp.sum(c * u_cols[:, t : t + 1], axis=0, keepdims=True))
        hi, lo = split(total)
        row = lax.dot_general(ones, hi, NT, preferred_element_type=F32)
        row = row + lax.dot_general(ones, lo, NT, preferred_element_type=F32)
        sums.append(row[:1])
    acc[pl.ds(base, STEP), :] += jnp.concatenate(sums, axis=0)
    for s in range(slots):
        acc[pl.ds(base + offs[s], STEP), :] += jnp.concatenate(cols[s], axis=0)


def block_copies(hbm, buffer, sems, bases):
    return [
        pltpu.make_async_copy(
            hbm.at[pl.ds(base, STEP)], buffer.at[pl.ds(k * STEP, STEP)], sems.at[k]
        )
        for k, base in enumerate(bases)
    ]


def edge_bases(rows, pad):
    return list(range(0, pad, STEP)) + list(range(rows - pad, rows, STEP))


def write_edge(v_out, edge_out, rows):
    pad = v_out.shape[0] - rows
    edge_out[:pad] = v_out[:pad]
    edge_out[pad:] = v_out[rows:]


def first_main_kernel(scal, hbm, mask, v_out, kept, buffer, sems):
    rows, slots = hbm.shape[:2]
    offs = offsets(scal, slots)
    pad = v_out.shape[0] - rows
    inner = list(range(pad, rows - pad, STEP))
    bases = inner + edge_bases(rows, pad)
    copies = block_copies(hbm, buffer, sems, bases)
    for copy in copies:
        copy.start()
    v_out[...] = jnp.zeros_like(v_out)

    def go(diagonal):
        for k, base in enumerate(bases):
            copies[k].wait()
            at = k * STEP
            if base in inner:
                cover_block(offs, buffer, mask, v_out, base, diagonal, at, kept)
            else:
                for t in range(STEP):
                    for s in range(slots):
                        kept[base + t, s] = tile_value(buffer, at + t, s, diagonal)

    by_diagonal(offs, slots, go)


def first_edge_kernel(scal, kept, u_ref, inner_v, v_out, edge_out):
    rows, slots = kept.shape[:2]
    offs = offsets(scal, slots)
    v_out[...] = inner_v[...]
    for base in edge_bases(rows, u_ref.shape[0] - rows):
        cover_block(offs, kept, u_ref, v_out, base, -1, base)
    write_edge(v_out, edge_out, rows)


def edge_kernel(scal, kept, mask, *refs):
    v_out, edge_out, u_out = refs[-3:]
    rows, slots = kept.shape[:2]
    offs = offsets(scal, slots)
    u_out[...] = scale_from(mask, refs[:-4])
    v_out[...] = jnp.zeros_like(v_out)
    for base in edge_bases(rows, mask.shape[0] - rows):
        cover_block(offs, kept, u_out, v_out, base, -1, base)
    write_edge(v_out, edge_out, rows)


def main_kernel(scal, kept, u_ref, edge_v, v_out):
    rows, slots = kept.shape[:2]
    offs = offsets(scal, slots)
    pad = edge_v.shape[0] - rows
    v_out[...] = edge_v[...]
    for base in range(pad, rows - pad, STEP):
        cover_block(offs, kept, u_ref, v_out, base, -1, base)


def first_main(scal, counts, mask, ext):
    rows, slots, tile = counts.shape[:3]
    outs = [jax.ShapeDtypeStruct((ext, tile), F32), pltpu.VMEM(counts.shape, F32)]
    return kernel_call(
        first_main_kernel,
        "first_main",
        scal,
        [counts, mask],
        outs,
        [pltpu.VMEM(counts.shape, counts.dtype), pltpu.SemaphoreType.DMA((rows // STEP,))],
        specs=[pl.BlockSpec(memory_space=pltpu.HBM), vmem()],
    )


def first_edge(scal, kept, u, inner_v):
    rows, tile = kept.shape[0], kept.shape[2]
    flat = jax.ShapeDtypeStruct(u.shape, F32)
    edge = jax.ShapeDtypeStruct((2 * (u.shape[0] - rows), tile), F32)
    return kernel_call(first_edge_kernel, "first_edge", scal, [kept, u, inner_v], [flat, edge])


def cover_edge(scal, kept, mask_ext, parts, after):
    rows, tile = kept.shape[0], kept.shape[2]
    flat = jax.ShapeDtypeStruct(mask_ext.shape, F32)
    edge = jax.ShapeDtypeStruct((2 * (mask_ext.shape[0] - rows), tile), F32)
    args = [kept, mask_ext, *parts, after]
    return kernel_call(edge_kernel, "cover_edge", scal, args, [flat, edge, flat])


def cover_main(scal, kept, u, edge_v):
    outs = [jax.ShapeDtypeStruct(u.shape, F32)]
    return kernel_call(main_kernel, "cover_main", scal, [kept, u, edge_v], outs)[0]


def ratio_kernel(start, count, pad, scal, kept, w_ref, h_ref, after, *refs):
    slots, tile = kept.shape[1:3]
    offs = offsets(scal, slots)
    if start == 0:
        hi_out, lo_out, same, h_terms = refs
        same[...] = after[...]
    else:
        hi_out, lo_out, h_terms = refs[-3:]

    def prepare(j, carry):
        hi, lo = split(h_ref[:, pl.ds(pl.multiple_of(j * tile, tile), tile)])
        h_terms[j - start] = jnp.concatenate([hi, lo, hi, lo], axis=0)
        return carry

    lax.fori_loop(start, start + count + pad, prepare, 0, unroll=4)

    def go(diagonal):
        def body(i, carry):
            hi, lo = split(w_ref[:, pl.ds(pl.multiple_of(i * tile, tile), tile)])
            w_terms = jnp.concatenate([hi, hi, lo, lo], axis=0)
            for s in range(slots):
                model = lax.dot_general(
                    w_terms, h_terms[i - start + offs[s]], TN, preferred_element_type=F32
                )
                values = kept[i, s]
                if s == diagonal:
                    values = values + values.T
                r_hi, r_lo = split(values * (1.0 / model))
                hi_out[i, :, s * tile : (s + 1) * tile] = r_hi
                lo_out[i, :, s * tile : (s + 1) * tile] = r_lo
            return carry

        lax.fori_loop(start, start + count, body, 0, unroll=4)

    by_diagonal(offs, slots, go)


def ratio(scal, kept, row_factors, col_ext, after, earlier, start, count):
    rows, slots, tile = kept.shape[:3]
    factors = row_factors.shape[0]
    pad = after.shape[0] - rows
    out = pltpu.VMEM((rows, tile, slots * tile), BF16)
    return kernel_call(
        functools.partial(ratio_kernel, start, count, pad),
        "ratio",
        scal,
        [kept, row_factors, col_ext, after, *earlier],
        [out, out] + [jax.ShapeDtypeStruct(after.shape, F32)] * (start == 0),
        [pltpu.VMEM((count + pad, 4 * factors, tile), BF16)],
        {5: 0, 6: 1} if earlier else {},
    )


def row_numer(offs, g_all, hi_ref, lo_ref, u_ref, i):
    slots = hi_ref.shape[2] // g_all.shape[2]
    factors = g_all.shape[1] // 2
    g = jnp.concatenate([g_all[i + offs[s]] for s in range(slots)], axis=1)
    big = lax.dot_general(g, hi_ref[i], NT, preferred_element_type=F32)
    small = lax.dot_general(g[:factors], lo_ref[i], NT, preferred_element_type=F32)
    return (big[:factors] + big[factors:] + small) * u_ref[pl.ds(i, 1), :]


def col_numer(w_ref, hi_ref, lo_ref, u_ref, i):
    tile = u_ref.shape[1]
    factors = w_ref.shape[0]
    w = w_ref[:, pl.ds(pl.multiple_of(i * tile, tile), tile)]
    hi, lo = split(w * u_ref[pl.ds(i, 1), :])
    big = jnp.dot(jnp.concatenate([hi, lo], axis=0), hi_ref[i], preferred_element_type=F32)
    small = jnp.dot(hi, lo_ref[i], preferred_element_type=F32)
    return big[:factors] + big[factors:] + small


def col_loop(offs, w_ref, hi_ref, lo_ref, u_ref, acc, start, count, shift):
    tile = u_ref.shape[1]

    def body(n, carry):
        i = start + n
        cols = col_numer(w_ref, hi_ref, lo_ref, u_ref, i)
        for s in range(hi_ref.shape[2] // tile):
            acc[i + offs[s] - shift] += cols[:, s * tile : (s + 1) * tile]
        return carry

    lax.fori_loop(0, count, body, 0, unroll=4)


def row_pieces(scal, offs, g_ref, hi_ref, lo_ref, u_ref, order, outs):
    for k, out in zip(order, outs):
        per = out.shape[0]
        first = jnp.bitwise_xor(scal[0], k) * per

        def body(t, carry):
            out[t] = row_numer(offs, g_ref, hi_ref, lo_ref, u_ref, first + t)
            return carry

        lax.fori_loop(0, per, body, 0, unroll=4)


def scaled_terms(h_ref, u_ref, terms, start, count):
    tile = u_ref.shape[1]
    factors = h_ref.shape[0]

    def fill(n, carry):
        j = start + n
        x = h_ref[:, pl.ds(pl.multiple_of(j * tile, tile), tile)] * u_ref[pl.ds(j, 1), :]
        hi, lo = split(x)
        terms[j, :factors] = hi
        terms[j, factors:] = lo
        return carry

    lax.fori_loop(0, count, fill, 0, unroll=4)


def numer_first_kernel(k, shares, scal, hi_ref, lo_ref, w_ref, h_ref, mask, *refs):
    parts = refs[:shares]
    u_out, tail_out, out, acc, terms = refs[shares:]
    rows = hi_ref.shape[0]
    ext, tile = mask.shape
    offs = offsets(scal, hi_ref.shape[2] // tile)
    per = rows // shares
    pad = ext - rows
    u_out[...] = scale_from(mask, parts)

    acc[...] = jnp.zeros_like(acc)
    col_loop(offs, w_ref, hi_ref, lo_ref, u_out, acc, rows - pad, pad, rows - pad)
    for t in range(pad):
        tail_out[t] = acc[pad + t] * u_out[rows + t : rows + t + 1, :]
    lane = lax.broadcasted_iota(jnp.int32, tail_out.shape[1:], 1)
    ends = jnp.zeros(tail_out.shape[1:], F32)
    for t in range(pad):
        ends = jnp.where(lane == t, tile_sum(w_ref, mask, rows - pad + t), ends)
    tail_out[pad] = ends

    first = jnp.bitwise_xor(scal[0], k) * per
    scaled_terms(h_ref, u_out, terms, first, per + pad)
    row_pieces(scal, offs, terms, hi_ref, lo_ref, u_out, [k], [out])


def numer_col_kernel(order, scal, hi_ref, lo_ref, w_ref, *refs):
    scales, refs = refs[: ITERS + 1], refs[ITERS + 1 :]
    sums_out, outs, acc = refs[0], refs[1:-1], refs[-1]
    u_ref = scales[-1]
    rows = hi_ref.shape[0]
    tile = u_ref.shape[1]
    offs = offsets(scal, hi_ref.shape[2] // tile)
    per = outs[0].shape[0]
    acc[...] = jnp.zeros_like(acc)
    col_loop(offs, w_ref, hi_ref, lo_ref, u_ref, acc, 0, rows, 0)
    for k, out in zip(order, outs):
        first = jnp.bitwise_xor(scal[0], k) * per

        def body(t, carry):
            out[t] = acc[first + t] * u_ref[pl.ds(first + t, 1), :]
            return carry

        lax.fori_loop(0, per, body, 0, unroll=4)
    write_sums(sums_out, scales, rows)


def write_sums(sums_out, scales, rows):
    sums_out[...] = jnp.zeros_like(sums_out)
    mask = scales[0][:rows]
    totals = [mask]
    for t in range(ITERS):
        below = jnp.where(mask > 0, scales[t + 1][:rows], 1.0)
        totals.append(jnp.where(mask > 0, scales[t][:rows] / below, 0.0))
    for t, total in enumerate(totals):
        line = jnp.sum(jnp.sum(total, axis=0, keepdims=True), axis=1, keepdims=True)
        sums_out[t : t + 1, :] = jnp.broadcast_to(line, (1, mask.shape[1]))


def numer_row_kernel(order, scal, hi_ref, lo_ref, h_ref, u_ref, after, *refs):
    outs, terms = refs[:-1], refs[-1]
    ext, tile = u_ref.shape
    offs = offsets(scal, hi_ref.shape[2] // tile)
    scaled_terms(h_ref, u_ref, terms, 0, ext)
    row_pieces(scal, offs, terms, hi_ref, lo_ref, u_ref, order, outs)


def numer_first(scal, r_hi, r_lo, row_factors, col_ext, mask_ext, parts, k):
    shares = len(parts)
    rows, tile = r_hi.shape[:2]
    factors = row_factors.shape[0]
    ext = mask_ext.shape[0]
    pad = ext - rows
    per = rows // shares
    return kernel_call(
        functools.partial(numer_first_kernel, k, shares),
        "numer_first",
        scal,
        [r_hi, r_lo, row_factors, col_ext, mask_ext, *parts],
        [
            jax.ShapeDtypeStruct((ext, tile), F32),
            jax.ShapeDtypeStruct((pad + 1, factors, tile), F32),
            jax.ShapeDtypeStruct((per, factors, tile), F32),
        ],
        [
            pltpu.VMEM((2 * pad, factors, tile), F32),
            pltpu.VMEM((ext, 2 * factors, tile), BF16),
        ],
    )


def numer_col(scal, r_hi, r_lo, row_factors, scales, order, shares):
    rows, tile = r_hi.shape[:2]
    factors = row_factors.shape[0]
    piece = jax.ShapeDtypeStruct((rows // shares, factors, tile), F32)
    res = kernel_call(
        functools.partial(numer_col_kernel, order),
        "numer_col",
        scal,
        [r_hi, r_lo, row_factors, *scales],
        [jax.ShapeDtypeStruct((8, tile), F32)] + [piece] * len(order),
        [pltpu.VMEM((scales[0].shape[0], factors, tile), F32)],
    )
    return res[0], res[1:]


def numer_row(scal, r_hi, r_lo, col_ext, u, after, order, shares):
    rows, tile = r_hi.shape[:2]
    factors = col_ext.shape[0]
    piece = jax.ShapeDtypeStruct((rows // shares, factors, tile), F32)
    return kernel_call(
        functools.partial(numer_row_kernel, order),
        "numer_row",
        scal,
        [r_hi, r_lo, col_ext, u, after],
        [piece] * len(order),
        [pltpu.VMEM((u.shape[0], 2 * factors, tile), BF16)],
    )


def mean_scale(sums):
    scale = sums[1:2, :] / sums[0:1, :]
    for t in range(1, ITERS):
        scale = scale * (sums[t + 1 : t + 2, :] / sums[0:1, :])
    return scale


def tile_sum(factor_ref, mask, j):
    tile = mask.shape[1]
    x = factor_ref[:, pl.ds(pl.multiple_of(j * tile, tile), tile)] * mask[pl.ds(j, 1), :]
    return jnp.sum(x, axis=1, keepdims=True)


def windows(sums, per):
    return [tree_sum(sums[t : t + len(sums) - per]) for t in range(per)]


def write_coefficient(old_ref, mask, first, lowers, times_out, plus_out):
    tile = mask.shape[1]
    for t, lower in enumerate(lowers):
        live = mask[pl.ds(first + t, 1), :]
        old = old_ref[:, t * tile : (t + 1) * tile]
        times_out[t] = jnp.where(live > 0, old / jnp.where(live > 0, lower * live, 1.0), 0.0)
        plus_out[t] = jnp.where(live > 0, 0.0, old)


def row_coefficient_kernel(pad, scal, old_ref, mask, other, times_out, plus_out):
    per = times_out.shape[0]
    first = scal[0] * per
    sums = [tile_sum(other, mask, first + t) for t in range(per + pad)]
    write_coefficient(old_ref, mask, first, windows(sums, per), times_out, plus_out)


def col_coefficient_kernel(pad, scal, old_ref, mask, other, ends, times_out, plus_out):
    per = times_out.shape[0]
    first = scal[0] * per
    sums = []
    for j in range(1, per + pad):
        total = tile_sum(other, mask, jnp.maximum(first - pad + j, 0))
        for start in range(0, pad, per):
            if start + j < pad:
                before = jnp.where(scal[scal.shape[0] - 1] > 0, ends[:, start + j : start + j + 1], 0.0)
                total = jnp.where(first == start, before, total)
        sums.append(total)
    sums.append(jnp.zeros_like(sums[0]))
    write_coefficient(old_ref, mask, first, windows(sums, per), times_out, plus_out)


def coefficient(kernel, scal, shares, old, mask_ext, other, *ends):
    factors = old.shape[0]
    tile = mask_ext.shape[1]
    rows = old.shape[1] // tile
    per = rows // shares
    specs = [pl.BlockSpec((factors, per * tile), lambda i, scal: (0, scal[0]))]
    specs += [vmem() for _ in range(2 + len(ends))]
    return kernel_call(
        functools.partial(kernel, mask_ext.shape[0] - rows),
        "coefficient",
        scal,
        [old, mask_ext, other, *ends],
        [jax.ShapeDtypeStruct((per, factors, tile), F32)] * 2,
        specs=specs,
    )


def update_kernel(scal, sums, times, plus, *refs):
    terms, out = refs[:-1], refs[-1]
    per, _, tile = times.shape
    c = mean_scale(sums[...])
    for t in range(per):
        numer = terms[0][t]
        for term in terms[1:]:
            numer = numer + term[t]
        out[:, t * tile : (t + 1) * tile] = times[t] * (numer * c * c) + plus[t]


def update(scal, sums, times, plus, terms):
    per, count, tile = terms[0].shape
    return kernel_call(
        update_kernel,
        "update",
        scal,
        [sums, times, plus, *terms],
        [jax.ShapeDtypeStruct((count, per * tile), F32)],
    )[0]


def xor_exchange(x, axis, k):
    return lax.ppermute(x, axis, [(i, i ^ k) for i in range(lax.axis_size(axis))])


def both_sides(x, even):
    size = lax.axis_size("genome")
    a = lax.ppermute(x, "genome", [(i, i ^ 1) for i in range(size)])
    b = lax.ppermute(x, "genome", [(i, (((i + 1) ^ 1) - 1) % size) for i in range(size)])
    return jnp.where(even > 0, a, b), jnp.where(even > 0, b, a)


def scatter_terms(pieces):
    size = lax.axis_size("offset")
    if size == 4:
        far = pieces[3] + xor_exchange(pieces[2], "offset", 1)
        far = xor_exchange(far, "offset", 3)
        return [pieces[0], xor_exchange(pieces[1], "offset", 1), far]
    return [pieces[0]] + [xor_exchange(pieces[k], "offset", k) for k in range(1, size)]


def per_device(counts, band_offset, bin_mask, row_factors, col_factors):
    rows, slots, tile = counts.shape[:3]
    factors = row_factors.shape[0]
    offset_count = lax.axis_size("offset")
    genome_count = lax.axis_size("genome")
    g = lax.axis_index("genome")
    o = lax.axis_index("offset").astype(jnp.int32)
    reach = slots * offset_count - 1
    pad = reach + 1

    line = jnp.broadcast_to(g, (1, tile))
    even = (line % 2 == 0).astype(F32)
    has_next = (line < genome_count - 1).astype(F32)
    has_prev = (line > 0).astype(F32)
    count = offset_count * -(-pad * offset_count // rows)
    index = lax.broadcasted_iota(jnp.int32, (count, tile), 0)
    share, k = index // offset_count, index % offset_count
    mine = (jnp.bitwise_xor(share, k) == o).astype(F32) * has_prev
    flags = jnp.concatenate([even, has_next, has_prev, mine])
    before = jnp.broadcast_to((g > 0).astype(jnp.int32), (1,))
    scal = jnp.concatenate([jnp.broadcast_to(o, (1,)), band_offset, before])
    flags, scal, bin_mask = lax.optimization_barrier((flags, scal, bin_mask))
    even, has_next, has_prev = flags[0:1], flags[1:2], flags[2:3]
    mine = flags[3:]

    mask = bin_mask.astype(F32).reshape(rows, tile)
    mask_next, _ = both_sides(mask[:pad], even)
    keep = lax.broadcasted_iota(jnp.int32, (pad, 1), 0) < reach
    mask_ext = jnp.concatenate([mask, jnp.where(keep, mask_next * has_next, 0.0)])

    counts = pltpu.with_memory_space_constraint(counts, pltpu.HBM)
    inner_v, kept = first_main(scal, counts, mask, rows + pad)

    scales = []
    quarter = rows // (ITERS + 1)
    for t in range(ITERS):
        if t == 0:
            u = mask_ext
            v, edge = first_edge(scal, kept, u, inner_v)
        else:
            v, edge, u = cover_edge(scal, kept, mask_ext, parts, ratios[0])
        scales.append(u)
        after, before = both_sides(edge, even)
        if t > 0:
            v = cover_main(scal, kept, u, v)
        else:
            *ratios, v = ratio(scal, kept, row_factors, col_factors, v, [], 0, 2 * quarter)
        front = v[:pad] + before[pad:] * has_prev
        back = v[rows:] + after[:pad] * has_next
        x = jnp.concatenate([front, v[pad:rows], back])
        others = {k: xor_exchange(x, "offset", k) for k in reversed(range(1, offset_count))}
        parts = [x, *others.values()]
        if t == 0:
            col_late, _ = lax.optimization_barrier((col_factors, x))
            ring_left = [(i, (i - 1) % genome_count) for i in range(genome_count)]
            col_next = lax.ppermute(col_late[:, : pad * tile], "genome", ring_left)
            col_next = jnp.where(has_next[:, :1] > 0, col_next, 1.0)
            col_ext = jnp.concatenate([col_factors, col_next], axis=1)
        else:
            columns = col_ext if t == ITERS - 1 else col_factors
            start = (t + 1) * quarter
            ratios = ratio(scal, kept, row_factors, columns, x, ratios, start, quarter)

    r_hi, r_lo = ratios
    per = rows // offset_count
    u, tail, early = numer_first(
        scal, r_hi, r_lo, row_factors, col_ext, mask_ext, parts, EARLY
    )
    scales.append(u)
    order = [EARLY, *(k for k in range(offset_count) if k != EARLY)]
    sums, pieces = numer_col(scal, r_hi, r_lo, row_factors, scales, order, offset_count)
    h_parts = dict(zip(order, pieces))

    right = [(i, (i + 1) % genome_count) for i in range(genome_count)]
    arrived = lax.ppermute(tail, "genome", right)
    for s in range(-(-pad // per)):
        piece = arrived[s * per : min(pad, (s + 1) * per)]
        for k in range(offset_count):
            at = s * offset_count + k
            h_parts[k] = h_parts[k].at[: piece.shape[0]].add(piece * mine[at : at + 1])

    row_terms = coefficient(
        row_coefficient_kernel, scal, offset_count, row_factors, mask_ext, col_ext
    )
    col_terms = coefficient(
        col_coefficient_kernel, scal, offset_count, col_factors, mask_ext, row_factors, arrived[pad]
    )
    order = [k for k in (3, 1, 0, *range(4, offset_count))]
    pieces = numer_row(scal, r_hi, r_lo, col_ext, u, h_parts[EARLY], order, offset_count)
    w_parts = dict(zip(order, pieces)) | {EARLY: early}
    w_terms = scatter_terms([w_parts[k] for k in range(offset_count)])
    h_terms = scatter_terms([h_parts[k] for k in range(offset_count)])

    sums, _ = lax.optimization_barrier((sums, w_terms[2]))
    sums = jnp.sum(lax.all_gather(sums, "genome"), axis=0)
    bias = (u[:rows] * mean_scale(sums)).reshape(-1)

    col_update = update(scal, sums, *col_terms, h_terms)
    row_update = update(scal, sums, *row_terms, w_terms)
    return bias, row_update, col_update


def solution(mesh):
    return jax.shard_map(
        per_device,
        mesh=mesh,
        in_specs=(
            P("genome", "offset", None, None),
            P("offset"),
            P("genome"),
            P(None, "genome"),
            P(None, "genome"),
        ),
        out_specs=(P("genome"), P(None, ("genome", "offset")), P(None, ("genome", "offset"))),
        check_vma=False,
    )
```

```python
import functools

import jax
import jax.numpy as jnp
from jax import lax
from jax.experimental import pallas as pl
from jax.experimental.pallas import tpu as pltpu
from jax.sharding import PartitionSpec as P

ITERS = 3
STEP = 8
EARLY = 2
F32 = jnp.float32
BF16 = jnp.bfloat16
VMEM_LIMIT = 20 * 1024 * 1024
NT = (((1,), (1,)), ((), ()))
TN = (((0,), (0,)), ((), ()))


def split(x):
    hi = x.astype(BF16)
    lo = (x - hi.astype(F32)).astype(BF16)
    return hi, lo


def tree_sum(parts):
    while len(parts) > 1:
        parts = [a + b for a, b in zip(parts[::2], parts[1::2])]
    return parts[0]


def params():
    return pltpu.CompilerParams(vmem_limit_bytes=VMEM_LIMIT)


def scale_from(mask, parts):
    cover = tree_sum([p[...] for p in parts[:1] + parts[:0:-1]])
    live = mask[...] > 0
    return jnp.where(live, 1.0 / jnp.where(live, cover, 1.0), 0.0)


def vmem():
    return pl.BlockSpec(memory_space=pltpu.VMEM)


def kernel_call(body, name, scalars, args, outs, scratch=(), aliases=None, specs=None):
    return pl.pallas_call(
        body,
        grid_spec=pltpu.PrefetchScalarGridSpec(
            num_scalar_prefetch=1,
            grid=(1,),
            in_specs=specs or [vmem() for _ in args],
            out_specs=[vmem() for _ in outs],
            scratch_shapes=list(scratch),
        ),
        out_shape=outs,
        input_output_aliases=aliases or {},
        compiler_params=params(),
        name=name,
    )(scalars, *args)


def offsets(scal, slots):
    return [scal[1 + s] for s in range(slots)]


def by_diagonal(offs, slots, go):
    for s in range(slots):

        @pl.when(offs[s] == 0)
        def _():
            go(s)

    @pl.when(functools.reduce(jnp.logical_and, [offs[s] != 0 for s in range(slots)]))
    def _():
        go(-1)


def tile_value(counts, i, s, diagonal):
    c = counts[i, s].astype(F32)
    if s == diagonal:
        tile = c.shape[0]
        r = lax.broadcasted_iota(jnp.int32, (tile, tile), 0)
        q = lax.broadcasted_iota(jnp.int32, (tile, tile), 1)
        c = jnp.where(r < q, c, jnp.where(r == q, 0.5 * c, 0.0))
    return c


def cover_block(offs, counts, u_ref, acc, base, diagonal, at, kept=None):
    slots, tile = counts.shape[1:3]
    ones = jnp.ones((8, tile), BF16)
    u_block = u_ref[pl.ds(base, STEP), :]
    u_cols = u_block.T
    u_across = [u_ref[pl.ds(base + offs[s], STEP), :] for s in range(slots)]
    cols = [[] for _ in range(slots)]
    sums = []
    for t in range(STEP):
        total = None
        for s in range(slots):
            c = tile_value(counts, at + t, s, diagonal)
            if kept is not None:
                kept[base + t, s] = c
            term = c * u_across[s][t : t + 1]
            total = term if total is None else total + term
            cols[s].append(jnp.sum(c * u_cols[:, t : t + 1], axis=0, keepdims=True))
        hi, lo = split(total)
        row = lax.dot_general(ones, hi, NT, preferred_element_type=F32)
        row = row + lax.dot_general(ones, lo, NT, preferred_element_type=F32)
        sums.append(row[:1])
    acc[pl.ds(base, STEP), :] += jnp.concatenate(sums, axis=0)
    for s in range(slots):
        acc[pl.ds(base + offs[s], STEP), :] += jnp.concatenate(cols[s], axis=0)


def block_copies(hbm, buffer, sems, bases):
    return [
        pltpu.make_async_copy(
            hbm.at[pl.ds(base, STEP)], buffer.at[pl.ds(k * STEP, STEP)], sems.at[k]
        )
        for k, base in enumerate(bases)
    ]


def edge_bases(rows, pad):
    return list(range(0, pad, STEP)) + list(range(rows - pad, rows, STEP))


def write_edge(v_out, edge_out, rows):
    pad = v_out.shape[0] - rows
    edge_out[:pad] = v_out[:pad]
    edge_out[pad:] = v_out[rows:]


def first_main_kernel(scal, hbm, mask, v_out, kept, buffer, sems):
    rows, slots = hbm.shape[:2]
    offs = offsets(scal, slots)
    pad = v_out.shape[0] - rows
    inner = list(range(pad, rows - pad, STEP))
    bases = inner + edge_bases(rows, pad)
    copies = block_copies(hbm, buffer, sems, bases)
    for copy in copies:
        copy.start()
    v_out[...] = jnp.zeros_like(v_out)

    def go(diagonal):
        for k, base in enumerate(bases):
            copies[k].wait()
            at = k * STEP
            if base in inner:
                cover_block(offs, buffer, mask, v_out, base, diagonal, at, kept)
            else:
                for t in range(STEP):
                    for s in range(slots):
                        kept[base + t, s] = tile_value(buffer, at + t, s, diagonal)

    by_diagonal(offs, slots, go)


def first_edge_kernel(scal, kept, u_ref, inner_v, v_out, edge_out):
    rows, slots = kept.shape[:2]
    offs = offsets(scal, slots)
    v_out[...] = inner_v[...]
    for base in edge_bases(rows, u_ref.shape[0] - rows):
        cover_block(offs, kept, u_ref, v_out, base, -1, base)
    write_edge(v_out, edge_out, rows)


def edge_kernel(scal, kept, mask, *refs):
    v_out, edge_out, u_out = refs[-3:]
    rows, slots = kept.shape[:2]
    offs = offsets(scal, slots)
    u_out[...] = scale_from(mask, refs[:-4])
    v_out[...] = jnp.zeros_like(v_out)
    for base in edge_bases(rows, mask.shape[0] - rows):
        cover_block(offs, kept, u_out, v_out, base, -1, base)
    write_edge(v_out, edge_out, rows)


def main_kernel(scal, kept, u_ref, edge_v, v_out):
    rows, slots = kept.shape[:2]
    offs = offsets(scal, slots)
    pad = edge_v.shape[0] - rows
    v_out[...] = edge_v[...]
    for base in range(pad, rows - pad, STEP):
        cover_block(offs, kept, u_ref, v_out, base, -1, base)


def first_main(scal, counts, mask, ext):
    rows, slots, tile = counts.shape[:3]
    outs = [jax.ShapeDtypeStruct((ext, tile), F32), pltpu.VMEM(counts.shape, F32)]
    return kernel_call(
        first_main_kernel,
        "first_main",
        scal,
        [counts, mask],
        outs,
        [pltpu.VMEM(counts.shape, counts.dtype), pltpu.SemaphoreType.DMA((rows // STEP,))],
        specs=[pl.BlockSpec(memory_space=pltpu.HBM), vmem()],
    )


def first_edge(scal, kept, u, inner_v):
    rows, tile = kept.shape[0], kept.shape[2]
    flat = jax.ShapeDtypeStruct(u.shape, F32)
    edge = jax.ShapeDtypeStruct((2 * (u.shape[0] - rows), tile), F32)
    return kernel_call(first_edge_kernel, "first_edge", scal, [kept, u, inner_v], [flat, edge])


def cover_edge(scal, kept, mask_ext, parts, after):
    rows, tile = kept.shape[0], kept.shape[2]
    flat = jax.ShapeDtypeStruct(mask_ext.shape, F32)
    edge = jax.ShapeDtypeStruct((2 * (mask_ext.shape[0] - rows), tile), F32)
    args = [kept, mask_ext, *parts, after]
    return kernel_call(edge_kernel, "cover_edge", scal, args, [flat, edge, flat])


def cover_main(scal, kept, u, edge_v):
    outs = [jax.ShapeDtypeStruct(u.shape, F32)]
    return kernel_call(main_kernel, "cover_main", scal, [kept, u, edge_v], outs)[0]


def ratio_kernel(start, count, pad, scal, kept, w_ref, h_ref, after, *refs):
    slots, tile = kept.shape[1:3]
    offs = offsets(scal, slots)
    if start == 0:
        hi_out, lo_out, same, h_terms = refs
        same[...] = after[...]
    else:
        hi_out, lo_out, h_terms = refs[-3:]

    def prepare(j, carry):
        hi, lo = split(h_ref[:, pl.ds(pl.multiple_of(j * tile, tile), tile)])
        h_terms[j - start] = jnp.concatenate([hi, lo, hi, lo], axis=0)
        return carry

    lax.fori_loop(start, start + count + pad, prepare, 0, unroll=4)

    def go(diagonal):
        def body(i, carry):
            hi, lo = split(w_ref[:, pl.ds(pl.multiple_of(i * tile, tile), tile)])
            w_terms = jnp.concatenate([hi, hi, lo, lo], axis=0)
            for s in range(slots):
                model = lax.dot_general(
                    w_terms, h_terms[i - start + offs[s]], TN, preferred_element_type=F32
                )
                values = kept[i, s]
                if s == diagonal:
                    values = values + values.T
                r_hi, r_lo = split(values * (1.0 / model))
                hi_out[i, :, s * tile : (s + 1) * tile] = r_hi
                lo_out[i, :, s * tile : (s + 1) * tile] = r_lo
            return carry

        lax.fori_loop(start, start + count, body, 0, unroll=4)

    by_diagonal(offs, slots, go)


def ratio(scal, kept, row_factors, col_ext, after, earlier, start, count):
    rows, slots, tile = kept.shape[:3]
    factors = row_factors.shape[0]
    pad = after.shape[0] - rows
    out = pltpu.VMEM((rows, tile, slots * tile), BF16)
    return kernel_call(
        functools.partial(ratio_kernel, start, count, pad),
        "ratio",
        scal,
        [kept, row_factors, col_ext, after, *earlier],
        [out, out] + [jax.ShapeDtypeStruct(after.shape, F32)] * (start == 0),
        [pltpu.VMEM((count + pad, 4 * factors, tile), BF16)],
        {5: 0, 6: 1} if earlier else {},
    )


def row_numer(offs, g_all, hi_ref, lo_ref, u_ref, i):
    slots = hi_ref.shape[2] // g_all.shape[2]
    factors = g_all.shape[1] // 2
    g = jnp.concatenate([g_all[i + offs[s]] for s in range(slots)], axis=1)
    big = lax.dot_general(g, hi_ref[i], NT, preferred_element_type=F32)
    small = lax.dot_general(g[:factors], lo_ref[i], NT, preferred_element_type=F32)
    return (big[:factors] + big[factors:] + small) * u_ref[pl.ds(i, 1), :]


def col_numer(w_ref, hi_ref, lo_ref, u_ref, i):
    tile = u_ref.shape[1]
    factors = w_ref.shape[0]
    w = w_ref[:, pl.ds(pl.multiple_of(i * tile, tile), tile)]
    hi, lo = split(w * u_ref[pl.ds(i, 1), :])
    big = jnp.dot(jnp.concatenate([hi, lo], axis=0), hi_ref[i], preferred_element_type=F32)
    small = jnp.dot(hi, lo_ref[i], preferred_element_type=F32)
    return big[:factors] + big[factors:] + small


def col_loop(offs, w_ref, hi_ref, lo_ref, u_ref, acc, start, count, shift):
    tile = u_ref.shape[1]

    def body(n, carry):
        i = start + n
        cols = col_numer(w_ref, hi_ref, lo_ref, u_ref, i)
        for s in range(hi_ref.shape[2] // tile):
            acc[i + offs[s] - shift] += cols[:, s * tile : (s + 1) * tile]
        return carry

    lax.fori_loop(0, count, body, 0, unroll=4)


def row_pieces(scal, offs, g_ref, hi_ref, lo_ref, u_ref, order, outs):
    for k, out in zip(order, outs):
        per = out.shape[0]
        first = jnp.bitwise_xor(scal[0], k) * per

        def body(t, carry):
            out[t] = row_numer(offs, g_ref, hi_ref, lo_ref, u_ref, first + t)
            return carry

        lax.fori_loop(0, per, body, 0, unroll=4)


def scaled_terms(h_ref, u_ref, terms, start, count):
    tile = u_ref.shape[1]
    factors = h_ref.shape[0]

    def fill(n, carry):
        j = start + n
        x = h_ref[:, pl.ds(pl.multiple_of(j * tile, tile), tile)] * u_ref[pl.ds(j, 1), :]
        hi, lo = split(x)
        terms[j, :factors] = hi
        terms[j, factors:] = lo
        return carry

    lax.fori_loop(0, count, fill, 0, unroll=4)


def numer_first_kernel(k, shares, scal, hi_ref, lo_ref, w_ref, h_ref, mask, *refs):
    parts = refs[:shares]
    u_out, tail_out, out, acc, terms = refs[shares:]
    rows = hi_ref.shape[0]
    ext, tile = mask.shape
    offs = offsets(scal, hi_ref.shape[2] // tile)
    per = rows // shares
    pad = ext - rows
    u_out[...] = scale_from(mask, parts)

    acc[...] = jnp.zeros_like(acc)
    col_loop(offs, w_ref, hi_ref, lo_ref, u_out, acc, rows - pad, pad, rows - pad)
    for t in range(pad):
        tail_out[t] = acc[pad + t] * u_out[rows + t : rows + t + 1, :]
    lane = lax.broadcasted_iota(jnp.int32, tail_out.shape[1:], 1)
    ends = jnp.zeros(tail_out.shape[1:], F32)
    for t in range(pad):
        ends = jnp.where(lane == t, tile_sum(w_ref, mask, rows - pad + t), ends)
    tail_out[pad] = ends

    first = jnp.bitwise_xor(scal[0], k) * per
    scaled_terms(h_ref, u_out, terms, first, per + pad)
    row_pieces(scal, offs, terms, hi_ref, lo_ref, u_out, [k], [out])


def numer_col_kernel(order, scal, hi_ref, lo_ref, w_ref, *refs):
    scales, refs = refs[: ITERS + 1], refs[ITERS + 1 :]
    sums_out, outs, acc = refs[0], refs[1:-1], refs[-1]
    u_ref = scales[-1]
    rows = hi_ref.shape[0]
    tile = u_ref.shape[1]
    offs = offsets(scal, hi_ref.shape[2] // tile)
    per = outs[0].shape[0]
    acc[...] = jnp.zeros_like(acc)
    col_loop(offs, w_ref, hi_ref, lo_ref, u_ref, acc, 0, rows, 0)
    for k, out in zip(order, outs):
        first = jnp.bitwise_xor(scal[0], k) * per

        def body(t, carry):
            out[t] = acc[first + t] * u_ref[pl.ds(first + t, 1), :]
            return carry

        lax.fori_loop(0, per, body, 0, unroll=4)
    write_sums(sums_out, scales, rows)


def write_sums(sums_out, scales, rows):
    sums_out[...] = jnp.zeros_like(sums_out)
    mask = scales[0][:rows]
    totals = [mask]
    for t in range(ITERS):
        below = jnp.where(mask > 0, scales[t + 1][:rows], 1.0)
        totals.append(jnp.where(mask > 0, scales[t][:rows] / below, 0.0))
    for t, total in enumerate(totals):
        line = jnp.sum(jnp.sum(total, axis=0, keepdims=True), axis=1, keepdims=True)
        sums_out[t : t + 1, :] = jnp.broadcast_to(line, (1, mask.shape[1]))


def numer_row_kernel(order, scal, hi_ref, lo_ref, h_ref, u_ref, after, *refs):
    outs, terms = refs[:-1], refs[-1]
    ext, tile = u_ref.shape
    offs = offsets(scal, hi_ref.shape[2] // tile)
    scaled_terms(h_ref, u_ref, terms, 0, ext)
    row_pieces(scal, offs, terms, hi_ref, lo_ref, u_ref, order, outs)


def numer_first(scal, r_hi, r_lo, row_factors, col_ext, mask_ext, parts, k):
    shares = len(parts)
    rows, tile = r_hi.shape[:2]
    factors = row_factors.shape[0]
    ext = mask_ext.shape[0]
    pad = ext - rows
    per = rows // shares
    return kernel_call(
        functools.partial(numer_first_kernel, k, shares),
        "numer_first",
        scal,
        [r_hi, r_lo, row_factors, col_ext, mask_ext, *parts],
        [
            jax.ShapeDtypeStruct((ext, tile), F32),
            jax.ShapeDtypeStruct((pad + 1, factors, tile), F32),
            jax.ShapeDtypeStruct((per, factors, tile), F32),
        ],
        [
            pltpu.VMEM((2 * pad, factors, tile), F32),
            pltpu.VMEM((ext, 2 * factors, tile), BF16),
        ],
    )


def numer_col(scal, r_hi, r_lo, row_factors, scales, order, shares):
    rows, tile = r_hi.shape[:2]
    factors = row_factors.shape[0]
    piece = jax.ShapeDtypeStruct((rows // shares, factors, tile), F32)
    res = kernel_call(
        functools.partial(numer_col_kernel, order),
        "numer_col",
        scal,
        [r_hi, r_lo, row_factors, *scales],
        [jax.ShapeDtypeStruct((8, tile), F32)] + [piece] * len(order),
        [pltpu.VMEM((scales[0].shape[0], factors, tile), F32)],
    )
    return res[0], res[1:]


def numer_row(scal, r_hi, r_lo, col_ext, u, after, order, shares):
    rows, tile = r_hi.shape[:2]
    factors = col_ext.shape[0]
    piece = jax.ShapeDtypeStruct((rows // shares, factors, tile), F32)
    return kernel_call(
        functools.partial(numer_row_kernel, order),
        "numer_row",
        scal,
        [r_hi, r_lo, col_ext, u, after],
        [piece] * len(order),
        [pltpu.VMEM((u.shape[0], 2 * factors, tile), BF16)],
    )


def mean_scale(sums):
    scale = sums[1:2, :] / sums[0:1, :]
    for t in range(1, ITERS):
        scale = scale * (sums[t + 1 : t + 2, :] / sums[0:1, :])
    return scale


def tile_sum(factor_ref, mask, j):
    tile = mask.shape[1]
    x = factor_ref[:, pl.ds(pl.multiple_of(j * tile, tile), tile)] * mask[pl.ds(j, 1), :]
    return jnp.sum(x, axis=1, keepdims=True)


def windows(sums, per):
    return [tree_sum(sums[t : t + len(sums) - per]) for t in range(per)]


def write_coefficient(old_ref, mask, first, lowers, times_out, plus_out):
    tile = mask.shape[1]
    for t, lower in enumerate(lowers):
        live = mask[pl.ds(first + t, 1), :]
        old = old_ref[:, t * tile : (t + 1) * tile]
        times_out[t] = jnp.where(live > 0, old / jnp.where(live > 0, lower * live, 1.0), 0.0)
        plus_out[t] = jnp.where(live > 0, 0.0, old)


def row_coefficient_kernel(pad, scal, old_ref, mask, other, times_out, plus_out):
    per = times_out.shape[0]
    first = scal[0] * per
    sums = [tile_sum(other, mask, first + t) for t in range(per + pad)]
    write_coefficient(old_ref, mask, first, windows(sums, per), times_out, plus_out)


def col_coefficient_kernel(pad, scal, old_ref, mask, other, ends, times_out, plus_out):
    per = times_out.shape[0]
    first = scal[0] * per
    sums = []
    for j in range(1, per + pad):
        total = tile_sum(other, mask, jnp.maximum(first - pad + j, 0))
        for start in range(0, pad, per):
            if start + j < pad:
                before = jnp.where(scal[scal.shape[0] - 1] > 0, ends[:, start + j : start + j + 1], 0.0)
                total = jnp.where(first == start, before, total)
        sums.append(total)
    sums.append(jnp.zeros_like(sums[0]))
    write_coefficient(old_ref, mask, first, windows(sums, per), times_out, plus_out)


def coefficient(kernel, scal, shares, old, mask_ext, other, *ends):
    factors = old.shape[0]
    tile = mask_ext.shape[1]
    rows = old.shape[1] // tile
    per = rows // shares
    specs = [pl.BlockSpec((factors, per * tile), lambda i, scal: (0, scal[0]))]
    specs += [vmem() for _ in range(2 + len(ends))]
    return kernel_call(
        functools.partial(kernel, mask_ext.shape[0] - rows),
        "coefficient",
        scal,
        [old, mask_ext, other, *ends],
        [jax.ShapeDtypeStruct((per, factors, tile), F32)] * 2,
        specs=specs,
    )


def update_kernel(scal, sums, times, plus, *refs):
    terms, out = refs[:-1], refs[-1]
    per, _, tile = times.shape
    c = mean_scale(sums[...])
    for t in range(per):
        numer = terms[0][t]
        for term in terms[1:]:
            numer = numer + term[t]
        out[:, t * tile : (t + 1) * tile] = times[t] * (numer * c * c) + plus[t]


def update(scal, sums, times, plus, terms):
    per, count, tile = terms[0].shape
    return kernel_call(
        update_kernel,
        "update",
        scal,
        [sums, times, plus, *terms],
        [jax.ShapeDtypeStruct((count, per * tile), F32)],
    )[0]


def xor_exchange(x, axis, k):
    return lax.ppermute(x, axis, [(i, i ^ k) for i in range(lax.axis_size(axis))])


def both_sides(x, even):
    size = lax.axis_size("genome")
    a = lax.ppermute(x, "genome", [(i, i ^ 1) for i in range(size)])
    b = lax.ppermute(x, "genome", [(i, (((i + 1) ^ 1) - 1) % size) for i in range(size)])
    return jnp.where(even > 0, a, b), jnp.where(even > 0, b, a)


def scatter_terms(pieces):
    size = lax.axis_size("offset")
    if size == 4:
        far = pieces[3] + xor_exchange(pieces[2], "offset", 1)
        far = xor_exchange(far, "offset", 3)
        return [pieces[0], xor_exchange(pieces[1], "offset", 1), far]
    return [pieces[0]] + [xor_exchange(pieces[k], "offset", k) for k in range(1, size)]


def per_device(counts, band_offset, bin_mask, row_factors, col_factors):
    rows, slots, tile = counts.shape[:3]
    factors = row_factors.shape[0]
    offset_count = lax.axis_size("offset")
    genome_count = lax.axis_size("genome")
    g = lax.axis_index("genome")
    o = lax.axis_index("offset").astype(jnp.int32)
    reach = slots * offset_count - 1
    pad = reach + 1

    line = jnp.broadcast_to(g, (1, tile))
    even = (line % 2 == 0).astype(F32)
    has_next = (line < genome_count - 1).astype(F32)
    has_prev = (line > 0).astype(F32)
    count = offset_count * -(-pad * offset_count // rows)
    index = lax.broadcasted_iota(jnp.int32, (count, tile), 0)
    share, k = index // offset_count, index % offset_count
    mine = (jnp.bitwise_xor(share, k) == o).astype(F32) * has_prev
    flags = jnp.concatenate([even, has_next, has_prev, mine])
    before = jnp.broadcast_to((g > 0).astype(jnp.int32), (1,))
    scal = jnp.concatenate([jnp.broadcast_to(o, (1,)), band_offset, before])
    flags, scal, bin_mask = lax.optimization_barrier((flags, scal, bin_mask))
    even, has_next, has_prev = flags[0:1], flags[1:2], flags[2:3]
    mine = flags[3:]

    mask = bin_mask.astype(F32).reshape(rows, tile)
    mask_next, _ = both_sides(mask[:pad], even)
    keep = lax.broadcasted_iota(jnp.int32, (pad, 1), 0) < reach
    mask_ext = jnp.concatenate([mask, jnp.where(keep, mask_next * has_next, 0.0)])

    counts = pltpu.with_memory_space_constraint(counts, pltpu.HBM)
    inner_v, kept = first_main(scal, counts, mask, rows + pad)
    col_late, _ = lax.optimization_barrier((col_factors, inner_v))
    ring_left = [(i, (i - 1) % genome_count) for i in range(genome_count)]
    col_next = lax.ppermute(col_late[:, : pad * tile], "genome", ring_left)
    col_ext = jnp.concatenate([col_factors, col_next], axis=1)

    scales = []
    quarter = rows // (ITERS + 1)
    for t in range(ITERS):
        if t == 0:
            u = mask_ext
            v, edge = first_edge(scal, kept, u, inner_v)
        else:
            v, edge, u = cover_edge(scal, kept, mask_ext, parts, ratios[0])
        scales.append(u)
        after, before = both_sides(edge, even)
        if t > 0:
            v = cover_main(scal, kept, u, v)
        else:
            *ratios, v = ratio(scal, kept, row_factors, col_factors, v, [], 0, 2 * quarter)
        front = v[:pad] + before[pad:] * has_prev
        back = v[rows:] + after[:pad] * has_next
        x = jnp.concatenate([front, v[pad:rows], back])
        others = {k: xor_exchange(x, "offset", k) for k in reversed(range(1, offset_count))}
        parts = [x, *others.values()]
        if t == 0:
            ratios = ratio(scal, kept, row_factors, col_factors, x, ratios, 2 * quarter, quarter)
        elif t == ITERS - 1:
            ratios = ratio(scal, kept, row_factors, col_ext, x, ratios, 3 * quarter, quarter)

    r_hi, r_lo = ratios
    per = rows // offset_count
    u, tail, early = numer_first(
        scal, r_hi, r_lo, row_factors, col_ext, mask_ext, parts, EARLY
    )
    scales.append(u)
    order = [EARLY, *(k for k in range(offset_count) if k != EARLY)]
    sums, pieces = numer_col(scal, r_hi, r_lo, row_factors, scales, order, offset_count)
    h_parts = dict(zip(order, pieces))

    right = [(i, (i + 1) % genome_count) for i in range(genome_count)]
    arrived = lax.ppermute(tail, "genome", right)
    for s in range(-(-pad // per)):
        piece = arrived[s * per : min(pad, (s + 1) * per)]
        for k in range(offset_count):
            at = s * offset_count + k
            h_parts[k] = h_parts[k].at[: piece.shape[0]].add(piece * mine[at : at + 1])

    row_terms = coefficient(
        row_coefficient_kernel, scal, offset_count, row_factors, mask_ext, col_ext
    )
    col_terms = coefficient(
        col_coefficient_kernel, scal, offset_count, col_factors, mask_ext, row_factors, arrived[pad]
    )
    order = [k for k in (3, 1, 0, *range(4, offset_count))]
    pieces = numer_row(scal, r_hi, r_lo, col_ext, u, h_parts[EARLY], order, offset_count)
    w_parts = dict(zip(order, pieces)) | {EARLY: early}
    w_terms = scatter_terms([w_parts[k] for k in range(offset_count)])
    h_terms = scatter_terms([h_parts[k] for k in range(offset_count)])

    sums, _ = lax.optimization_barrier((sums, w_terms[2]))
    sums = jnp.sum(lax.all_gather(sums, "genome"), axis=0)
    bias = (u[:rows] * mean_scale(sums)).reshape(-1)

    col_update = update(scal, sums, *col_terms, h_terms)
    row_update = update(scal, sums, *row_terms, w_terms)
    return bias, row_update, col_update


def solution(mesh):
    return jax.shard_map(
        per_device,
        mesh=mesh,
        in_specs=(
            P("genome", "offset", None, None),
            P("offset"),
            P("genome"),
            P(None, "genome"),
            P(None, "genome"),
        ),
        out_specs=(P("genome"), P(None, ("genome", "offset")), P(None, ("genome", "offset"))),
        check_vma=False,
    )
```

```python
import functools

import jax
import jax.numpy as jnp
from jax import lax
from jax.experimental import pallas as pl
from jax.experimental.pallas import tpu as pltpu
from jax.sharding import PartitionSpec as P

ITERS = 3
STEP = 8
EARLY = 2
F32 = jnp.float32
BF16 = jnp.bfloat16
VMEM_LIMIT = 20 * 1024 * 1024
NT = (((1,), (1,)), ((), ()))
TN = (((0,), (0,)), ((), ()))


def split(x):
    hi = x.astype(BF16)
    lo = (x - hi.astype(F32)).astype(BF16)
    return hi, lo


def tree_sum(parts):
    while len(parts) > 1:
        parts = [a + b for a, b in zip(parts[::2], parts[1::2])]
    return parts[0]


def params():
    return pltpu.CompilerParams(vmem_limit_bytes=VMEM_LIMIT)


def scale_from(mask, parts):
    cover = tree_sum([p[...] for p in parts[:1] + parts[:0:-1]])
    live = mask[...] > 0
    return jnp.where(live, 1.0 / jnp.where(live, cover, 1.0), 0.0)


def vmem():
    return pl.BlockSpec(memory_space=pltpu.VMEM)


def kernel_call(body, name, scalars, args, outs, scratch=(), aliases=None, specs=None):
    return pl.pallas_call(
        body,
        grid_spec=pltpu.PrefetchScalarGridSpec(
            num_scalar_prefetch=1,
            grid=(1,),
            in_specs=specs or [vmem() for _ in args],
            out_specs=[vmem() for _ in outs],
            scratch_shapes=list(scratch),
        ),
        out_shape=outs,
        input_output_aliases=aliases or {},
        compiler_params=params(),
        name=name,
    )(scalars, *args)


def offsets(scal, slots):
    return [scal[1 + s] for s in range(slots)]


def by_diagonal(offs, slots, go):
    for s in range(slots):

        @pl.when(offs[s] == 0)
        def _():
            go(s)

    @pl.when(functools.reduce(jnp.logical_and, [offs[s] != 0 for s in range(slots)]))
    def _():
        go(-1)


def tile_value(counts, i, s, diagonal):
    c = counts[i, s].astype(F32)
    if s == diagonal:
        tile = c.shape[0]
        r = lax.broadcasted_iota(jnp.int32, (tile, tile), 0)
        q = lax.broadcasted_iota(jnp.int32, (tile, tile), 1)
        c = jnp.where(r < q, c, jnp.where(r == q, 0.5 * c, 0.0))
    return c


def cover_block(offs, counts, u_ref, acc, base, diagonal, at, kept=None):
    slots, tile = counts.shape[1:3]
    ones = jnp.ones((8, tile), BF16)
    u_block = u_ref[pl.ds(base, STEP), :]
    u_cols = u_block.T
    u_across = [u_ref[pl.ds(base + offs[s], STEP), :] for s in range(slots)]
    cols = [[] for _ in range(slots)]
    sums = []
    for t in range(STEP):
        total = None
        for s in range(slots):
            c = tile_value(counts, at + t, s, diagonal)
            if kept is not None:
                kept[base + t, s] = c
            term = c * u_across[s][t : t + 1]
            total = term if total is None else total + term
            cols[s].append(jnp.sum(c * u_cols[:, t : t + 1], axis=0, keepdims=True))
        hi, lo = split(total)
        row = lax.dot_general(ones, hi, NT, preferred_element_type=F32)
        row = row + lax.dot_general(ones, lo, NT, preferred_element_type=F32)
        sums.append(row[:1])
    acc[pl.ds(base, STEP), :] += jnp.concatenate(sums, axis=0)
    for s in range(slots):
        acc[pl.ds(base + offs[s], STEP), :] += jnp.concatenate(cols[s], axis=0)


def block_copies(hbm, buffer, sems, bases):
    return [
        pltpu.make_async_copy(
            hbm.at[pl.ds(base, STEP)], buffer.at[pl.ds(k * STEP, STEP)], sems.at[k]
        )
        for k, base in enumerate(bases)
    ]


def edge_bases(rows, pad):
    return list(range(0, pad, STEP)) + list(range(rows - pad, rows, STEP))


def write_edge(v_out, edge_out, rows):
    pad = v_out.shape[0] - rows
    edge_out[:pad] = v_out[:pad]
    edge_out[pad:] = v_out[rows:]


def first_main_kernel(scal, hbm, mask, v_out, kept, buffer, sems):
    rows, slots = hbm.shape[:2]
    offs = offsets(scal, slots)
    pad = v_out.shape[0] - rows
    inner = list(range(pad, rows - pad, STEP))
    bases = inner + edge_bases(rows, pad)
    copies = block_copies(hbm, buffer, sems, bases)
    for copy in copies:
        copy.start()
    v_out[...] = jnp.zeros_like(v_out)

    def go(diagonal):
        for k, base in enumerate(bases):
            copies[k].wait()
            at = k * STEP
            if base in inner:
                cover_block(offs, buffer, mask, v_out, base, diagonal, at, kept)
            else:
                for t in range(STEP):
                    for s in range(slots):
                        kept[base + t, s] = tile_value(buffer, at + t, s, diagonal)

    by_diagonal(offs, slots, go)


def first_edge_kernel(scal, kept, u_ref, inner_v, v_out, edge_out):
    rows, slots = kept.shape[:2]
    offs = offsets(scal, slots)
    v_out[...] = inner_v[...]
    for base in edge_bases(rows, u_ref.shape[0] - rows):
        cover_block(offs, kept, u_ref, v_out, base, -1, base)
    write_edge(v_out, edge_out, rows)


def edge_kernel(scal, kept, mask, *refs):
    v_out, edge_out, u_out = refs[-3:]
    rows, slots = kept.shape[:2]
    offs = offsets(scal, slots)
    u_out[...] = scale_from(mask, refs[:-4])
    v_out[...] = jnp.zeros_like(v_out)
    for base in edge_bases(rows, mask.shape[0] - rows):
        cover_block(offs, kept, u_out, v_out, base, -1, base)
    write_edge(v_out, edge_out, rows)


def main_kernel(scal, kept, u_ref, edge_v, v_out):
    rows, slots = kept.shape[:2]
    offs = offsets(scal, slots)
    pad = edge_v.shape[0] - rows
    v_out[...] = edge_v[...]
    for base in range(pad, rows - pad, STEP):
        cover_block(offs, kept, u_ref, v_out, base, -1, base)


def first_main(scal, counts, mask, ext):
    rows, slots, tile = counts.shape[:3]
    outs = [jax.ShapeDtypeStruct((ext, tile), F32), pltpu.VMEM(counts.shape, F32)]
    return kernel_call(
        first_main_kernel,
        "first_main",
        scal,
        [counts, mask],
        outs,
        [pltpu.VMEM(counts.shape, counts.dtype), pltpu.SemaphoreType.DMA((rows // STEP,))],
        specs=[pl.BlockSpec(memory_space=pltpu.HBM), vmem()],
    )


def first_edge(scal, kept, u, inner_v):
    rows, tile = kept.shape[0], kept.shape[2]
    flat = jax.ShapeDtypeStruct(u.shape, F32)
    edge = jax.ShapeDtypeStruct((2 * (u.shape[0] - rows), tile), F32)
    return kernel_call(first_edge_kernel, "first_edge", scal, [kept, u, inner_v], [flat, edge])


def cover_edge(scal, kept, mask_ext, parts, after):
    rows, tile = kept.shape[0], kept.shape[2]
    flat = jax.ShapeDtypeStruct(mask_ext.shape, F32)
    edge = jax.ShapeDtypeStruct((2 * (mask_ext.shape[0] - rows), tile), F32)
    args = [kept, mask_ext, *parts, after]
    return kernel_call(edge_kernel, "cover_edge", scal, args, [flat, edge, flat])


def cover_main(scal, kept, u, edge_v):
    outs = [jax.ShapeDtypeStruct(u.shape, F32)]
    return kernel_call(main_kernel, "cover_main", scal, [kept, u, edge_v], outs)[0]


def ratio_kernel(start, count, pad, scal, kept, w_ref, h_ref, after, *refs):
    slots, tile = kept.shape[1:3]
    offs = offsets(scal, slots)
    if start == 0:
        hi_out, lo_out, same, h_terms = refs
        same[...] = after[...]
    else:
        hi_out, lo_out, h_terms = refs[-3:]

    def prepare(j, carry):
        hi, lo = split(h_ref[:, pl.ds(pl.multiple_of(j * tile, tile), tile)])
        h_terms[j - start] = jnp.concatenate([hi, lo, hi, lo], axis=0)
        return carry

    lax.fori_loop(start, start + count + pad, prepare, 0, unroll=4)

    def go(diagonal):
        def body(i, carry):
            hi, lo = split(w_ref[:, pl.ds(pl.multiple_of(i * tile, tile), tile)])
            w_terms = jnp.concatenate([hi, hi, lo, lo], axis=0)
            for s in range(slots):
                model = lax.dot_general(
                    w_terms, h_terms[i - start + offs[s]], TN, preferred_element_type=F32
                )
                values = kept[i, s]
                if s == diagonal:
                    values = values + values.T
                r_hi, r_lo = split(values * (1.0 / model))
                hi_out[i, :, s * tile : (s + 1) * tile] = r_hi
                lo_out[i, :, s * tile : (s + 1) * tile] = r_lo
            return carry

        lax.fori_loop(start, start + count, body, 0, unroll=4)

    by_diagonal(offs, slots, go)


def ratio(scal, kept, row_factors, col_ext, after, earlier, start, count):
    rows, slots, tile = kept.shape[:3]
    factors = row_factors.shape[0]
    pad = after.shape[0] - rows
    out = pltpu.VMEM((rows, tile, slots * tile), BF16)
    return kernel_call(
        functools.partial(ratio_kernel, start, count, pad),
        "ratio",
        scal,
        [kept, row_factors, col_ext, after, *earlier],
        [out, out] + [jax.ShapeDtypeStruct(after.shape, F32)] * (start == 0),
        [pltpu.VMEM((count + pad, 4 * factors, tile), BF16)],
        {5: 0, 6: 1} if earlier else {},
    )


def row_numer(offs, g_all, hi_ref, lo_ref, u_ref, i):
    slots = hi_ref.shape[2] // g_all.shape[2]
    factors = g_all.shape[1] // 2
    g = jnp.concatenate([g_all[i + offs[s]] for s in range(slots)], axis=1)
    big = lax.dot_general(g, hi_ref[i], NT, preferred_element_type=F32)
    small = lax.dot_general(g[:factors], lo_ref[i], NT, preferred_element_type=F32)
    return (big[:factors] + big[factors:] + small) * u_ref[pl.ds(i, 1), :]


def col_numer(w_ref, hi_ref, lo_ref, u_ref, i):
    tile = u_ref.shape[1]
    factors = w_ref.shape[0]
    w = w_ref[:, pl.ds(pl.multiple_of(i * tile, tile), tile)]
    hi, lo = split(w * u_ref[pl.ds(i, 1), :])
    big = jnp.dot(jnp.concatenate([hi, lo], axis=0), hi_ref[i], preferred_element_type=F32)
    small = jnp.dot(hi, lo_ref[i], preferred_element_type=F32)
    return big[:factors] + big[factors:] + small


def col_loop(offs, w_ref, hi_ref, lo_ref, u_ref, acc, start, count, shift):
    tile = u_ref.shape[1]

    def body(n, carry):
        i = start + n
        cols = col_numer(w_ref, hi_ref, lo_ref, u_ref, i)
        for s in range(hi_ref.shape[2] // tile):
            acc[i + offs[s] - shift] += cols[:, s * tile : (s + 1) * tile]
        return carry

    lax.fori_loop(0, count, body, 0, unroll=4)


def row_pieces(scal, offs, g_ref, hi_ref, lo_ref, u_ref, order, outs):
    for k, out in zip(order, outs):
        per = out.shape[0]
        first = jnp.bitwise_xor(scal[0], k) * per

        def body(t, carry):
            out[t] = row_numer(offs, g_ref, hi_ref, lo_ref, u_ref, first + t)
            return carry

        lax.fori_loop(0, per, body, 0, unroll=4)


def scaled_terms(h_ref, u_ref, terms, start, count):
    tile = u_ref.shape[1]
    factors = h_ref.shape[0]

    def fill(n, carry):
        j = start + n
        x = h_ref[:, pl.ds(pl.multiple_of(j * tile, tile), tile)] * u_ref[pl.ds(j, 1), :]
        hi, lo = split(x)
        terms[j, :factors] = hi
        terms[j, factors:] = lo
        return carry

    lax.fori_loop(0, count, fill, 0, unroll=4)


def numer_first_kernel(k, shares, scal, hi_ref, lo_ref, w_ref, h_ref, mask, *refs):
    parts = refs[:shares]
    u_out, tail_out, out, acc, terms = refs[shares:]
    rows = hi_ref.shape[0]
    ext, tile = mask.shape
    offs = offsets(scal, hi_ref.shape[2] // tile)
    per = rows // shares
    pad = ext - rows
    u_out[...] = scale_from(mask, parts)

    acc[...] = jnp.zeros_like(acc)
    col_loop(offs, w_ref, hi_ref, lo_ref, u_out, acc, rows - pad, pad, rows - pad)
    for t in range(pad):
        tail_out[t] = acc[pad + t] * u_out[rows + t : rows + t + 1, :]
    lane = lax.broadcasted_iota(jnp.int32, tail_out.shape[1:], 1)
    ends = jnp.zeros(tail_out.shape[1:], F32)
    for t in range(pad):
        ends = jnp.where(lane == t, tile_sum(w_ref, mask, rows - pad + t), ends)
    tail_out[pad] = ends

    first = jnp.bitwise_xor(scal[0], k) * per
    scaled_terms(h_ref, u_out, terms, first, per + pad)
    row_pieces(scal, offs, terms, hi_ref, lo_ref, u_out, [k], [out])


def numer_col_kernel(order, scal, hi_ref, lo_ref, w_ref, *refs):
    scales, refs = refs[: ITERS + 1], refs[ITERS + 2 :]
    sums_out, outs, acc = refs[0], refs[1:-1], refs[-1]
    u_ref = scales[-1]
    rows = hi_ref.shape[0]
    tile = u_ref.shape[1]
    offs = offsets(scal, hi_ref.shape[2] // tile)
    per = outs[0].shape[0]
    acc[...] = jnp.zeros_like(acc)
    col_loop(offs, w_ref, hi_ref, lo_ref, u_ref, acc, 0, rows, 0)
    for k, out in zip(order, outs):
        first = jnp.bitwise_xor(scal[0], k) * per

        def body(t, carry):
            out[t] = acc[first + t] * u_ref[pl.ds(first + t, 1), :]
            return carry

        lax.fori_loop(0, per, body, 0, unroll=4)
    write_sums(sums_out, scales, rows)


def write_sums(sums_out, scales, rows):
    sums_out[...] = jnp.zeros_like(sums_out)
    mask = scales[0][:rows]
    totals = [mask]
    for t in range(ITERS):
        below = jnp.where(mask > 0, scales[t + 1][:rows], 1.0)
        totals.append(jnp.where(mask > 0, scales[t][:rows] / below, 0.0))
    for t, total in enumerate(totals):
        line = jnp.sum(jnp.sum(total, axis=0, keepdims=True), axis=1, keepdims=True)
        sums_out[t : t + 1, :] = jnp.broadcast_to(line, (1, mask.shape[1]))


def numer_row_kernel(order, scal, hi_ref, lo_ref, h_ref, u_ref, after, *refs):
    outs, terms = refs[:-1], refs[-1]
    ext, tile = u_ref.shape
    offs = offsets(scal, hi_ref.shape[2] // tile)
    rows, per = hi_ref.shape[0], outs[0].shape[0]
    if len(order) > 1:
        scaled_terms(h_ref, u_ref, terms, 0, ext)
    else:
        first = jnp.bitwise_xor(scal[0], order[0]) * per
        scaled_terms(h_ref, u_ref, terms, first, per + ext - rows)
    row_pieces(scal, offs, terms, hi_ref, lo_ref, u_ref, order, outs)


def numer_first(scal, r_hi, r_lo, row_factors, col_ext, mask_ext, parts, k):
    shares = len(parts)
    rows, tile = r_hi.shape[:2]
    factors = row_factors.shape[0]
    ext = mask_ext.shape[0]
    pad = ext - rows
    per = rows // shares
    return kernel_call(
        functools.partial(numer_first_kernel, k, shares),
        "numer_first",
        scal,
        [r_hi, r_lo, row_factors, col_ext, mask_ext, *parts],
        [
            jax.ShapeDtypeStruct((ext, tile), F32),
            jax.ShapeDtypeStruct((pad + 1, factors, tile), F32),
            jax.ShapeDtypeStruct((per, factors, tile), F32),
        ],
        [
            pltpu.VMEM((2 * pad, factors, tile), F32),
            pltpu.VMEM((ext, 2 * factors, tile), BF16),
        ],
    )


def numer_col(scal, r_hi, r_lo, row_factors, scales, after, order, shares):
    rows, tile = r_hi.shape[:2]
    factors = row_factors.shape[0]
    piece = jax.ShapeDtypeStruct((rows // shares, factors, tile), F32)
    res = kernel_call(
        functools.partial(numer_col_kernel, order),
        "numer_col",
        scal,
        [r_hi, r_lo, row_factors, *scales, after],
        [jax.ShapeDtypeStruct((8, tile), F32)] + [piece] * len(order),
        [pltpu.VMEM((scales[0].shape[0], factors, tile), F32)],
    )
    return res[0], res[1:]


def numer_row(scal, r_hi, r_lo, col_ext, u, after, order, shares):
    rows, tile = r_hi.shape[:2]
    factors = col_ext.shape[0]
    piece = jax.ShapeDtypeStruct((rows // shares, factors, tile), F32)
    return kernel_call(
        functools.partial(numer_row_kernel, order),
        "numer_row",
        scal,
        [r_hi, r_lo, col_ext, u, after],
        [piece] * len(order),
        [pltpu.VMEM((u.shape[0], 2 * factors, tile), BF16)],
    )


def mean_scale(sums):
    scale = sums[1:2, :] / sums[0:1, :]
    for t in range(1, ITERS):
        scale = scale * (sums[t + 1 : t + 2, :] / sums[0:1, :])
    return scale


def tile_sum(factor_ref, mask, j):
    tile = mask.shape[1]
    x = factor_ref[:, pl.ds(pl.multiple_of(j * tile, tile), tile)] * mask[pl.ds(j, 1), :]
    return jnp.sum(x, axis=1, keepdims=True)


def windows(sums, per):
    return [tree_sum(sums[t : t + len(sums) - per]) for t in range(per)]


def write_coefficient(old_ref, mask, first, lowers, times_out, plus_out):
    tile = mask.shape[1]
    for t, lower in enumerate(lowers):
        live = mask[pl.ds(first + t, 1), :]
        old = old_ref[:, t * tile : (t + 1) * tile]
        times_out[t] = jnp.where(live > 0, old / jnp.where(live > 0, lower * live, 1.0), 0.0)
        plus_out[t] = jnp.where(live > 0, 0.0, old)


def row_coefficient_kernel(pad, scal, old_ref, mask, other, times_out, plus_out):
    per = times_out.shape[0]
    first = scal[0] * per
    sums = [tile_sum(other, mask, first + t) for t in range(per + pad)]
    write_coefficient(old_ref, mask, first, windows(sums, per), times_out, plus_out)


def col_coefficient_kernel(pad, scal, old_ref, mask, other, ends, times_out, plus_out):
    per = times_out.shape[0]
    first = scal[0] * per
    sums = []
    for j in range(1, per + pad):
        total = tile_sum(other, mask, jnp.maximum(first - pad + j, 0))
        for start in range(0, pad, per):
            if start + j < pad:
                before = jnp.where(scal[scal.shape[0] - 1] > 0, ends[:, start + j : start + j + 1], 0.0)
                total = jnp.where(first == start, before, total)
        sums.append(total)
    sums.append(jnp.zeros_like(sums[0]))
    write_coefficient(old_ref, mask, first, windows(sums, per), times_out, plus_out)


def coefficient(kernel, scal, shares, old, mask_ext, other, *ends):
    factors = old.shape[0]
    tile = mask_ext.shape[1]
    rows = old.shape[1] // tile
    per = rows // shares
    specs = [pl.BlockSpec((factors, per * tile), lambda i, scal: (0, scal[0]))]
    specs += [vmem() for _ in range(2 + len(ends))]
    return kernel_call(
        functools.partial(kernel, mask_ext.shape[0] - rows),
        "coefficient",
        scal,
        [old, mask_ext, other, *ends],
        [jax.ShapeDtypeStruct((per, factors, tile), F32)] * 2,
        specs=specs,
    )


def update_kernel(scal, sums, times, plus, *refs):
    terms, out = refs[:-1], refs[-1]
    per, _, tile = times.shape
    c = mean_scale(sums[...])
    for t in range(per):
        numer = terms[0][t]
        for term in terms[1:]:
            numer = numer + term[t]
        out[:, t * tile : (t + 1) * tile] = times[t] * (numer * c * c) + plus[t]


def update(scal, sums, times, plus, terms):
    per, count, tile = terms[0].shape
    return kernel_call(
        update_kernel,
        "update",
        scal,
        [sums, times, plus, *terms],
        [jax.ShapeDtypeStruct((count, per * tile), F32)],
    )[0]


def xor_exchange(x, axis, k):
    return lax.ppermute(x, axis, [(i, i ^ k) for i in range(lax.axis_size(axis))])


def both_sides(x, even):
    size = lax.axis_size("genome")
    a = lax.ppermute(x, "genome", [(i, i ^ 1) for i in range(size)])
    b = lax.ppermute(x, "genome", [(i, (((i + 1) ^ 1) - 1) % size) for i in range(size)])
    return jnp.where(even > 0, a, b), jnp.where(even > 0, b, a)


def scatter_terms(pieces, far=None):
    size = lax.axis_size("offset")
    if size == 4:
        if far is None:
            far = pieces[3] + xor_exchange(pieces[2], "offset", 1)
            far = xor_exchange(far, "offset", 3)
        return [pieces[0], xor_exchange(pieces[1], "offset", 1), far]
    return [pieces[0]] + [xor_exchange(pieces[k], "offset", k) for k in range(1, size)]


def per_device(counts, band_offset, bin_mask, row_factors, col_factors):
    rows, slots, tile = counts.shape[:3]
    factors = row_factors.shape[0]
    offset_count = lax.axis_size("offset")
    genome_count = lax.axis_size("genome")
    g = lax.axis_index("genome")
    o = lax.axis_index("offset").astype(jnp.int32)
    reach = slots * offset_count - 1
    pad = reach + 1

    line = jnp.broadcast_to(g, (1, tile))
    even = (line % 2 == 0).astype(F32)
    has_next = (line < genome_count - 1).astype(F32)
    has_prev = (line > 0).astype(F32)
    count = offset_count * -(-pad * offset_count // rows)
    index = lax.broadcasted_iota(jnp.int32, (count, tile), 0)
    share, k = index // offset_count, index % offset_count
    mine = (jnp.bitwise_xor(share, k) == o).astype(F32) * has_prev
    flags = jnp.concatenate([even, has_next, has_prev, mine])
    before = jnp.broadcast_to((g > 0).astype(jnp.int32), (1,))
    scal = jnp.concatenate([jnp.broadcast_to(o, (1,)), band_offset, before])
    flags, scal, bin_mask = lax.optimization_barrier((flags, scal, bin_mask))
    even, has_next, has_prev = flags[0:1], flags[1:2], flags[2:3]
    mine = flags[3:]

    mask = bin_mask.astype(F32).reshape(rows, tile)
    mask_next, _ = both_sides(mask[:pad], even)
    keep = lax.broadcasted_iota(jnp.int32, (pad, 1), 0) < reach
    mask_ext = jnp.concatenate([mask, jnp.where(keep, mask_next * has_next, 0.0)])

    counts = pltpu.with_memory_space_constraint(counts, pltpu.HBM)
    inner_v, kept = first_main(scal, counts, mask, rows + pad)
    col_late, _ = lax.optimization_barrier((col_factors, inner_v))
    ring_left = [(i, (i - 1) % genome_count) for i in range(genome_count)]
    col_next = lax.ppermute(col_late[:, : pad * tile], "genome", ring_left)
    col_ext = jnp.concatenate([col_factors, col_next], axis=1)

    scales = []
    quarter = rows // (ITERS + 1)
    for t in range(ITERS):
        if t == 0:
            u = mask_ext
            v, edge = first_edge(scal, kept, u, inner_v)
        else:
            v, edge, u = cover_edge(scal, kept, mask_ext, parts, ratios[0])
        scales.append(u)
        after, before = both_sides(edge, even)
        if t > 0:
            v = cover_main(scal, kept, u, v)
        else:
            *ratios, v = ratio(scal, kept, row_factors, col_factors, v, [], 0, 2 * quarter)
        front = v[:pad] + before[pad:] * has_prev
        back = v[rows:] + after[:pad] * has_next
        x = jnp.concatenate([front, v[pad:rows], back])
        others = {k: xor_exchange(x, "offset", k) for k in reversed(range(1, offset_count))}
        parts = [x, *others.values()]
        if t == 0:
            ratios = ratio(scal, kept, row_factors, col_factors, x, ratios, 2 * quarter, quarter)
        elif t == ITERS - 1:
            ratios = ratio(scal, kept, row_factors, col_ext, x, ratios, 3 * quarter, quarter)

    r_hi, r_lo = ratios
    per = rows // offset_count
    u, tail, early = numer_first(
        scal, r_hi, r_lo, row_factors, col_ext, mask_ext, parts, EARLY
    )
    scales.append(u)
    order = [EARLY, *(k for k in range(offset_count) if k != EARLY)]
    (second,) = numer_row(scal, r_hi, r_lo, col_ext, u, early, [3], offset_count)
    sums, pieces = numer_col(
        scal, r_hi, r_lo, row_factors, scales, second, order, offset_count
    )
    h_parts = dict(zip(order, pieces))

    right = [(i, (i + 1) % genome_count) for i in range(genome_count)]
    arrived = lax.ppermute(tail, "genome", right)
    for s in range(-(-pad // per)):
        piece = arrived[s * per : min(pad, (s + 1) * per)]
        for k in range(offset_count):
            at = s * offset_count + k
            h_parts[k] = h_parts[k].at[: piece.shape[0]].add(piece * mine[at : at + 1])

    row_terms = coefficient(
        row_coefficient_kernel, scal, offset_count, row_factors, mask_ext, col_ext
    )
    col_terms = coefficient(
        col_coefficient_kernel, scal, offset_count, col_factors, mask_ext, row_factors, arrived[pad]
    )
    w_parts = {EARLY: early, 3: second}
    hop = None
    if offset_count == 4:
        half_way = second + xor_exchange(early, "offset", 1)
        hop = xor_exchange(half_way, "offset", 3)
    else:
        half_way = h_parts[EARLY]
    order = [k for k in range(offset_count) if k not in w_parts]
    pieces = numer_row(scal, r_hi, r_lo, col_ext, u, half_way, order, offset_count)
    w_parts |= dict(zip(order, pieces))
    w_terms = scatter_terms([w_parts[k] for k in range(offset_count)], hop)
    h_terms = scatter_terms([h_parts[k] for k in range(offset_count)])

    sums, _ = lax.optimization_barrier((sums, w_terms[2]))
    sums = jnp.sum(lax.all_gather(sums, "genome"), axis=0)
    bias = (u[:rows] * mean_scale(sums)).reshape(-1)

    col_update = update(scal, sums, *col_terms, h_terms)
    row_update = update(scal, sums, *row_terms, w_terms)
    return bias, row_update, col_update


def solution(mesh):
    return jax.shard_map(
        per_device,
        mesh=mesh,
        in_specs=(
            P("genome", "offset", None, None),
            P("offset"),
            P("genome"),
            P(None, "genome"),
            P(None, "genome"),
        ),
        out_specs=(P("genome"), P(None, ("genome", "offset")), P(None, ("genome", "offset"))),
        check_vma=False,
    )
```

```python
import functools

import jax
import jax.numpy as jnp
from jax import lax
from jax.experimental import pallas as pl
from jax.experimental.pallas import tpu as pltpu
from jax.sharding import PartitionSpec as P

ITERS = 3
STEP = 8
EARLY = 2
F32 = jnp.float32
BF16 = jnp.bfloat16
VMEM_LIMIT = 20 * 1024 * 1024
NT = (((1,), (1,)), ((), ()))
TN = (((0,), (0,)), ((), ()))


def split(x):
    hi = x.astype(BF16)
    lo = (x - hi.astype(F32)).astype(BF16)
    return hi, lo


def tree_sum(parts):
    while len(parts) > 1:
        parts = [a + b for a, b in zip(parts[::2], parts[1::2])]
    return parts[0]


def params():
    return pltpu.CompilerParams(vmem_limit_bytes=VMEM_LIMIT)


def scale_from(mask, parts):
    cover = tree_sum([p[...] for p in parts])
    live = mask[...] > 0
    return jnp.where(live, 1.0 / jnp.where(live, cover, 1.0), 0.0)


def vmem():
    return pl.BlockSpec(memory_space=pltpu.VMEM)


def kernel_call(body, name, scalars, args, outs, scratch=(), aliases=None, specs=None):
    return pl.pallas_call(
        body,
        grid_spec=pltpu.PrefetchScalarGridSpec(
            num_scalar_prefetch=1,
            grid=(1,),
            in_specs=specs or [vmem() for _ in args],
            out_specs=[vmem() for _ in outs],
            scratch_shapes=list(scratch),
        ),
        out_shape=outs,
        input_output_aliases=aliases or {},
        compiler_params=params(),
        name=name,
    )(scalars, *args)


def offsets(scal, slots):
    return [scal[1 + s] for s in range(slots)]


def by_diagonal(offs, slots, go):
    for s in range(slots):

        @pl.when(offs[s] == 0)
        def _():
            go(s)

    @pl.when(functools.reduce(jnp.logical_and, [offs[s] != 0 for s in range(slots)]))
    def _():
        go(-1)


def tile_value(counts, i, s, diagonal):
    c = counts[i, s].astype(F32)
    if s == diagonal:
        tile = c.shape[0]
        r = lax.broadcasted_iota(jnp.int32, (tile, tile), 0)
        q = lax.broadcasted_iota(jnp.int32, (tile, tile), 1)
        c = jnp.where(r < q, c, jnp.where(r == q, 0.5 * c, 0.0))
    return c


def cover_block(offs, counts, u_ref, acc, base, diagonal, at, kept=None):
    slots, tile = counts.shape[1:3]
    ones = jnp.ones((8, tile), BF16)
    u_block = u_ref[pl.ds(base, STEP), :]
    u_cols = u_block.T
    u_across = [u_ref[pl.ds(base + offs[s], STEP), :] for s in range(slots)]
    cols = [[] for _ in range(slots)]
    sums = []
    for t in range(STEP):
        total = None
        for s in range(slots):
            c = tile_value(counts, at + t, s, diagonal)
            if kept is not None:
                kept[base + t, s] = c
            term = c * u_across[s][t : t + 1]
            total = term if total is None else total + term
            cols[s].append(jnp.sum(c * u_cols[:, t : t + 1], axis=0, keepdims=True))
        hi, lo = split(total)
        row = lax.dot_general(ones, hi, NT, preferred_element_type=F32)
        row = row + lax.dot_general(ones, lo, NT, preferred_element_type=F32)
        sums.append(row[:1])
    acc[pl.ds(base, STEP), :] += jnp.concatenate(sums, axis=0)
    for s in range(slots):
        acc[pl.ds(base + offs[s], STEP), :] += jnp.concatenate(cols[s], axis=0)


def block_copies(hbm, buffer, sems, bases):
    return [
        pltpu.make_async_copy(
            hbm.at[pl.ds(base, STEP)], buffer.at[pl.ds(k * STEP, STEP)], sems.at[k]
        )
        for k, base in enumerate(bases)
    ]


def edge_bases(rows, pad):
    return list(range(0, pad, STEP)) + list(range(rows - pad, rows, STEP))


def write_edge(v_out, edge_out, rows):
    pad = v_out.shape[0] - rows
    edge_out[:pad] = v_out[:pad]
    edge_out[pad:] = v_out[rows:]


def first_main_kernel(scal, hbm, mask, v_out, kept, buffer, sems):
    rows, slots = hbm.shape[:2]
    offs = offsets(scal, slots)
    pad = v_out.shape[0] - rows
    inner = list(range(pad, rows - pad, STEP))
    bases = inner + edge_bases(rows, pad)
    copies = block_copies(hbm, buffer, sems, bases)
    for copy in copies:
        copy.start()
    v_out[...] = jnp.zeros_like(v_out)

    def go(diagonal):
        for k, base in enumerate(bases):
            copies[k].wait()
            at = k * STEP
            if base in inner:
                cover_block(offs, buffer, mask, v_out, base, diagonal, at, kept)
            else:
                for t in range(STEP):
                    for s in range(slots):
                        kept[base + t, s] = tile_value(buffer, at + t, s, diagonal)

    by_diagonal(offs, slots, go)


def first_edge_kernel(scal, kept, u_ref, inner_v, v_out, edge_out):
    rows, slots = kept.shape[:2]
    offs = offsets(scal, slots)
    v_out[...] = inner_v[...]
    for base in edge_bases(rows, u_ref.shape[0] - rows):
        cover_block(offs, kept, u_ref, v_out, base, -1, base)
    write_edge(v_out, edge_out, rows)


def edge_kernel(scal, kept, mask, *refs):
    v_out, edge_out, u_out = refs[-3:]
    rows, slots = kept.shape[:2]
    offs = offsets(scal, slots)
    u_out[...] = scale_from(mask, refs[:-4])
    v_out[...] = jnp.zeros_like(v_out)
    for base in edge_bases(rows, mask.shape[0] - rows):
        cover_block(offs, kept, u_out, v_out, base, -1, base)
    write_edge(v_out, edge_out, rows)


def main_kernel(scal, kept, u_ref, edge_v, v_out):
    rows, slots = kept.shape[:2]
    offs = offsets(scal, slots)
    pad = edge_v.shape[0] - rows
    v_out[...] = edge_v[...]
    for base in range(pad, rows - pad, STEP):
        cover_block(offs, kept, u_ref, v_out, base, -1, base)


def first_main(scal, counts, mask, ext):
    rows, slots, tile = counts.shape[:3]
    outs = [jax.ShapeDtypeStruct((ext, tile), F32), pltpu.VMEM(counts.shape, F32)]
    return kernel_call(
        first_main_kernel,
        "first_main",
        scal,
        [counts, mask],
        outs,
        [pltpu.VMEM(counts.shape, counts.dtype), pltpu.SemaphoreType.DMA((rows // STEP,))],
        specs=[pl.BlockSpec(memory_space=pltpu.HBM), vmem()],
    )


def first_edge(scal, kept, u, inner_v):
    rows, tile = kept.shape[0], kept.shape[2]
    flat = jax.ShapeDtypeStruct(u.shape, F32)
    edge = jax.ShapeDtypeStruct((2 * (u.shape[0] - rows), tile), F32)
    return kernel_call(first_edge_kernel, "first_edge", scal, [kept, u, inner_v], [flat, edge])


def cover_edge(scal, kept, mask_ext, parts, after):
    rows, tile = kept.shape[0], kept.shape[2]
    flat = jax.ShapeDtypeStruct(mask_ext.shape, F32)
    edge = jax.ShapeDtypeStruct((2 * (mask_ext.shape[0] - rows), tile), F32)
    args = [kept, mask_ext, *parts, after]
    return kernel_call(edge_kernel, "cover_edge", scal, args, [flat, edge, flat])


def cover_main(scal, kept, u, edge_v):
    outs = [jax.ShapeDtypeStruct(u.shape, F32)]
    return kernel_call(main_kernel, "cover_main", scal, [kept, u, edge_v], outs)[0]


def ratio_kernel(start, count, pad, scal, kept, w_ref, h_ref, after, *refs):
    slots, tile = kept.shape[1:3]
    offs = offsets(scal, slots)
    if start == 0:
        hi_out, lo_out, same, h_terms = refs
        same[...] = after[...]
    else:
        hi_out, lo_out, h_terms = refs[-3:]

    def prepare(j, carry):
        hi, lo = split(h_ref[:, pl.ds(pl.multiple_of(j * tile, tile), tile)])
        h_terms[j - start] = jnp.concatenate([hi, lo, hi, lo], axis=0)
        return carry

    lax.fori_loop(start, start + count + pad, prepare, 0, unroll=4)

    def go(diagonal):
        def body(i, carry):
            hi, lo = split(w_ref[:, pl.ds(pl.multiple_of(i * tile, tile), tile)])
            w_terms = jnp.concatenate([hi, hi, lo, lo], axis=0)
            for s in range(slots):
                model = lax.dot_general(
                    w_terms, h_terms[i - start + offs[s]], TN, preferred_element_type=F32
                )
                values = kept[i, s]
                if s == diagonal:
                    values = values + values.T
                r_hi, r_lo = split(values * (1.0 / model))
                hi_out[i, :, s * tile : (s + 1) * tile] = r_hi
                lo_out[i, :, s * tile : (s + 1) * tile] = r_lo
            return carry

        lax.fori_loop(start, start + count, body, 0, unroll=4)

    by_diagonal(offs, slots, go)


def ratio(scal, kept, row_factors, col_ext, after, earlier, start, count):
    rows, slots, tile = kept.shape[:3]
    factors = row_factors.shape[0]
    pad = after.shape[0] - rows
    out = pltpu.VMEM((rows, tile, slots * tile), BF16)
    return kernel_call(
        functools.partial(ratio_kernel, start, count, pad),
        "ratio",
        scal,
        [kept, row_factors, col_ext, after, *earlier],
        [out, out] + [jax.ShapeDtypeStruct(after.shape, F32)] * (start == 0),
        [pltpu.VMEM((count + pad, 4 * factors, tile), BF16)],
        {5: 0, 6: 1} if earlier else {},
    )


def row_numer(offs, g_all, hi_ref, lo_ref, u_ref, i):
    slots = hi_ref.shape[2] // g_all.shape[2]
    factors = g_all.shape[1] // 2
    g = jnp.concatenate([g_all[i + offs[s]] for s in range(slots)], axis=1)
    big = lax.dot_general(g, hi_ref[i], NT, preferred_element_type=F32)
    small = lax.dot_general(g[:factors], lo_ref[i], NT, preferred_element_type=F32)
    return (big[:factors] + big[factors:] + small) * u_ref[pl.ds(i, 1), :]


def col_numer(w_ref, hi_ref, lo_ref, u_ref, i):
    tile = u_ref.shape[1]
    factors = w_ref.shape[0]
    w = w_ref[:, pl.ds(pl.multiple_of(i * tile, tile), tile)]
    hi, lo = split(w * u_ref[pl.ds(i, 1), :])
    big = jnp.dot(jnp.concatenate([hi, lo], axis=0), hi_ref[i], preferred_element_type=F32)
    small = jnp.dot(hi, lo_ref[i], preferred_element_type=F32)
    return big[:factors] + big[factors:] + small


def col_loop(offs, w_ref, hi_ref, lo_ref, u_ref, acc, start, count, shift):
    tile = u_ref.shape[1]

    def body(n, carry):
        i = start + n
        cols = col_numer(w_ref, hi_ref, lo_ref, u_ref, i)
        for s in range(hi_ref.shape[2] // tile):
            acc[i + offs[s] - shift] += cols[:, s * tile : (s + 1) * tile]
        return carry

    lax.fori_loop(0, count, body, 0, unroll=4)


def row_pieces(scal, offs, g_ref, hi_ref, lo_ref, u_ref, order, outs):
    for k, out in zip(order, outs):
        per = out.shape[0]
        first = jnp.bitwise_xor(scal[0], k) * per

        def body(t, carry):
            out[t] = row_numer(offs, g_ref, hi_ref, lo_ref, u_ref, first + t)
            return carry

        lax.fori_loop(0, per, body, 0, unroll=4)


def scaled_terms(h_ref, u_ref, terms, start, count):
    tile = u_ref.shape[1]
    factors = h_ref.shape[0]

    def fill(n, carry):
        j = start + n
        x = h_ref[:, pl.ds(pl.multiple_of(j * tile, tile), tile)] * u_ref[pl.ds(j, 1), :]
        hi, lo = split(x)
        terms[j, :factors] = hi
        terms[j, factors:] = lo
        return carry

    lax.fori_loop(0, count, fill, 0, unroll=4)


def numer_first_kernel(k, shares, scal, hi_ref, lo_ref, w_ref, h_ref, mask, *refs):
    parts = refs[:shares]
    u_out, tail_out, out, acc, terms = refs[shares:]
    rows = hi_ref.shape[0]
    ext, tile = mask.shape
    offs = offsets(scal, hi_ref.shape[2] // tile)
    per = rows // shares
    pad = ext - rows
    u_out[...] = scale_from(mask, parts)

    acc[...] = jnp.zeros_like(acc)
    col_loop(offs, w_ref, hi_ref, lo_ref, u_out, acc, rows - pad, pad, rows - pad)
    for t in range(pad):
        tail_out[t] = acc[pad + t] * u_out[rows + t : rows + t + 1, :]
    lane = lax.broadcasted_iota(jnp.int32, tail_out.shape[1:], 1)
    ends = jnp.zeros(tail_out.shape[1:], F32)
    for t in range(pad):
        ends = jnp.where(lane == t, tile_sum(w_ref, mask, rows - pad + t), ends)
    tail_out[pad] = ends

    first = jnp.bitwise_xor(scal[0], k) * per
    scaled_terms(h_ref, u_out, terms, first, per + pad)
    row_pieces(scal, offs, terms, hi_ref, lo_ref, u_out, [k], [out])


def numer_col_kernel(order, scal, hi_ref, lo_ref, w_ref, *refs):
    scales, refs = refs[: ITERS + 1], refs[ITERS + 1 :]
    sums_out, outs, acc = refs[0], refs[1:-1], refs[-1]
    u_ref = scales[-1]
    rows = hi_ref.shape[0]
    tile = u_ref.shape[1]
    offs = offsets(scal, hi_ref.shape[2] // tile)
    per = outs[0].shape[0]
    acc[...] = jnp.zeros_like(acc)
    col_loop(offs, w_ref, hi_ref, lo_ref, u_ref, acc, 0, rows, 0)
    for k, out in zip(order, outs):
        first = jnp.bitwise_xor(scal[0], k) * per

        def body(t, carry):
            out[t] = acc[first + t] * u_ref[pl.ds(first + t, 1), :]
            return carry

        lax.fori_loop(0, per, body, 0, unroll=4)
    write_sums(sums_out, scales, rows)


def write_sums(sums_out, scales, rows):
    sums_out[...] = jnp.zeros_like(sums_out)
    mask = scales[0][:rows]
    totals = [mask]
    for t in range(ITERS):
        below = jnp.where(mask > 0, scales[t + 1][:rows], 1.0)
        totals.append(jnp.where(mask > 0, scales[t][:rows] / below, 0.0))
    for t, total in enumerate(totals):
        line = jnp.sum(jnp.sum(total, axis=0, keepdims=True), axis=1, keepdims=True)
        sums_out[t : t + 1, :] = jnp.broadcast_to(line, (1, mask.shape[1]))


def numer_row_kernel(order, scal, hi_ref, lo_ref, h_ref, u_ref, after, *refs):
    outs, terms = refs[:-1], refs[-1]
    ext, tile = u_ref.shape
    offs = offsets(scal, hi_ref.shape[2] // tile)
    scaled_terms(h_ref, u_ref, terms, 0, ext)
    row_pieces(scal, offs, terms, hi_ref, lo_ref, u_ref, order, outs)


def numer_first(scal, r_hi, r_lo, row_factors, col_ext, mask_ext, parts, k):
    shares = len(parts)
    rows, tile = r_hi.shape[:2]
    factors = row_factors.shape[0]
    ext = mask_ext.shape[0]
    pad = ext - rows
    per = rows // shares
    return kernel_call(
        functools.partial(numer_first_kernel, k, shares),
        "numer_first",
        scal,
        [r_hi, r_lo, row_factors, col_ext, mask_ext, *parts],
        [
            jax.ShapeDtypeStruct((ext, tile), F32),
            jax.ShapeDtypeStruct((pad + 1, factors, tile), F32),
            jax.ShapeDtypeStruct((per, factors, tile), F32),
        ],
        [
            pltpu.VMEM((2 * pad, factors, tile), F32),
            pltpu.VMEM((ext, 2 * factors, tile), BF16),
        ],
    )


def numer_col(scal, r_hi, r_lo, row_factors, scales, order, shares):
    rows, tile = r_hi.shape[:2]
    factors = row_factors.shape[0]
    piece = jax.ShapeDtypeStruct((rows // shares, factors, tile), F32)
    res = kernel_call(
        functools.partial(numer_col_kernel, order),
        "numer_col",
        scal,
        [r_hi, r_lo, row_factors, *scales],
        [jax.ShapeDtypeStruct((8, tile), F32)] + [piece] * len(order),
        [pltpu.VMEM((scales[0].shape[0], factors, tile), F32)],
    )
    return res[0], res[1:]


def numer_row(scal, r_hi, r_lo, col_ext, u, after, order, shares):
    rows, tile = r_hi.shape[:2]
    factors = col_ext.shape[0]
    piece = jax.ShapeDtypeStruct((rows // shares, factors, tile), F32)
    return kernel_call(
        functools.partial(numer_row_kernel, order),
        "numer_row",
        scal,
        [r_hi, r_lo, col_ext, u, after],
        [piece] * len(order),
        [pltpu.VMEM((u.shape[0], 2 * factors, tile), BF16)],
    )


def mean_scale(sums):
    scale = sums[1:2, :] / sums[0:1, :]
    for t in range(1, ITERS):
        scale = scale * (sums[t + 1 : t + 2, :] / sums[0:1, :])
    return scale


def tile_sum(factor_ref, mask, j):
    tile = mask.shape[1]
    x = factor_ref[:, pl.ds(pl.multiple_of(j * tile, tile), tile)] * mask[pl.ds(j, 1), :]
    return jnp.sum(x, axis=1, keepdims=True)


def windows(sums, per):
    return [tree_sum(sums[t : t + len(sums) - per]) for t in range(per)]


def write_coefficient(old_ref, mask, first, lowers, times_out, plus_out):
    tile = mask.shape[1]
    for t, lower in enumerate(lowers):
        live = mask[pl.ds(first + t, 1), :]
        old = old_ref[:, t * tile : (t + 1) * tile]
        times_out[t] = jnp.where(live > 0, old / jnp.where(live > 0, lower * live, 1.0), 0.0)
        plus_out[t] = jnp.where(live > 0, 0.0, old)


def row_coefficient_kernel(pad, scal, old_ref, mask, other, times_out, plus_out):
    per = times_out.shape[0]
    first = scal[0] * per
    sums = [tile_sum(other, mask, first + t) for t in range(per + pad)]
    write_coefficient(old_ref, mask, first, windows(sums, per), times_out, plus_out)


def col_coefficient_kernel(pad, scal, old_ref, mask, other, ends, times_out, plus_out):
    per = times_out.shape[0]
    first = scal[0] * per
    sums = []
    for j in range(1, per + pad):
        total = tile_sum(other, mask, jnp.maximum(first - pad + j, 0))
        for start in range(0, pad, per):
            if start + j < pad:
                before = jnp.where(scal[scal.shape[0] - 1] > 0, ends[:, start + j : start + j + 1], 0.0)
                total = jnp.where(first == start, before, total)
        sums.append(total)
    sums.append(jnp.zeros_like(sums[0]))
    write_coefficient(old_ref, mask, first, windows(sums, per), times_out, plus_out)


def coefficient(kernel, scal, shares, old, mask_ext, other, *ends):
    factors = old.shape[0]
    tile = mask_ext.shape[1]
    rows = old.shape[1] // tile
    per = rows // shares
    specs = [pl.BlockSpec((factors, per * tile), lambda i, scal: (0, scal[0]))]
    specs += [vmem() for _ in range(2 + len(ends))]
    return kernel_call(
        functools.partial(kernel, mask_ext.shape[0] - rows),
        "coefficient",
        scal,
        [old, mask_ext, other, *ends],
        [jax.ShapeDtypeStruct((per, factors, tile), F32)] * 2,
        specs=specs,
    )


def update_kernel(scal, sums, times, plus, *refs):
    terms, out = refs[:-1], refs[-1]
    per, _, tile = times.shape
    c = mean_scale(sums[...])
    for t in range(per):
        numer = terms[0][t]
        for term in terms[1:]:
            numer = numer + term[t]
        out[:, t * tile : (t + 1) * tile] = times[t] * (numer * c * c) + plus[t]


def update(scal, sums, times, plus, terms):
    per, count, tile = terms[0].shape
    return kernel_call(
        update_kernel,
        "update",
        scal,
        [sums, times, plus, *terms],
        [jax.ShapeDtypeStruct((count, per * tile), F32)],
    )[0]


def xor_exchange(x, axis, k):
    return lax.ppermute(x, axis, [(i, i ^ k) for i in range(lax.axis_size(axis))])


def both_sides(x, even):
    size = lax.axis_size("genome")
    a = lax.ppermute(x, "genome", [(i, i ^ 1) for i in range(size)])
    b = lax.ppermute(x, "genome", [(i, (((i + 1) ^ 1) - 1) % size) for i in range(size)])
    return jnp.where(even > 0, a, b), jnp.where(even > 0, b, a)


def scatter_terms(pieces):
    size = lax.axis_size("offset")
    if size == 4:
        far = pieces[3] + xor_exchange(pieces[2], "offset", 1)
        far = xor_exchange(far, "offset", 3)
        return [pieces[0], xor_exchange(pieces[1], "offset", 1), far]
    return [pieces[0]] + [xor_exchange(pieces[k], "offset", k) for k in range(1, size)]


def per_device(counts, band_offset, bin_mask, row_factors, col_factors):
    rows, slots, tile = counts.shape[:3]
    factors = row_factors.shape[0]
    offset_count = lax.axis_size("offset")
    genome_count = lax.axis_size("genome")
    g = lax.axis_index("genome")
    o = lax.axis_index("offset").astype(jnp.int32)
    reach = slots * offset_count - 1
    pad = reach + 1

    line = jnp.broadcast_to(g, (1, tile))
    even = (line % 2 == 0).astype(F32)
    has_next = (line < genome_count - 1).astype(F32)
    has_prev = (line > 0).astype(F32)
    count = offset_count * -(-pad * offset_count // rows)
    index = lax.broadcasted_iota(jnp.int32, (count, tile), 0)
    share, k = index // offset_count, index % offset_count
    mine = (jnp.bitwise_xor(share, k) == o).astype(F32) * has_prev
    flags = jnp.concatenate([even, has_next, has_prev, mine])
    before = jnp.broadcast_to((g > 0).astype(jnp.int32), (1,))
    scal = jnp.concatenate([jnp.broadcast_to(o, (1,)), band_offset, before])
    flags, scal, bin_mask = lax.optimization_barrier((flags, scal, bin_mask))
    even, has_next, has_prev = flags[0:1], flags[1:2], flags[2:3]
    mine = flags[3:]

    mask = bin_mask.astype(F32).reshape(rows, tile)
    mask_next, _ = both_sides(mask[:pad], even)
    keep = lax.broadcasted_iota(jnp.int32, (pad, 1), 0) < reach
    mask_ext = jnp.concatenate([mask, jnp.where(keep, mask_next * has_next, 0.0)])

    counts = pltpu.with_memory_space_constraint(counts, pltpu.HBM)
    inner_v, kept = first_main(scal, counts, mask, rows + pad)
    col_late, _ = lax.optimization_barrier((col_factors, inner_v))
    ring_left = [(i, (i - 1) % genome_count) for i in range(genome_count)]
    col_next = lax.ppermute(col_late[:, : pad * tile], "genome", ring_left)
    col_ext = jnp.concatenate([col_factors, col_next], axis=1)

    scales = []
    quarter = rows // (ITERS + 1)
    for t in range(ITERS):
        if t == 0:
            u = mask_ext
            v, edge = first_edge(scal, kept, u, inner_v)
        else:
            v, edge, u = cover_edge(scal, kept, mask_ext, parts, ratios[0])
        scales.append(u)
        after, before = both_sides(edge, even)
        if t > 0:
            v = cover_main(scal, kept, u, v)
        else:
            *ratios, v = ratio(scal, kept, row_factors, col_factors, v, [], 0, 2 * quarter)
        front = v[:pad] + before[pad:] * has_prev
        back = v[rows:] + after[:pad] * has_next
        x = jnp.concatenate([front, v[pad:rows], back])
        others = {k: xor_exchange(x, "offset", k) for k in range(1, offset_count)}
        parts = [x, *others.values()]
        if t == 0:
            ratios = ratio(scal, kept, row_factors, col_factors, x, ratios, 2 * quarter, quarter)
        elif t == ITERS - 1:
            ratios = ratio(scal, kept, row_factors, col_ext, x, ratios, 3 * quarter, quarter)

    r_hi, r_lo = ratios
    per = rows // offset_count
    u, tail, early = numer_first(
        scal, r_hi, r_lo, row_factors, col_ext, mask_ext, parts, EARLY
    )
    scales.append(u)
    order = [EARLY, *(k for k in range(offset_count) if k != EARLY)]
    sums, pieces = numer_col(scal, r_hi, r_lo, row_factors, scales, order, offset_count)
    h_parts = dict(zip(order, pieces))

    right = [(i, (i + 1) % genome_count) for i in range(genome_count)]
    arrived = lax.ppermute(tail, "genome", right)
    for s in range(-(-pad // per)):
        piece = arrived[s * per : min(pad, (s + 1) * per)]
        for k in range(offset_count):
            at = s * offset_count + k
            h_parts[k] = h_parts[k].at[: piece.shape[0]].add(piece * mine[at : at + 1])

    row_terms = coefficient(
        row_coefficient_kernel, scal, offset_count, row_factors, mask_ext, col_ext
    )
    col_terms = coefficient(
        col_coefficient_kernel, scal, offset_count, col_factors, mask_ext, row_factors, arrived[pad]
    )
    order = [k for k in (3, 1, 0, *range(4, offset_count))]
    pieces = numer_row(scal, r_hi, r_lo, col_ext, u, h_parts[EARLY], order, offset_count)
    w_parts = dict(zip(order, pieces)) | {EARLY: early}
    w_terms = scatter_terms([w_parts[k] for k in range(offset_count)])
    h_terms = scatter_terms([h_parts[k] for k in range(offset_count)])

    sums, _ = lax.optimization_barrier((sums, w_terms[2]))
    sums = jnp.sum(lax.all_gather(sums, "genome"), axis=0)
    bias = (u[:rows] * mean_scale(sums)).reshape(-1)

    col_update = update(scal, sums, *col_terms, h_terms)
    row_update = update(scal, sums, *row_terms, w_terms)
    return bias, row_update, col_update


def solution(mesh):
    return jax.shard_map(
        per_device,
        mesh=mesh,
        in_specs=(
            P("genome", "offset", None, None),
            P("offset"),
            P("genome"),
            P(None, "genome"),
            P(None, "genome"),
        ),
        out_specs=(P("genome"), P(None, ("genome", "offset")), P(None, ("genome", "offset"))),
        check_vma=False,
    )
```

```python
import functools

import jax
import jax.numpy as jnp
from jax import lax
from jax.experimental import pallas as pl
from jax.experimental.pallas import tpu as pltpu
from jax.sharding import PartitionSpec as P

ITERS = 3
STEP = 8
EARLY = 2
F32 = jnp.float32
BF16 = jnp.bfloat16
VMEM_LIMIT = 20 * 1024 * 1024
NT = (((1,), (1,)), ((), ()))
TN = (((0,), (0,)), ((), ()))


def split(x):
    hi = x.astype(BF16)
    lo = (x - hi.astype(F32)).astype(BF16)
    return hi, lo


def tree_sum(parts):
    while len(parts) > 1:
        parts = [a + b for a, b in zip(parts[::2], parts[1::2])]
    return parts[0]


def params():
    return pltpu.CompilerParams(vmem_limit_bytes=VMEM_LIMIT)


def scale_from(mask, parts):
    cover = tree_sum([p[...] for p in parts[:1] + parts[:0:-1]])
    live = mask[...] > 0
    return jnp.where(live, 1.0 / jnp.where(live, cover, 1.0), 0.0)


def vmem():
    return pl.BlockSpec(memory_space=pltpu.VMEM)


def kernel_call(body, name, scalars, args, outs, scratch=(), aliases=None, specs=None):
    return pl.pallas_call(
        body,
        grid_spec=pltpu.PrefetchScalarGridSpec(
            num_scalar_prefetch=1,
            grid=(1,),
            in_specs=specs or [vmem() for _ in args],
            out_specs=[vmem() for _ in outs],
            scratch_shapes=list(scratch),
        ),
        out_shape=outs,
        input_output_aliases=aliases or {},
        compiler_params=params(),
        name=name,
    )(scalars, *args)


def offsets(scal, slots):
    return [scal[1 + s] for s in range(slots)]


def by_diagonal(offs, slots, go):
    for s in range(slots):

        @pl.when(offs[s] == 0)
        def _():
            go(s)

    @pl.when(functools.reduce(jnp.logical_and, [offs[s] != 0 for s in range(slots)]))
    def _():
        go(-1)


def tile_value(counts, i, s, diagonal):
    c = counts[i, s].astype(F32)
    if s == diagonal:
        tile = c.shape[0]
        r = lax.broadcasted_iota(jnp.int32, (tile, tile), 0)
        q = lax.broadcasted_iota(jnp.int32, (tile, tile), 1)
        c = jnp.where(r < q, c, jnp.where(r == q, 0.5 * c, 0.0))
    return c


def cover_block(offs, counts, u_ref, acc, base, diagonal, at, kept=None):
    slots, tile = counts.shape[1:3]
    ones = jnp.ones((8, tile), BF16)
    u_block = u_ref[pl.ds(base, STEP), :]
    u_cols = u_block.T
    u_across = [u_ref[pl.ds(base + offs[s], STEP), :] for s in range(slots)]
    cols = [[] for _ in range(slots)]
    sums = []
    for t in range(STEP):
        total = None
        for s in range(slots):
            c = tile_value(counts, at + t, s, diagonal)
            if kept is not None:
                kept[base + t, s] = c
            term = c * u_across[s][t : t + 1]
            total = term if total is None else total + term
            cols[s].append(jnp.sum(c * u_cols[:, t : t + 1], axis=0, keepdims=True))
        hi, lo = split(total)
        row = lax.dot_general(ones, hi, NT, preferred_element_type=F32)
        row = row + lax.dot_general(ones, lo, NT, preferred_element_type=F32)
        sums.append(row[:1])
    acc[pl.ds(base, STEP), :] += jnp.concatenate(sums, axis=0)
    for s in range(slots):
        acc[pl.ds(base + offs[s], STEP), :] += jnp.concatenate(cols[s], axis=0)


def block_copies(hbm, buffer, sems, bases):
    return [
        pltpu.make_async_copy(
            hbm.at[pl.ds(base, STEP)], buffer.at[pl.ds(k * STEP, STEP)], sems.at[k]
        )
        for k, base in enumerate(bases)
    ]


def edge_bases(rows, pad):
    return list(range(0, pad, STEP)) + list(range(rows - pad, rows, STEP))


def write_edge(v_out, edge_out, rows):
    pad = v_out.shape[0] - rows
    edge_out[:pad] = v_out[:pad]
    edge_out[pad:] = v_out[rows:]


def first_main_kernel(scal, hbm, mask, v_out, kept, buffer, sems):
    rows, slots = hbm.shape[:2]
    offs = offsets(scal, slots)
    pad = v_out.shape[0] - rows
    inner = list(range(pad, rows - pad, STEP))
    bases = inner + edge_bases(rows, pad)
    copies = block_copies(hbm, buffer, sems, bases)
    for copy in copies:
        copy.start()
    v_out[...] = jnp.zeros_like(v_out)

    def go(diagonal):
        for k, base in enumerate(bases):
            copies[k].wait()
            at = k * STEP
            if base in inner:
                cover_block(offs, buffer, mask, v_out, base, diagonal, at, kept)
            else:
                for t in range(STEP):
                    for s in range(slots):
                        kept[base + t, s] = tile_value(buffer, at + t, s, diagonal)

    by_diagonal(offs, slots, go)


def first_edge_kernel(scal, kept, u_ref, inner_v, v_out, edge_out):
    rows, slots = kept.shape[:2]
    offs = offsets(scal, slots)
    v_out[...] = inner_v[...]
    for base in edge_bases(rows, u_ref.shape[0] - rows):
        cover_block(offs, kept, u_ref, v_out, base, -1, base)
    write_edge(v_out, edge_out, rows)


def edge_kernel(scal, kept, mask, *refs):
    v_out, edge_out, u_out = refs[-3:]
    rows, slots = kept.shape[:2]
    offs = offsets(scal, slots)
    u_out[...] = scale_from(mask, refs[:-4])
    v_out[...] = jnp.zeros_like(v_out)
    for base in edge_bases(rows, mask.shape[0] - rows):
        cover_block(offs, kept, u_out, v_out, base, -1, base)
    write_edge(v_out, edge_out, rows)


def main_kernel(scal, kept, u_ref, edge_v, v_out):
    rows, slots = kept.shape[:2]
    offs = offsets(scal, slots)
    pad = edge_v.shape[0] - rows
    v_out[...] = edge_v[...]
    for base in range(pad, rows - pad, STEP):
        cover_block(offs, kept, u_ref, v_out, base, -1, base)


def first_main(scal, counts, mask, ext):
    rows, slots, tile = counts.shape[:3]
    outs = [jax.ShapeDtypeStruct((ext, tile), F32), pltpu.VMEM(counts.shape, F32)]
    return kernel_call(
        first_main_kernel,
        "first_main",
        scal,
        [counts, mask],
        outs,
        [pltpu.VMEM(counts.shape, counts.dtype), pltpu.SemaphoreType.DMA((rows // STEP,))],
        specs=[pl.BlockSpec(memory_space=pltpu.HBM), vmem()],
    )


def first_edge(scal, kept, u, inner_v):
    rows, tile = kept.shape[0], kept.shape[2]
    flat = jax.ShapeDtypeStruct(u.shape, F32)
    edge = jax.ShapeDtypeStruct((2 * (u.shape[0] - rows), tile), F32)
    return kernel_call(first_edge_kernel, "first_edge", scal, [kept, u, inner_v], [flat, edge])


def cover_edge(scal, kept, mask_ext, parts, after):
    rows, tile = kept.shape[0], kept.shape[2]
    flat = jax.ShapeDtypeStruct(mask_ext.shape, F32)
    edge = jax.ShapeDtypeStruct((2 * (mask_ext.shape[0] - rows), tile), F32)
    args = [kept, mask_ext, *parts, after]
    return kernel_call(edge_kernel, "cover_edge", scal, args, [flat, edge, flat])


def cover_main(scal, kept, u, edge_v):
    outs = [jax.ShapeDtypeStruct(u.shape, F32)]
    return kernel_call(main_kernel, "cover_main", scal, [kept, u, edge_v], outs)[0]


def ratio_kernel(start, count, pad, scal, kept, w_ref, h_ref, after, *refs):
    slots, tile = kept.shape[1:3]
    offs = offsets(scal, slots)
    if start == 0:
        hi_out, lo_out, same, h_terms = refs
        same[...] = after[...]
    else:
        hi_out, lo_out, h_terms = refs[-3:]

    def prepare(j, carry):
        hi, lo = split(h_ref[:, pl.ds(pl.multiple_of(j * tile, tile), tile)])
        h_terms[j - start] = jnp.concatenate([hi, lo, hi, lo], axis=0)
        return carry

    lax.fori_loop(start, start + count + pad, prepare, 0, unroll=4)

    def go(diagonal):
        def body(i, carry):
            hi, lo = split(w_ref[:, pl.ds(pl.multiple_of(i * tile, tile), tile)])
            w_terms = jnp.concatenate([hi, hi, lo, lo], axis=0)
            for s in range(slots):
                model = lax.dot_general(
                    w_terms, h_terms[i - start + offs[s]], TN, preferred_element_type=F32
                )
                values = kept[i, s]
                if s == diagonal:
                    values = values + values.T
                r_hi, r_lo = split(values * (1.0 / model))
                hi_out[i, :, s * tile : (s + 1) * tile] = r_hi
                lo_out[i, :, s * tile : (s + 1) * tile] = r_lo
            return carry

        lax.fori_loop(start, start + count, body, 0, unroll=8)

    by_diagonal(offs, slots, go)


def ratio(scal, kept, row_factors, col_ext, after, earlier, start, count):
    rows, slots, tile = kept.shape[:3]
    factors = row_factors.shape[0]
    pad = after.shape[0] - rows
    out = pltpu.VMEM((rows, tile, slots * tile), BF16)
    return kernel_call(
        functools.partial(ratio_kernel, start, count, pad),
        "ratio",
        scal,
        [kept, row_factors, col_ext, after, *earlier],
        [out, out] + [jax.ShapeDtypeStruct(after.shape, F32)] * (start == 0),
        [pltpu.VMEM((count + pad, 4 * factors, tile), BF16)],
        {5: 0, 6: 1} if earlier else {},
    )


def row_numer(offs, g_all, hi_ref, lo_ref, u_ref, i):
    slots = hi_ref.shape[2] // g_all.shape[2]
    factors = g_all.shape[1] // 2
    g = jnp.concatenate([g_all[i + offs[s]] for s in range(slots)], axis=1)
    big = lax.dot_general(g, hi_ref[i], NT, preferred_element_type=F32)
    small = lax.dot_general(g[:factors], lo_ref[i], NT, preferred_element_type=F32)
    return (big[:factors] + big[factors:] + small) * u_ref[pl.ds(i, 1), :]


def col_numer(w_ref, hi_ref, lo_ref, u_ref, i):
    tile = u_ref.shape[1]
    factors = w_ref.shape[0]
    w = w_ref[:, pl.ds(pl.multiple_of(i * tile, tile), tile)]
    hi, lo = split(w * u_ref[pl.ds(i, 1), :])
    big = jnp.dot(jnp.concatenate([hi, lo], axis=0), hi_ref[i], preferred_element_type=F32)
    small = jnp.dot(hi, lo_ref[i], preferred_element_type=F32)
    return big[:factors] + big[factors:] + small


def col_loop(offs, w_ref, hi_ref, lo_ref, u_ref, acc, start, count, shift):
    tile = u_ref.shape[1]

    def body(n, carry):
        i = start + n
        cols = col_numer(w_ref, hi_ref, lo_ref, u_ref, i)
        for s in range(hi_ref.shape[2] // tile):
            acc[i + offs[s] - shift] += cols[:, s * tile : (s + 1) * tile]
        return carry

    lax.fori_loop(0, count, body, 0, unroll=8)


def row_pieces(scal, offs, g_ref, hi_ref, lo_ref, u_ref, order, outs):
    for k, out in zip(order, outs):
        per = out.shape[0]
        first = jnp.bitwise_xor(scal[0], k) * per

        def body(t, carry):
            out[t] = row_numer(offs, g_ref, hi_ref, lo_ref, u_ref, first + t)
            return carry

        lax.fori_loop(0, per, body, 0, unroll=4)


def scaled_terms(h_ref, u_ref, terms, start, count):
    tile = u_ref.shape[1]
    factors = h_ref.shape[0]

    def fill(n, carry):
        j = start + n
        x = h_ref[:, pl.ds(pl.multiple_of(j * tile, tile), tile)] * u_ref[pl.ds(j, 1), :]
        hi, lo = split(x)
        terms[j, :factors] = hi
        terms[j, factors:] = lo
        return carry

    lax.fori_loop(0, count, fill, 0, unroll=4)


def numer_first_kernel(k, shares, scal, hi_ref, lo_ref, w_ref, h_ref, mask, *refs):
    parts = refs[:shares]
    u_out, tail_out, out, acc, terms = refs[shares:]
    rows = hi_ref.shape[0]
    ext, tile = mask.shape
    offs = offsets(scal, hi_ref.shape[2] // tile)
    per = rows // shares
    pad = ext - rows
    u_out[...] = scale_from(mask, parts)

    acc[...] = jnp.zeros_like(acc)
    col_loop(offs, w_ref, hi_ref, lo_ref, u_out, acc, rows - pad, pad, rows - pad)
    for t in range(pad):
        tail_out[t] = acc[pad + t] * u_out[rows + t : rows + t + 1, :]
    lane = lax.broadcasted_iota(jnp.int32, tail_out.shape[1:], 1)
    ends = jnp.zeros(tail_out.shape[1:], F32)
    for t in range(pad):
        ends = jnp.where(lane == t, tile_sum(w_ref, mask, rows - pad + t), ends)
    tail_out[pad] = ends

    first = jnp.bitwise_xor(scal[0], k) * per
    scaled_terms(h_ref, u_out, terms, first, per + pad)
    row_pieces(scal, offs, terms, hi_ref, lo_ref, u_out, [k], [out])


def numer_col_kernel(order, scal, hi_ref, lo_ref, w_ref, *refs):
    scales, refs = refs[: ITERS + 1], refs[ITERS + 1 :]
    sums_out, outs, acc = refs[0], refs[1:-1], refs[-1]
    u_ref = scales[-1]
    rows = hi_ref.shape[0]
    tile = u_ref.shape[1]
    offs = offsets(scal, hi_ref.shape[2] // tile)
    per = outs[0].shape[0]
    acc[...] = jnp.zeros_like(acc)
    col_loop(offs, w_ref, hi_ref, lo_ref, u_ref, acc, 0, rows, 0)
    for k, out in zip(order, outs):
        first = jnp.bitwise_xor(scal[0], k) * per

        def body(t, carry):
            out[t] = acc[first + t] * u_ref[pl.ds(first + t, 1), :]
            return carry

        lax.fori_loop(0, per, body, 0, unroll=4)
    write_sums(sums_out, scales, rows)


def write_sums(sums_out, scales, rows):
    sums_out[...] = jnp.zeros_like(sums_out)
    mask = scales[0][:rows]
    totals = [mask]
    for t in range(ITERS):
        below = jnp.where(mask > 0, scales[t + 1][:rows], 1.0)
        totals.append(jnp.where(mask > 0, scales[t][:rows] / below, 0.0))
    for t, total in enumerate(totals):
        line = jnp.sum(jnp.sum(total, axis=0, keepdims=True), axis=1, keepdims=True)
        sums_out[t : t + 1, :] = jnp.broadcast_to(line, (1, mask.shape[1]))


def numer_row_kernel(order, scal, hi_ref, lo_ref, h_ref, u_ref, after, *refs):
    outs, terms = refs[:-1], refs[-1]
    ext, tile = u_ref.shape
    offs = offsets(scal, hi_ref.shape[2] // tile)
    scaled_terms(h_ref, u_ref, terms, 0, ext)
    row_pieces(scal, offs, terms, hi_ref, lo_ref, u_ref, order, outs)


def numer_first(scal, r_hi, r_lo, row_factors, col_ext, mask_ext, parts, k):
    shares = len(parts)
    rows, tile = r_hi.shape[:2]
    factors = row_factors.shape[0]
    ext = mask_ext.shape[0]
    pad = ext - rows
    per = rows // shares
    return kernel_call(
        functools.partial(numer_first_kernel, k, shares),
        "numer_first",
        scal,
        [r_hi, r_lo, row_factors, col_ext, mask_ext, *parts],
        [
            jax.ShapeDtypeStruct((ext, tile), F32),
            jax.ShapeDtypeStruct((pad + 1, factors, tile), F32),
            jax.ShapeDtypeStruct((per, factors, tile), F32),
        ],
        [
            pltpu.VMEM((2 * pad, factors, tile), F32),
            pltpu.VMEM((ext, 2 * factors, tile), BF16),
        ],
    )


def numer_col(scal, r_hi, r_lo, row_factors, scales, order, shares):
    rows, tile = r_hi.shape[:2]
    factors = row_factors.shape[0]
    piece = jax.ShapeDtypeStruct((rows // shares, factors, tile), F32)
    res = kernel_call(
        functools.partial(numer_col_kernel, order),
        "numer_col",
        scal,
        [r_hi, r_lo, row_factors, *scales],
        [jax.ShapeDtypeStruct((8, tile), F32)] + [piece] * len(order),
        [pltpu.VMEM((scales[0].shape[0], factors, tile), F32)],
    )
    return res[0], res[1:]


def numer_row(scal, r_hi, r_lo, col_ext, u, after, order, shares):
    rows, tile = r_hi.shape[:2]
    factors = col_ext.shape[0]
    piece = jax.ShapeDtypeStruct((rows // shares, factors, tile), F32)
    return kernel_call(
        functools.partial(numer_row_kernel, order),
        "numer_row",
        scal,
        [r_hi, r_lo, col_ext, u, after],
        [piece] * len(order),
        [pltpu.VMEM((u.shape[0], 2 * factors, tile), BF16)],
    )


def mean_scale(sums):
    scale = sums[1:2, :] / sums[0:1, :]
    for t in range(1, ITERS):
        scale = scale * (sums[t + 1 : t + 2, :] / sums[0:1, :])
    return scale


def tile_sum(factor_ref, mask, j):
    tile = mask.shape[1]
    x = factor_ref[:, pl.ds(pl.multiple_of(j * tile, tile), tile)] * mask[pl.ds(j, 1), :]
    return jnp.sum(x, axis=1, keepdims=True)


def windows(sums, per):
    return [tree_sum(sums[t : t + len(sums) - per]) for t in range(per)]


def write_coefficient(old_ref, mask, first, lowers, times_out, plus_out):
    tile = mask.shape[1]
    for t, lower in enumerate(lowers):
        live = mask[pl.ds(first + t, 1), :]
        old = old_ref[:, t * tile : (t + 1) * tile]
        times_out[t] = jnp.where(live > 0, old / jnp.where(live > 0, lower * live, 1.0), 0.0)
        plus_out[t] = jnp.where(live > 0, 0.0, old)


def row_coefficient_kernel(pad, scal, old_ref, mask, other, times_out, plus_out):
    per = times_out.shape[0]
    first = scal[0] * per
    sums = [tile_sum(other, mask, first + t) for t in range(per + pad)]
    write_coefficient(old_ref, mask, first, windows(sums, per), times_out, plus_out)


def col_coefficient_kernel(pad, scal, old_ref, mask, other, ends, times_out, plus_out):
    per = times_out.shape[0]
    first = scal[0] * per
    sums = []
    for j in range(1, per + pad):
        total = tile_sum(other, mask, jnp.maximum(first - pad + j, 0))
        for start in range(0, pad, per):
            if start + j < pad:
                before = jnp.where(scal[scal.shape[0] - 1] > 0, ends[:, start + j : start + j + 1], 0.0)
                total = jnp.where(first == start, before, total)
        sums.append(total)
    sums.append(jnp.zeros_like(sums[0]))
    write_coefficient(old_ref, mask, first, windows(sums, per), times_out, plus_out)


def coefficient(kernel, scal, shares, old, mask_ext, other, *ends):
    factors = old.shape[0]
    tile = mask_ext.shape[1]
    rows = old.shape[1] // tile
    per = rows // shares
    specs = [pl.BlockSpec((factors, per * tile), lambda i, scal: (0, scal[0]))]
    specs += [vmem() for _ in range(2 + len(ends))]
    return kernel_call(
        functools.partial(kernel, mask_ext.shape[0] - rows),
        "coefficient",
        scal,
        [old, mask_ext, other, *ends],
        [jax.ShapeDtypeStruct((per, factors, tile), F32)] * 2,
        specs=specs,
    )


def update_kernel(scal, sums, times, plus, *refs):
    terms, out = refs[:-1], refs[-1]
    per, _, tile = times.shape
    c = mean_scale(sums[...])
    for t in range(per):
        numer = terms[0][t]
        for term in terms[1:]:
            numer = numer + term[t]
        out[:, t * tile : (t + 1) * tile] = times[t] * (numer * c * c) + plus[t]


def update(scal, sums, times, plus, terms):
    per, count, tile = terms[0].shape
    return kernel_call(
        update_kernel,
        "update",
        scal,
        [sums, times, plus, *terms],
        [jax.ShapeDtypeStruct((count, per * tile), F32)],
    )[0]


def xor_exchange(x, axis, k):
    return lax.ppermute(x, axis, [(i, i ^ k) for i in range(lax.axis_size(axis))])


def both_sides(x, even):
    size = lax.axis_size("genome")
    a = lax.ppermute(x, "genome", [(i, i ^ 1) for i in range(size)])
    b = lax.ppermute(x, "genome", [(i, (((i + 1) ^ 1) - 1) % size) for i in range(size)])
    return jnp.where(even > 0, a, b), jnp.where(even > 0, b, a)


def scatter_terms(pieces):
    size = lax.axis_size("offset")
    if size == 4:
        far = pieces[3] + xor_exchange(pieces[2], "offset", 1)
        far = xor_exchange(far, "offset", 3)
        return [pieces[0], xor_exchange(pieces[1], "offset", 1), far]
    return [pieces[0]] + [xor_exchange(pieces[k], "offset", k) for k in range(1, size)]


def per_device(counts, band_offset, bin_mask, row_factors, col_factors):
    rows, slots, tile = counts.shape[:3]
    factors = row_factors.shape[0]
    offset_count = lax.axis_size("offset")
    genome_count = lax.axis_size("genome")
    g = lax.axis_index("genome")
    o = lax.axis_index("offset").astype(jnp.int32)
    reach = slots * offset_count - 1
    pad = reach + 1

    line = jnp.broadcast_to(g, (1, tile))
    even = (line % 2 == 0).astype(F32)
    has_next = (line < genome_count - 1).astype(F32)
    has_prev = (line > 0).astype(F32)
    count = offset_count * -(-pad * offset_count // rows)
    index = lax.broadcasted_iota(jnp.int32, (count, tile), 0)
    share, k = index // offset_count, index % offset_count
    mine = (jnp.bitwise_xor(share, k) == o).astype(F32) * has_prev
    flags = jnp.concatenate([even, has_next, has_prev, mine])
    before = jnp.broadcast_to((g > 0).astype(jnp.int32), (1,))
    scal = jnp.concatenate([jnp.broadcast_to(o, (1,)), band_offset, before])
    flags, scal, bin_mask = lax.optimization_barrier((flags, scal, bin_mask))
    even, has_next, has_prev = flags[0:1], flags[1:2], flags[2:3]
    mine = flags[3:]

    mask = bin_mask.astype(F32).reshape(rows, tile)
    mask_next, _ = both_sides(mask[:pad], even)
    keep = lax.broadcasted_iota(jnp.int32, (pad, 1), 0) < reach
    mask_ext = jnp.concatenate([mask, jnp.where(keep, mask_next * has_next, 0.0)])

    counts = pltpu.with_memory_space_constraint(counts, pltpu.HBM)
    inner_v, kept = first_main(scal, counts, mask, rows + pad)
    col_late, _ = lax.optimization_barrier((col_factors, inner_v))
    ring_left = [(i, (i - 1) % genome_count) for i in range(genome_count)]
    col_next = lax.ppermute(col_late[:, : pad * tile], "genome", ring_left)
    col_ext = jnp.concatenate([col_factors, col_next], axis=1)

    scales = []
    quarter = rows // (ITERS + 1)
    for t in range(ITERS):
        if t == 0:
            u = mask_ext
            v, edge = first_edge(scal, kept, u, inner_v)
        else:
            v, edge, u = cover_edge(scal, kept, mask_ext, parts, ratios[0])
        scales.append(u)
        after, before = both_sides(edge, even)
        if t > 0:
            v = cover_main(scal, kept, u, v)
        else:
            *ratios, v = ratio(scal, kept, row_factors, col_factors, v, [], 0, 2 * quarter)
        front = v[:pad] + before[pad:] * has_prev
        back = v[rows:] + after[:pad] * has_next
        x = jnp.concatenate([front, v[pad:rows], back])
        others = {k: xor_exchange(x, "offset", k) for k in reversed(range(1, offset_count))}
        parts = [x, *others.values()]
        if t == 0:
            ratios = ratio(scal, kept, row_factors, col_factors, x, ratios, 2 * quarter, quarter)
        elif t == ITERS - 1:
            ratios = ratio(scal, kept, row_factors, col_ext, x, ratios, 3 * quarter, quarter)

    r_hi, r_lo = ratios
    per = rows // offset_count
    u, tail, early = numer_first(
        scal, r_hi, r_lo, row_factors, col_ext, mask_ext, parts, EARLY
    )
    scales.append(u)
    order = [EARLY, *(k for k in range(offset_count) if k != EARLY)]
    sums, pieces = numer_col(scal, r_hi, r_lo, row_factors, scales, order, offset_count)
    h_parts = dict(zip(order, pieces))

    right = [(i, (i + 1) % genome_count) for i in range(genome_count)]
    arrived = lax.ppermute(tail, "genome", right)
    for s in range(-(-pad // per)):
        piece = arrived[s * per : min(pad, (s + 1) * per)]
        for k in range(offset_count):
            at = s * offset_count + k
            h_parts[k] = h_parts[k].at[: piece.shape[0]].add(piece * mine[at : at + 1])

    row_terms = coefficient(
        row_coefficient_kernel, scal, offset_count, row_factors, mask_ext, col_ext
    )
    col_terms = coefficient(
        col_coefficient_kernel, scal, offset_count, col_factors, mask_ext, row_factors, arrived[pad]
    )
    order = [k for k in (3, 1, 0, *range(4, offset_count))]
    pieces = numer_row(scal, r_hi, r_lo, col_ext, u, h_parts[EARLY], order, offset_count)
    w_parts = dict(zip(order, pieces)) | {EARLY: early}
    w_terms = scatter_terms([w_parts[k] for k in range(offset_count)])
    h_terms = scatter_terms([h_parts[k] for k in range(offset_count)])

    sums, _ = lax.optimization_barrier((sums, w_terms[2]))
    sums = jnp.sum(lax.all_gather(sums, "genome"), axis=0)
    bias = (u[:rows] * mean_scale(sums)).reshape(-1)

    col_update = update(scal, sums, *col_terms, h_terms)
    row_update = update(scal, sums, *row_terms, w_terms)
    return bias, row_update, col_update


def solution(mesh):
    return jax.shard_map(
        per_device,
        mesh=mesh,
        in_specs=(
            P("genome", "offset", None, None),
            P("offset"),
            P("genome"),
            P(None, "genome"),
            P(None, "genome"),
        ),
        out_specs=(P("genome"), P(None, ("genome", "offset")), P(None, ("genome", "offset"))),
        check_vma=False,
    )
```

```python
import functools

import jax
import jax.numpy as jnp
from jax import lax
from jax.experimental import pallas as pl
from jax.experimental.pallas import tpu as pltpu
from jax.sharding import PartitionSpec as P

ITERS = 3
STEP = 8
EARLY = 2
F32 = jnp.float32
BF16 = jnp.bfloat16
VMEM_LIMIT = 20 * 1024 * 1024
NT = (((1,), (1,)), ((), ()))
TN = (((0,), (0,)), ((), ()))


def split(x):
    hi = x.astype(BF16)
    lo = (x - hi.astype(F32)).astype(BF16)
    return hi, lo


def tree_sum(parts):
    while len(parts) > 1:
        parts = [a + b for a, b in zip(parts[::2], parts[1::2])]
    return parts[0]


def params():
    return pltpu.CompilerParams(vmem_limit_bytes=VMEM_LIMIT)


def scale_from(mask, parts):
    cover = tree_sum([p[...] for p in parts[:1] + parts[:0:-1]])
    live = mask[...] > 0
    return jnp.where(live, 1.0 / jnp.where(live, cover, 1.0), 0.0)


def vmem():
    return pl.BlockSpec(memory_space=pltpu.VMEM)


def kernel_call(body, name, scalars, args, outs, scratch=(), aliases=None, specs=None):
    return pl.pallas_call(
        body,
        grid_spec=pltpu.PrefetchScalarGridSpec(
            num_scalar_prefetch=1,
            grid=(1,),
            in_specs=specs or [vmem() for _ in args],
            out_specs=[vmem() for _ in outs],
            scratch_shapes=list(scratch),
        ),
        out_shape=outs,
        input_output_aliases=aliases or {},
        compiler_params=params(),
        name=name,
    )(scalars, *args)


def offsets(scal, slots):
    return [scal[1 + s] for s in range(slots)]


def by_diagonal(offs, slots, go):
    for s in range(slots):

        @pl.when(offs[s] == 0)
        def _():
            go(s)

    @pl.when(functools.reduce(jnp.logical_and, [offs[s] != 0 for s in range(slots)]))
    def _():
        go(-1)


def tile_value(counts, i, s, diagonal):
    c = counts[i, s].astype(F32)
    if s == diagonal:
        tile = c.shape[0]
        r = lax.broadcasted_iota(jnp.int32, (tile, tile), 0)
        q = lax.broadcasted_iota(jnp.int32, (tile, tile), 1)
        c = jnp.where(r < q, c, jnp.where(r == q, 0.5 * c, 0.0))
    return c


def cover_block(offs, counts, u_ref, acc, base, diagonal, at, kept=None):
    slots, tile = counts.shape[1:3]
    ones = jnp.ones((8, tile), BF16)
    u_block = u_ref[pl.ds(base, STEP), :]
    u_cols = u_block.T
    u_across = [u_ref[pl.ds(base + offs[s], STEP), :] for s in range(slots)]
    cols = [[] for _ in range(slots)]
    sums = []
    for t in range(STEP):
        total = None
        for s in range(slots):
            c = tile_value(counts, at + t, s, diagonal)
            if kept is not None:
                kept[base + t, s] = c
            term = c * u_across[s][t : t + 1]
            total = term if total is None else total + term
            cols[s].append(jnp.sum(c * u_cols[:, t : t + 1], axis=0, keepdims=True))
        hi, lo = split(total)
        row = lax.dot_general(ones, hi, NT, preferred_element_type=F32)
        row = row + lax.dot_general(ones, lo, NT, preferred_element_type=F32)
        sums.append(row[:1])
    acc[pl.ds(base, STEP), :] += jnp.concatenate(sums, axis=0)
    for s in range(slots):
        acc[pl.ds(base + offs[s], STEP), :] += jnp.concatenate(cols[s], axis=0)


def block_copies(hbm, buffer, sems, bases):
    return [
        pltpu.make_async_copy(
            hbm.at[pl.ds(base, STEP)], buffer.at[pl.ds(k * STEP, STEP)], sems.at[k]
        )
        for k, base in enumerate(bases)
    ]


def edge_bases(rows, pad):
    return list(range(0, pad, STEP)) + list(range(rows - pad, rows, STEP))


def write_edge(v_out, edge_out, rows):
    pad = v_out.shape[0] - rows
    edge_out[:pad] = v_out[:pad]
    edge_out[pad:] = v_out[rows:]


def first_main_kernel(scal, hbm, mask, v_out, kept, buffer, sems):
    rows, slots = hbm.shape[:2]
    offs = offsets(scal, slots)
    pad = v_out.shape[0] - rows
    inner = list(range(pad, rows - pad, STEP))
    bases = inner + edge_bases(rows, pad)
    copies = block_copies(hbm, buffer, sems, bases)
    for copy in copies:
        copy.start()
    v_out[...] = jnp.zeros_like(v_out)

    def go(diagonal):
        for k, base in enumerate(bases):
            copies[k].wait()
            at = k * STEP
            if base in inner:
                cover_block(offs, buffer, mask, v_out, base, diagonal, at, kept)
            else:
                for t in range(STEP):
                    for s in range(slots):
                        kept[base + t, s] = tile_value(buffer, at + t, s, diagonal)

    by_diagonal(offs, slots, go)


def first_edge_kernel(scal, kept, u_ref, inner_v, v_out, edge_out):
    rows, slots = kept.shape[:2]
    offs = offsets(scal, slots)
    v_out[...] = inner_v[...]
    for base in edge_bases(rows, u_ref.shape[0] - rows):
        cover_block(offs, kept, u_ref, v_out, base, -1, base)
    write_edge(v_out, edge_out, rows)


def edge_kernel(scal, kept, mask, *refs):
    v_out, edge_out, u_out = refs[-3:]
    rows, slots = kept.shape[:2]
    offs = offsets(scal, slots)
    u_out[...] = scale_from(mask, refs[:-4])
    v_out[...] = jnp.zeros_like(v_out)
    for base in edge_bases(rows, mask.shape[0] - rows):
        cover_block(offs, kept, u_out, v_out, base, -1, base)
    write_edge(v_out, edge_out, rows)


def main_kernel(scal, kept, u_ref, edge_v, v_out):
    rows, slots = kept.shape[:2]
    offs = offsets(scal, slots)
    pad = edge_v.shape[0] - rows
    v_out[...] = edge_v[...]
    for base in range(pad, rows - pad, STEP):
        cover_block(offs, kept, u_ref, v_out, base, -1, base)


def first_main(scal, counts, mask, ext):
    rows, slots, tile = counts.shape[:3]
    outs = [jax.ShapeDtypeStruct((ext, tile), F32), pltpu.VMEM(counts.shape, F32)]
    return kernel_call(
        first_main_kernel,
        "first_main",
        scal,
        [counts, mask],
        outs,
        [pltpu.VMEM(counts.shape, counts.dtype), pltpu.SemaphoreType.DMA((rows // STEP,))],
        specs=[pl.BlockSpec(memory_space=pltpu.HBM), vmem()],
    )


def first_edge(scal, kept, u, inner_v):
    rows, tile = kept.shape[0], kept.shape[2]
    flat = jax.ShapeDtypeStruct(u.shape, F32)
    edge = jax.ShapeDtypeStruct((2 * (u.shape[0] - rows), tile), F32)
    return kernel_call(first_edge_kernel, "first_edge", scal, [kept, u, inner_v], [flat, edge])


def cover_edge(scal, kept, mask_ext, parts, after):
    rows, tile = kept.shape[0], kept.shape[2]
    flat = jax.ShapeDtypeStruct(mask_ext.shape, F32)
    edge = jax.ShapeDtypeStruct((2 * (mask_ext.shape[0] - rows), tile), F32)
    args = [kept, mask_ext, *parts, after]
    return kernel_call(edge_kernel, "cover_edge", scal, args, [flat, edge, flat])


def cover_main(scal, kept, u, edge_v):
    outs = [jax.ShapeDtypeStruct(u.shape, F32)]
    return kernel_call(main_kernel, "cover_main", scal, [kept, u, edge_v], outs)[0]


def ratio_kernel(start, count, pad, scal, kept, w_ref, h_ref, after, *refs):
    slots, tile = kept.shape[1:3]
    offs = offsets(scal, slots)
    if start == 0:
        hi_out, lo_out, same, h_terms = refs
        same[...] = after[...]
    else:
        hi_out, lo_out, h_terms = refs[-3:]

    def prepare(j, carry):
        hi, lo = split(h_ref[:, pl.ds(pl.multiple_of(j * tile, tile), tile)])
        h_terms[j - start] = jnp.concatenate([hi, lo, hi, lo], axis=0)
        return carry

    lax.fori_loop(start, start + count + pad, prepare, 0, unroll=4)

    def go(diagonal):
        def body(i, carry):
            hi, lo = split(w_ref[:, pl.ds(pl.multiple_of(i * tile, tile), tile)])
            w_terms = jnp.concatenate([hi, hi, lo, lo], axis=0)
            for s in range(slots):
                model = lax.dot_general(
                    w_terms, h_terms[i - start + offs[s]], TN, preferred_element_type=F32
                )
                values = kept[i, s]
                if s == diagonal:
                    values = values + values.T
                r_hi, r_lo = split(values * (1.0 / model))
                hi_out[i, :, s * tile : (s + 1) * tile] = r_hi
                lo_out[i, :, s * tile : (s + 1) * tile] = r_lo
            return carry

        lax.fori_loop(start, start + count, body, 0, unroll=8)

    by_diagonal(offs, slots, go)


def ratio(scal, kept, row_factors, col_ext, after, earlier, start, count):
    rows, slots, tile = kept.shape[:3]
    factors = row_factors.shape[0]
    pad = after.shape[0] - rows
    out = pltpu.VMEM((rows, tile, slots * tile), BF16)
    return kernel_call(
        functools.partial(ratio_kernel, start, count, pad),
        "ratio",
        scal,
        [kept, row_factors, col_ext, after, *earlier],
        [out, out] + [jax.ShapeDtypeStruct(after.shape, F32)] * (start == 0),
        [pltpu.VMEM((count + pad, 4 * factors, tile), BF16)],
        {5: 0, 6: 1} if earlier else {},
    )


def row_numer(offs, g_all, hi_ref, lo_ref, u_ref, i):
    slots = hi_ref.shape[2] // g_all.shape[2]
    factors = g_all.shape[1] // 2
    g = jnp.concatenate([g_all[i + offs[s]] for s in range(slots)], axis=1)
    big = lax.dot_general(g, hi_ref[i], NT, preferred_element_type=F32)
    small = lax.dot_general(g[:factors], lo_ref[i], NT, preferred_element_type=F32)
    return (big[:factors] + big[factors:] + small) * u_ref[pl.ds(i, 1), :]


def col_numer(w_ref, hi_ref, lo_ref, u_ref, i):
    tile = u_ref.shape[1]
    factors = w_ref.shape[0]
    w = w_ref[:, pl.ds(pl.multiple_of(i * tile, tile), tile)]
    hi, lo = split(w * u_ref[pl.ds(i, 1), :])
    big = jnp.dot(jnp.concatenate([hi, lo], axis=0), hi_ref[i], preferred_element_type=F32)
    small = jnp.dot(hi, lo_ref[i], preferred_element_type=F32)
    return big[:factors] + big[factors:] + small


def col_loop(offs, w_ref, hi_ref, lo_ref, u_ref, acc, start, count, shift):
    tile = u_ref.shape[1]

    def body(n, carry):
        i = start + n
        cols = col_numer(w_ref, hi_ref, lo_ref, u_ref, i)
        for s in range(hi_ref.shape[2] // tile):
            acc[i + offs[s] - shift] += cols[:, s * tile : (s + 1) * tile]
        return carry

    lax.fori_loop(0, count, body, 0, unroll=8)


def row_pieces(scal, offs, g_ref, hi_ref, lo_ref, u_ref, order, outs):
    for k, out in zip(order, outs):
        per = out.shape[0]
        first = jnp.bitwise_xor(scal[0], k) * per

        def body(t, carry):
            out[t] = row_numer(offs, g_ref, hi_ref, lo_ref, u_ref, first + t)
            return carry

        lax.fori_loop(0, per, body, 0, unroll=8)


def scaled_terms(h_ref, u_ref, terms, start, count):
    tile = u_ref.shape[1]
    factors = h_ref.shape[0]

    def fill(n, carry):
        j = start + n
        x = h_ref[:, pl.ds(pl.multiple_of(j * tile, tile), tile)] * u_ref[pl.ds(j, 1), :]
        hi, lo = split(x)
        terms[j, :factors] = hi
        terms[j, factors:] = lo
        return carry

    lax.fori_loop(0, count, fill, 0, unroll=4)


def numer_first_kernel(k, shares, scal, hi_ref, lo_ref, w_ref, h_ref, mask, *refs):
    parts = refs[:shares]
    u_out, tail_out, out, acc, terms = refs[shares:]
    rows = hi_ref.shape[0]
    ext, tile = mask.shape
    offs = offsets(scal, hi_ref.shape[2] // tile)
    per = rows // shares
    pad = ext - rows
    u_out[...] = scale_from(mask, parts)

    acc[...] = jnp.zeros_like(acc)
    col_loop(offs, w_ref, hi_ref, lo_ref, u_out, acc, rows - pad, pad, rows - pad)
    for t in range(pad):
        tail_out[t] = acc[pad + t] * u_out[rows + t : rows + t + 1, :]
    lane = lax.broadcasted_iota(jnp.int32, tail_out.shape[1:], 1)
    ends = jnp.zeros(tail_out.shape[1:], F32)
    for t in range(pad):
        ends = jnp.where(lane == t, tile_sum(w_ref, mask, rows - pad + t), ends)
    tail_out[pad] = ends

    first = jnp.bitwise_xor(scal[0], k) * per
    scaled_terms(h_ref, u_out, terms, first, per + pad)
    row_pieces(scal, offs, terms, hi_ref, lo_ref, u_out, [k], [out])


def numer_col_kernel(order, scal, hi_ref, lo_ref, w_ref, *refs):
    scales, refs = refs[: ITERS + 1], refs[ITERS + 1 :]
    sums_out, outs, acc = refs[0], refs[1:-1], refs[-1]
    u_ref = scales[-1]
    rows = hi_ref.shape[0]
    tile = u_ref.shape[1]
    offs = offsets(scal, hi_ref.shape[2] // tile)
    per = outs[0].shape[0]
    acc[...] = jnp.zeros_like(acc)
    col_loop(offs, w_ref, hi_ref, lo_ref, u_ref, acc, 0, rows, 0)
    for k, out in zip(order, outs):
        first = jnp.bitwise_xor(scal[0], k) * per

        def body(t, carry):
            out[t] = acc[first + t] * u_ref[pl.ds(first + t, 1), :]
            return carry

        lax.fori_loop(0, per, body, 0, unroll=4)
    write_sums(sums_out, scales, rows)


def write_sums(sums_out, scales, rows):
    sums_out[...] = jnp.zeros_like(sums_out)
    mask = scales[0][:rows]
    totals = [mask]
    for t in range(ITERS):
        below = jnp.where(mask > 0, scales[t + 1][:rows], 1.0)
        totals.append(jnp.where(mask > 0, scales[t][:rows] / below, 0.0))
    for t, total in enumerate(totals):
        line = jnp.sum(jnp.sum(total, axis=0, keepdims=True), axis=1, keepdims=True)
        sums_out[t : t + 1, :] = jnp.broadcast_to(line, (1, mask.shape[1]))


def numer_row_kernel(order, scal, hi_ref, lo_ref, h_ref, u_ref, after, *refs):
    outs, terms = refs[:-1], refs[-1]
    ext, tile = u_ref.shape
    offs = offsets(scal, hi_ref.shape[2] // tile)
    scaled_terms(h_ref, u_ref, terms, 0, ext)
    row_pieces(scal, offs, terms, hi_ref, lo_ref, u_ref, order, outs)


def numer_first(scal, r_hi, r_lo, row_factors, col_ext, mask_ext, parts, k):
    shares = len(parts)
    rows, tile = r_hi.shape[:2]
    factors = row_factors.shape[0]
    ext = mask_ext.shape[0]
    pad = ext - rows
    per = rows // shares
    return kernel_call(
        functools.partial(numer_first_kernel, k, shares),
        "numer_first",
        scal,
        [r_hi, r_lo, row_factors, col_ext, mask_ext, *parts],
        [
            jax.ShapeDtypeStruct((ext, tile), F32),
            jax.ShapeDtypeStruct((pad + 1, factors, tile), F32),
            jax.ShapeDtypeStruct((per, factors, tile), F32),
        ],
        [
            pltpu.VMEM((2 * pad, factors, tile), F32),
            pltpu.VMEM((ext, 2 * factors, tile), BF16),
        ],
    )


def numer_col(scal, r_hi, r_lo, row_factors, scales, order, shares):
    rows, tile = r_hi.shape[:2]
    factors = row_factors.shape[0]
    piece = jax.ShapeDtypeStruct((rows // shares, factors, tile), F32)
    res = kernel_call(
        functools.partial(numer_col_kernel, order),
        "numer_col",
        scal,
        [r_hi, r_lo, row_factors, *scales],
        [jax.ShapeDtypeStruct((8, tile), F32)] + [piece] * len(order),
        [pltpu.VMEM((scales[0].shape[0], factors, tile), F32)],
    )
    return res[0], res[1:]


def numer_row(scal, r_hi, r_lo, col_ext, u, after, order, shares):
    rows, tile = r_hi.shape[:2]
    factors = col_ext.shape[0]
    piece = jax.ShapeDtypeStruct((rows // shares, factors, tile), F32)
    return kernel_call(
        functools.partial(numer_row_kernel, order),
        "numer_row",
        scal,
        [r_hi, r_lo, col_ext, u, after],
        [piece] * len(order),
        [pltpu.VMEM((u.shape[0], 2 * factors, tile), BF16)],
    )


def mean_scale(sums):
    scale = sums[1:2, :] / sums[0:1, :]
    for t in range(1, ITERS):
        scale = scale * (sums[t + 1 : t + 2, :] / sums[0:1, :])
    return scale


def tile_sum(factor_ref, mask, j):
    tile = mask.shape[1]
    x = factor_ref[:, pl.ds(pl.multiple_of(j * tile, tile), tile)] * mask[pl.ds(j, 1), :]
    return jnp.sum(x, axis=1, keepdims=True)


def windows(sums, per):
    return [tree_sum(sums[t : t + len(sums) - per]) for t in range(per)]


def write_coefficient(old_ref, mask, first, lowers, times_out, plus_out):
    tile = mask.shape[1]
    for t, lower in enumerate(lowers):
        live = mask[pl.ds(first + t, 1), :]
        old = old_ref[:, t * tile : (t + 1) * tile]
        times_out[t] = jnp.where(live > 0, old / jnp.where(live > 0, lower * live, 1.0), 0.0)
        plus_out[t] = jnp.where(live > 0, 0.0, old)


def row_coefficient_kernel(pad, scal, old_ref, mask, other, times_out, plus_out):
    per = times_out.shape[0]
    first = scal[0] * per
    sums = [tile_sum(other, mask, first + t) for t in range(per + pad)]
    write_coefficient(old_ref, mask, first, windows(sums, per), times_out, plus_out)


def col_coefficient_kernel(pad, scal, old_ref, mask, other, ends, times_out, plus_out):
    per = times_out.shape[0]
    first = scal[0] * per
    sums = []
    for j in range(1, per + pad):
        total = tile_sum(other, mask, jnp.maximum(first - pad + j, 0))
        for start in range(0, pad, per):
            if start + j < pad:
                before = jnp.where(scal[scal.shape[0] - 1] > 0, ends[:, start + j : start + j + 1], 0.0)
                total = jnp.where(first == start, before, total)
        sums.append(total)
    sums.append(jnp.zeros_like(sums[0]))
    write_coefficient(old_ref, mask, first, windows(sums, per), times_out, plus_out)


def coefficient(kernel, scal, shares, old, mask_ext, other, *ends):
    factors = old.shape[0]
    tile = mask_ext.shape[1]
    rows = old.shape[1] // tile
    per = rows // shares
    specs = [pl.BlockSpec((factors, per * tile), lambda i, scal: (0, scal[0]))]
    specs += [vmem() for _ in range(2 + len(ends))]
    return kernel_call(
        functools.partial(kernel, mask_ext.shape[0] - rows),
        "coefficient",
        scal,
        [old, mask_ext, other, *ends],
        [jax.ShapeDtypeStruct((per, factors, tile), F32)] * 2,
        specs=specs,
    )


def update_kernel(scal, sums, times, plus, *refs):
    terms, out = refs[:-1], refs[-1]
    per, _, tile = times.shape
    c = mean_scale(sums[...])
    for t in range(per):
        numer = terms[0][t]
        for term in terms[1:]:
            numer = numer + term[t]
        out[:, t * tile : (t + 1) * tile] = times[t] * (numer * c * c) + plus[t]


def update(scal, sums, times, plus, terms):
    per, count, tile = terms[0].shape
    return kernel_call(
        update_kernel,
        "update",
        scal,
        [sums, times, plus, *terms],
        [jax.ShapeDtypeStruct((count, per * tile), F32)],
    )[0]


def xor_exchange(x, axis, k):
    return lax.ppermute(x, axis, [(i, i ^ k) for i in range(lax.axis_size(axis))])


def both_sides(x, even):
    size = lax.axis_size("genome")
    a = lax.ppermute(x, "genome", [(i, i ^ 1) for i in range(size)])
    b = lax.ppermute(x, "genome", [(i, (((i + 1) ^ 1) - 1) % size) for i in range(size)])
    return jnp.where(even > 0, a, b), jnp.where(even > 0, b, a)


def scatter_terms(pieces):
    size = lax.axis_size("offset")
    if size == 4:
        far = pieces[3] + xor_exchange(pieces[2], "offset", 1)
        far = xor_exchange(far, "offset", 3)
        return [pieces[0], xor_exchange(pieces[1], "offset", 1), far]
    return [pieces[0]] + [xor_exchange(pieces[k], "offset", k) for k in range(1, size)]


def per_device(counts, band_offset, bin_mask, row_factors, col_factors):
    rows, slots, tile = counts.shape[:3]
    factors = row_factors.shape[0]
    offset_count = lax.axis_size("offset")
    genome_count = lax.axis_size("genome")
    g = lax.axis_index("genome")
    o = lax.axis_index("offset").astype(jnp.int32)
    reach = slots * offset_count - 1
    pad = reach + 1

    line = jnp.broadcast_to(g, (1, tile))
    even = (line % 2 == 0).astype(F32)
    has_next = (line < genome_count - 1).astype(F32)
    has_prev = (line > 0).astype(F32)
    count = offset_count * -(-pad * offset_count // rows)
    index = lax.broadcasted_iota(jnp.int32, (count, tile), 0)
    share, k = index // offset_count, index % offset_count
    mine = (jnp.bitwise_xor(share, k) == o).astype(F32) * has_prev
    flags = jnp.concatenate([even, has_next, has_prev, mine])
    before = jnp.broadcast_to((g > 0).astype(jnp.int32), (1,))
    scal = jnp.concatenate([jnp.broadcast_to(o, (1,)), band_offset, before])
    flags, scal, bin_mask = lax.optimization_barrier((flags, scal, bin_mask))
    even, has_next, has_prev = flags[0:1], flags[1:2], flags[2:3]
    mine = flags[3:]

    mask = bin_mask.astype(F32).reshape(rows, tile)
    mask_next, _ = both_sides(mask[:pad], even)
    keep = lax.broadcasted_iota(jnp.int32, (pad, 1), 0) < reach
    mask_ext = jnp.concatenate([mask, jnp.where(keep, mask_next * has_next, 0.0)])

    counts = pltpu.with_memory_space_constraint(counts, pltpu.HBM)
    inner_v, kept = first_main(scal, counts, mask, rows + pad)
    col_late, _ = lax.optimization_barrier((col_factors, inner_v))
    ring_left = [(i, (i - 1) % genome_count) for i in range(genome_count)]
    col_next = lax.ppermute(col_late[:, : pad * tile], "genome", ring_left)
    col_ext = jnp.concatenate([col_factors, col_next], axis=1)

    scales = []
    quarter = rows // (ITERS + 1)
    for t in range(ITERS):
        if t == 0:
            u = mask_ext
            v, edge = first_edge(scal, kept, u, inner_v)
        else:
            v, edge, u = cover_edge(scal, kept, mask_ext, parts, ratios[0])
        scales.append(u)
        after, before = both_sides(edge, even)
        if t > 0:
            v = cover_main(scal, kept, u, v)
        else:
            *ratios, v = ratio(scal, kept, row_factors, col_factors, v, [], 0, 2 * quarter)
        front = v[:pad] + before[pad:] * has_prev
        back = v[rows:] + after[:pad] * has_next
        x = jnp.concatenate([front, v[pad:rows], back])
        others = {k: xor_exchange(x, "offset", k) for k in reversed(range(1, offset_count))}
        parts = [x, *others.values()]
        if t == 0:
            ratios = ratio(scal, kept, row_factors, col_factors, x, ratios, 2 * quarter, quarter)
        elif t == ITERS - 1:
            ratios = ratio(scal, kept, row_factors, col_ext, x, ratios, 3 * quarter, quarter)

    r_hi, r_lo = ratios
    per = rows // offset_count
    u, tail, early = numer_first(
        scal, r_hi, r_lo, row_factors, col_ext, mask_ext, parts, EARLY
    )
    scales.append(u)
    order = [EARLY, *(k for k in range(offset_count) if k != EARLY)]
    sums, pieces = numer_col(scal, r_hi, r_lo, row_factors, scales, order, offset_count)
    h_parts = dict(zip(order, pieces))

    right = [(i, (i + 1) % genome_count) for i in range(genome_count)]
    arrived = lax.ppermute(tail, "genome", right)
    for s in range(-(-pad // per)):
        piece = arrived[s * per : min(pad, (s + 1) * per)]
        for k in range(offset_count):
            at = s * offset_count + k
            h_parts[k] = h_parts[k].at[: piece.shape[0]].add(piece * mine[at : at + 1])

    row_terms = coefficient(
        row_coefficient_kernel, scal, offset_count, row_factors, mask_ext, col_ext
    )
    col_terms = coefficient(
        col_coefficient_kernel, scal, offset_count, col_factors, mask_ext, row_factors, arrived[pad]
    )
    order = [k for k in (3, 1, 0, *range(4, offset_count))]
    pieces = numer_row(scal, r_hi, r_lo, col_ext, u, h_parts[EARLY], order, offset_count)
    w_parts = dict(zip(order, pieces)) | {EARLY: early}
    w_terms = scatter_terms([w_parts[k] for k in range(offset_count)])
    h_terms = scatter_terms([h_parts[k] for k in range(offset_count)])

    sums, _ = lax.optimization_barrier((sums, w_terms[2]))
    sums = jnp.sum(lax.all_gather(sums, "genome"), axis=0)
    bias = (u[:rows] * mean_scale(sums)).reshape(-1)

    col_update = update(scal, sums, *col_terms, h_terms)
    row_update = update(scal, sums, *row_terms, w_terms)
    return bias, row_update, col_update


def solution(mesh):
    return jax.shard_map(
        per_device,
        mesh=mesh,
        in_specs=(
            P("genome", "offset", None, None),
            P("offset"),
            P("genome"),
            P(None, "genome"),
            P(None, "genome"),
        ),
        out_specs=(P("genome"), P(None, ("genome", "offset")), P(None, ("genome", "offset"))),
        check_vma=False,
    )
```
